128 devices in a mesh: grp: 4 (over y_lo, core), dev: 32 (over x, z, y_hi).
Axes of the slice: x: 4, y: 4 (y_hi: 2, y_lo: 2; y = y_hi * 2 + y_lo), z: 4, core: 2. Of those that a mesh axis runs over, the one named last changes fastest.
Arguments:
- entity: float32 [4, 65536, 256], P('grp', 'dev')
- entity_acc: float32 [4, 65536], P('grp', 'dev'), may hold values from 0.001 to 0.1
- relation: float32 [40, 256, 256], replicated, may hold values from -0.375 to 0.375
- relation_acc: float32 [40, 256], replicated, may hold values from 1 to 10000
- partner: int32 [4, 32], replicated, may hold values from 0 to 3
- src_row: int32 [4, 65536], P('grp', 'dev'), may hold values from 0 to 2047
- dst_owner: int32 [4, 65536, 1], P('grp', 'dev'), may hold values from 0 to 31; in each aligned block of 2048 rows (0 to 2047, 2048 to 4095, ..., all dimensions but the last counted through in order) at most 128 rows name the same one
- dst_row: int32 [4, 65536], P('grp', 'dev'), may hold values from 0 to 2047
- rel_ids: int32 [4, 64], P('grp', 'dev'), may hold values from 0 to 39
- neg_src: int32 [4, 64, 1024], P('grp', 'dev'), may hold values from 0 to 2047
- neg_dst: int32 [4, 64, 1024], P('grp', 'dev'), may hold values from 0 to 2047
- edge_count: int32 [4, 32], P('grp', 'dev'), may hold values from 1024 to 2048
Outputs:
- entity_new: float32 [4, 65536, 256], P('grp', 'dev')
- entity_acc_new: float32 [4, 65536], P('grp', 'dev')
- relation_new: float32 [40, 256, 256], replicated
- relation_acc_new: float32 [40, 256], replicated
The draws below stay inside these ranges and needn't reach their ends.
Inputs may be any that keep to these rules, and one draw needn't show every extreme that they name: `dst_owner`: among the edges of one device at most 128 name the same shard.
All inputs are finite; a program needn't handle non-finite values.
Results may differ from the reference program's by a relative error of at most 0.0085.
The reference program's roundings to bfloat16 on the way count: a program that leaves them out, or rounds other values in their place, can miss the bound.
Values may be sent and summed in bfloat16 or wider, within the bound.
No kernel may reach another device: no remote copies, remote signals or barrier semaphores. Data moves between devices by JAX's collectives and lax.ppermute only.
A program may use at most 192 MiB of HBM per device.

```python
import math
import jax
import jax.numpy as jnp
import numpy as np
from jax import lax

D = 256
REL = 40
NEG = 1024
BLOCK = 1024
BLOCKS = 2
ENT_DEV = 2048
EDGE_DEV = 2048
CAP = 128
N_GRP = 4
N_DEV = 32


def draw_entity(key, part):
    key = jax.random.fold_in(key, 3)
    base = jax.random.normal(key, (N_GRP, N_DEV * ENT_DEV, D), jnp.float32) * 0.5
    return base


def touch_ends(values, own_key, least, largest):
    spot = [jax.random.randint(jax.random.fold_in(own_key, axis), (), 0, length) for axis, length in enumerate(values.shape)]
    main_axis = values.shape.index(max(values.shape))
    next_to = spot[:main_axis] + [(spot[main_axis] + 1) % values.shape[main_axis]] + spot[main_axis + 1:]
    return values.at[tuple(spot)].set(least).at[tuple(next_to)].set(largest)


def block_levels(rng, dims, cuts, low, high):
    gain, own = 1.0, jax.random.fold_in(rng, 6)
    for axis_at, blocks in cuts:
        draws = jnp.exp(jax.random.uniform(jax.random.fold_in(own, axis_at), (blocks,), jnp.float32, low / len(cuts), high / len(cuts)))
        gain = gain * jnp.repeat(draws, dims[axis_at] // blocks).reshape([-1 if axis == axis_at else 1 for axis in range(len(dims))])
    return gain


def shared_out(key, own, number, rows, amount, top, most, skew):
    sequence = jax.random.permutation(key, amount)
    crowded, ordinary = load_shares(amount, rows * top, most, skew, True), load_shares(amount, rows * top, most, skew, False)
    places = jnp.arange(amount)

    def named(sizes, rotation):
        used = int((sizes > 0).sum())
        fixed = max(1, used // 4)
        shifted = fixed + (places - fixed + rotation * (used - fixed)) % max(1, amount - fixed)
        return jnp.zeros((amount,), jnp.int32).at[sequence[jnp.where(places < fixed, places, shifted)]].set(jnp.asarray(sizes, jnp.int32))

    sizes = jnp.where(number % 4 == 0, named(crowded, number // 4), named(ordinary, number - number // 4 - 1))
    mixed = jax.random.permutation(jax.random.fold_in(own, 3), amount)
    giver, taker = mixed[0:amount // 2 * 2:2], mixed[1:amount // 2 * 2:2]
    margin = jnp.minimum(sizes[giver] - 1, most - sizes[taker]) // 2
    margin = jnp.where((giver == sequence[0]) | (taker == sequence[0]) | (sizes[taker] == 0), 0, jnp.maximum(margin, 0))
    shifted = jax.random.randint(jax.random.fold_in(own, 4), (amount // 2,), 0, 1 << 20) % (margin + 1)
    sizes = sizes.at[giver].add(-shifted).at[taker].add(shifted)
    labels = jnp.searchsorted(jnp.cumsum(sizes), jnp.arange(rows * top), side="right").astype(jnp.int32)
    listing = labels.reshape(top, rows).T
    listing = listing[jax.random.permutation(jax.random.fold_in(own, 1), rows)]
    rotation = jax.random.randint(jax.random.fold_in(own, 2), (rows, 1), 0, top)
    return jnp.take_along_axis(listing, (jnp.arange(top)[None, :] + rotation) % top, axis=1)


def load_shares(number_of, total, reach, lean, full):
    weights = [(1 << 20) // math.isqrt(rank ** lean) + 1 for rank in range(1, number_of + 1)]
    largest = reach if full else min(reach, max(-(-total // number_of), total * weights[0] // sum(weights)))
    least = 1 if total - largest >= number_of - 1 else 0
    counts, surplus = [largest] + [least] * (number_of - 1), total - largest - least * (number_of - 1)
    while surplus > 0:
        candidates = [i for i in range(1, number_of) if counts[i] < largest] or [i for i in range(1, number_of) if counts[i] < reach]
        mass, budget = sum([weights[i] for i in candidates]), surplus
        for i in candidates:
            extra = min(reach - counts[i], max(1, budget * weights[i] // mass), surplus)
            counts[i] = counts[i] + extra
            surplus = surplus - extra
    return np.array(counts)


def noise(key, shape, spread, limit, held_as=jnp.bfloat16):
    return jnp.clip(spread * jax.random.normal(key, shape, jnp.float32), -limit, limit).astype(held_as)


def setup_inputs(seed: int = 0) -> dict:
    keys = jax.random.split(jax.random.key(seed), 13)
    entity = draw_entity(jax.random.fold_in(keys[12], 71), 0)
    entity_acc = jnp.clip(jnp.exp(math.log(0.1) - 4.6051702 * jax.random.uniform(keys[1], (N_GRP, N_DEV * ENT_DEV), jnp.float32) ** block_levels(keys[1], (N_GRP, N_DEV * ENT_DEV), ((0, 4), (1, 32)), -0.2, 0.2)), 0.001, 0.1)
    relation = noise(keys[2], (REL, D, D), D ** -0.5, 0.375, jnp.float32)
    relation_acc = jnp.clip(jnp.exp(jax.random.uniform(keys[3], (REL, D), jnp.float32, math.log(1.0), math.log(10000.0))), 1.0, 10000.0)
    partner = touch_ends(jax.random.randint(keys[4], (N_GRP, N_DEV), 0, N_GRP), jax.random.fold_in(keys[4], 1), 0, N_GRP - 1).astype(jnp.int32)
    src_row = touch_ends(jax.random.randint(keys[5], (N_GRP, N_DEV * EDGE_DEV), 0, ENT_DEV), jax.random.fold_in(keys[5], 1), 0, ENT_DEV - 1).astype(jnp.int32)
    dst_owner_keys = jax.random.split(jax.random.fold_in(keys[6], 1), N_GRP * (N_DEV * EDGE_DEV) // EDGE_DEV)
    dst_owner_turns = jax.random.permutation(jax.random.fold_in(keys[6], 3), N_GRP * (N_DEV * EDGE_DEV) // EDGE_DEV)
    dst_owner = jax.vmap(lambda own, number: shared_out(jax.random.fold_in(keys[6], 2), own, number, EDGE_DEV, N_DEV, 1, CAP, 2))(dst_owner_keys, dst_owner_turns).reshape((N_GRP, N_DEV * EDGE_DEV, 1))
    dst_row = touch_ends(jax.random.randint(keys[7], (N_GRP, N_DEV * EDGE_DEV), 0, ENT_DEV), jax.random.fold_in(keys[7], 1), 0, ENT_DEV - 1).astype(jnp.int32)
    rel_ids = touch_ends(jax.random.randint(keys[8], (N_GRP, N_DEV * BLOCKS), 0, REL), jax.random.fold_in(keys[8], 1), 0, REL - 1).astype(jnp.int32)
    neg_src = touch_ends(jax.random.randint(keys[9], (N_GRP, N_DEV * BLOCKS, NEG), 0, ENT_DEV), jax.random.fold_in(keys[9], 1), 0, ENT_DEV - 1).astype(jnp.int32)
    neg_dst = touch_ends(jax.random.randint(keys[10], (N_GRP, N_DEV * BLOCKS, NEG), 0, ENT_DEV), jax.random.fold_in(keys[10], 1), 0, ENT_DEV - 1).astype(jnp.int32)
    edge_count = touch_ends(jax.random.randint(keys[11], (N_GRP, N_DEV), EDGE_DEV // 2, EDGE_DEV + 1), jax.random.fold_in(keys[11], 1), EDGE_DEV // 2, EDGE_DEV).astype(jnp.int32)
    return dict(entity=entity, entity_acc=entity_acc, relation=relation, relation_acc=relation_acc, partner=partner, src_row=src_row, dst_owner=dst_owner, dst_row=dst_row, rel_ids=rel_ids, neg_src=neg_src, neg_dst=neg_dst, edge_count=edge_count)


step_rate = 0.1

def block_grads(src_rows, dst_rows, neg_src_rows, neg_dst_rows, operator, live):

    def loss_fn(src_rows, dst_rows, neg_src_rows, neg_dst_rows, operator):
        op_half = operator.astype(jnp.bfloat16)
        lhs_rows = jnp.dot(src_rows, op_half, preferred_element_type=jnp.float32).astype(jnp.bfloat16)
        rhs_rows = jnp.dot(dst_rows, op_half.T, preferred_element_type=jnp.float32).astype(jnp.bfloat16)
        positive = lax.optimization_barrier(jnp.sum(lhs_rows.astype(jnp.float32) * dst_rows.astype(jnp.float32), axis=1))
        dst_scores = jnp.dot(lhs_rows, neg_dst_rows.T, preferred_element_type=jnp.float32)
        src_scores = jnp.dot(rhs_rows, neg_src_rows.T, preferred_element_type=jnp.float32)

        def softmax_loss(scores):
            highest = lax.stop_gradient(jnp.maximum(lax.optimization_barrier(jnp.max(scores, axis=1)), positive))
            totals = jnp.exp(positive - highest) + lax.optimization_barrier(jnp.sum(jnp.exp(scores - highest[:, None]), axis=1))
            return highest + jnp.log(totals) - positive
        return jnp.sum(live * (softmax_loss(dst_scores) + softmax_loss(src_scores)))
    return jax.grad(loss_fn, argnums=(0, 1, 2, 3, 4))(src_rows, dst_rows, neg_src_rows, neg_dst_rows, operator)

def reference(entity, entity_acc, relation, relation_acc, partner, src_row, dst_owner, dst_row, rel_ids, neg_src, neg_dst, edge_count):
    emb_half = entity.astype(jnp.bfloat16)

    def device_step(carry, flat_index):
        ent_grad, rel_grad = carry
        group_id = flat_index // N_DEV
        place_id = flat_index % N_DEV
        visit_id = partner[group_id, place_id]
        own_part = emb_half[group_id]
        other_part = emb_half[visit_id]
        first_edge = (place_id * EDGE_DEV).astype(jnp.int32)
        src_ids = lax.dynamic_slice_in_dim(src_row[group_id], first_edge, EDGE_DEV) + place_id * ENT_DEV
        owners = lax.dynamic_slice_in_dim(dst_owner[group_id][:, 0], first_edge, EDGE_DEV)
        dst_ids = owners * ENT_DEV + lax.dynamic_slice_in_dim(dst_row[group_id], first_edge, EDGE_DEV)
        count = edge_count[group_id, place_id]
        for block_index in range(BLOCKS):
            start = block_index * BLOCK
            batch_id = (place_id * BLOCKS + block_index).astype(jnp.int32)
            s_ids = src_ids[start:start + BLOCK]
            d_ids = dst_ids[start:start + BLOCK]
            ns_ids = lax.dynamic_index_in_dim(neg_src[group_id], batch_id, 0, keepdims=False) + place_id * ENT_DEV
            nd_ids = lax.dynamic_index_in_dim(neg_dst[group_id], batch_id, 0, keepdims=False) + place_id * ENT_DEV
            rel_index = rel_ids[group_id, batch_id]
            live = (start + jnp.arange(BLOCK, dtype=jnp.int32) < count).astype(jnp.float32)
            grads = block_grads(own_part[s_ids], other_part[d_ids], own_part[ns_ids], other_part[nd_ids], relation[rel_index], live)
            ent_grad = ent_grad.at[group_id, s_ids].add(grads[0].astype(jnp.float32))
            ent_grad = ent_grad.at[group_id, ns_ids].add(grads[2].astype(jnp.float32))
            ent_grad = ent_grad.at[visit_id, d_ids].add(grads[1].astype(jnp.float32))
            ent_grad = ent_grad.at[visit_id, nd_ids].add(grads[3].astype(jnp.float32))
            rel_grad = rel_grad.at[rel_index].add(grads[4].astype(jnp.float32))
        return ((ent_grad, rel_grad), None)
    start_carry = (jnp.zeros(entity.shape, jnp.float32), jnp.zeros(relation.shape, jnp.float32))
    (ent_grad, rel_grad), _ = lax.scan(device_step, start_carry, jnp.arange(N_GRP * N_DEV, dtype=jnp.int32))
    entity_acc_new = entity_acc + lax.optimization_barrier(jnp.mean(ent_grad * ent_grad, axis=2))
    entity_new = entity - step_rate * ent_grad / jnp.sqrt(entity_acc_new)[:, :, None]
    relation_acc_new = relation_acc + lax.optimization_barrier(jnp.mean(rel_grad * rel_grad, axis=2))
    relation_new = relation - step_rate * rel_grad / jnp.sqrt(relation_acc_new)[:, :, None]
    return (entity_new, entity_acc_new, relation_new, relation_acc_new)
```

```python
import functools

import jax
import jax.numpy as jnp
from jax import lax
from jax.experimental import pallas as pl
from jax.experimental.pallas import tpu as pltpu
from jax.sharding import PartitionSpec as P

step_rate = 0.1
VMEM_BYTES = 50 * 1024 * 1024
half = jnp.bfloat16
full = jnp.float32
VMEM = pl.BlockSpec(memory_space=pltpu.VMEM)
SMEM = pl.BlockSpec(memory_space=pltpu.SMEM)


def dot(a, b, ca, cb):
    return lax.dot_general(a, b, (((ca,), (cb,)), ((), ())), preferred_element_type=full)


def turned(row):
    pieces = [
        jnp.broadcast_to(row[:, at : at + 128], (128, 128)).T for at in range(0, row.shape[1], 128)
    ]
    return pieces[0] if len(pieces) == 1 else jnp.concatenate(pieces, axis=0)


def pick(row, width):
    spread = turned(row.astype(full))
    lane = lax.broadcasted_iota(jnp.int32, (1, 128), 1).astype(full)
    pieces = [
        jnp.where(spread == lane + float(at), 1.0, 0.0).astype(half) for at in range(0, width, 128)
    ]
    return jnp.concatenate(pieces, axis=1)


def place(row, first, height):
    line = lax.broadcasted_iota(jnp.int32, (height, 1), 0) + first
    return jnp.where(row == line, 1.0, 0.0).astype(half)


def call(body, outs, scratch=(), specs=None, cost=None, **kw):
    return pl.pallas_call(
        body,
        out_shape=outs,
        in_specs=specs,
        out_specs=jax.tree.map(lambda _: VMEM, outs),
        scratch_shapes=list(scratch),
        compiler_params=pltpu.CompilerParams(vmem_limit_bytes=VMEM_BYTES),
        cost_estimate=cost,
        **kw,
    )


def cost(flops, moved):
    return pl.CostEstimate(flops=int(flops), bytes_accessed=int(moved), transcendentals=0)


def slots_body(owner_ref, row_ref, slot_ref, wanted_ref):
    peers, room = wanted_ref.shape
    edges = owner_ref.shape[1]
    step = 256
    before = lax.broadcasted_iota(jnp.int32, (step, step), 0)
    after = lax.broadcasted_iota(jnp.int32, (step, step), 1)
    upper = jnp.where(before <= after, 1.0, 0.0).astype(half)
    peer = lax.broadcasted_iota(jnp.int32, (peers, step), 0)
    carry = jnp.zeros((peers, 1), full)
    high = jnp.zeros((peers, room), full)
    low = jnp.zeros((peers, room), full)
    for at in range(0, edges, step):
        owner = owner_ref[:, at : at + step]
        hit = jnp.where(peer == owner, 1.0, 0.0)
        count = dot(hit.astype(half), upper, 1, 0) + carry
        carry = count[:, step - 1 :]
        order = (jnp.sum(count * hit, axis=0, keepdims=True) - 1.0).astype(jnp.int32)
        slot_ref[:, at : at + step] = owner * room + order
        spot = place(order, 0, room)
        row = row_ref[:, at : at + step]
        top = lax.shift_right_logical(row, 4)
        high += dot((hit * top.astype(full)).astype(half), spot, 1, 1)
        low += dot((hit * (row - top * 16).astype(full)).astype(half), spot, 1, 1)
    wanted_ref[...] = (high * 16.0 + low).astype(jnp.int32)


def list_peers(partner_ref, group_ref, list_ref, count_ref):
    peers = partner_ref.shape[1]
    me = group_ref[0]
    for part in range(4):
        count_ref[part] = 0

    def add(peer, carry):
        part = partner_ref[me, peer] ^ me
        at = count_ref[part]
        list_ref[part, at] = peer
        count_ref[part] = at + 1
        return carry

    lax.fori_loop(0, peers, add, 0)


def answer_body(partner_ref, group_ref, asked_ref, *refs):
    tables, (found_ref, list_ref, count_ref) = refs[:4], refs[4:]
    rows, width = tables[0].shape
    room = asked_ref.shape[1]
    list_peers(partner_ref, group_ref, list_ref, count_ref)
    for part in range(4):
        count = count_ref[part]

        def pair(t, carry, part=part, count=count):
            one = list_ref[part, 2 * t]
            two = list_ref[part, jnp.minimum(2 * t + 1, count - 1)]
            ask = jnp.concatenate([asked_ref[pl.ds(one, 1), :], asked_ref[pl.ds(two, 1), :]], axis=1)
            got = dot(pick(ask, rows), tables[part][...], 1, 0).astype(half)
            found_ref[pl.ds(one, 1)] = got[:room].reshape(1, room, width)
            found_ref[pl.ds(two, 1)] = got[room:].reshape(1, room, width)
            return carry

        lax.fori_loop(0, (count + 1) // 2, pair, 0)


def rows_body(visit_ref, src_ref, neg_src_ref, neg_dst_ref, *refs):
    tables, (src_out, neg_src_out, neg_dst_out, visit) = refs[:4], refs[4:]
    rows = tables[0].shape[0]
    for part in range(4):

        @pl.when(visit_ref[0] == part)
        def _(part=part):
            visit[...] = tables[part][...]

    step = 256
    blocks, negs = neg_src_ref.shape
    for at in range(0, src_ref.shape[1], step):
        src_out[at : at + step] = dot(
            pick(src_ref[:, at : at + step], rows), tables[0][...], 1, 0
        ).astype(half)
    for block in range(blocks):
        for at in range(0, negs, step):
            to = block * negs + at
            neg_src_out[to : to + step] = dot(
                pick(neg_src_ref[block : block + 1, at : at + step], rows), tables[0][...], 1, 0
            ).astype(half)
            neg_dst_out[to : to + step] = dot(
                pick(neg_dst_ref[block : block + 1, at : at + step], rows), visit[...], 1, 0
            ).astype(half)


def model_body(
    rel_ref,
    count_ref,
    slot_ref,
    fetched_ref,
    src_ref,
    neg_src_ref,
    neg_dst_ref,
    relation_ref,
    outgoing_ref,
    d_src_ref,
    d_neg_src_ref,
    d_neg_dst_ref,
    d_dst,
    operator,
    op_half,
    neg_dst_sum,
    neg_src_sum,
    op_sum,
    op_turned_sum,
    op_sem,
):
    slots, width = fetched_ref.shape
    edges = src_ref.shape[0]
    blocks = rel_ref.shape[1]
    block_len = edges // blocks
    negs = neg_src_ref.shape[0] // blocks
    peers, room, _ = outgoing_ref.shape
    extra = width // peers
    places = slots // peers
    step = 256
    copies = []
    for block in range(blocks):
        copies.append(
            pltpu.make_async_copy(
                relation_ref.at[rel_ref[0, block]], operator.at[block], op_sem.at[block]
            )
        )
        copies[-1].start()
    for block in range(blocks):
        copies[block].wait()
        op_half[...] = operator[block].astype(half)
        neg_dst_sum[...] = jnp.zeros_like(neg_dst_sum)
        neg_src_sum[...] = jnp.zeros_like(neg_src_sum)
        op_sum[...] = jnp.zeros_like(op_sum)
        op_turned_sum[...] = jnp.zeros_like(op_turned_sum)

        def chunk(t, carry, block=block):
            at = pl.multiple_of(block * block_len + t * step, step)
            here = pl.ds(at, step)
            op = op_half[...]
            dst = dot(pick(slot_ref[:, here], slots), fetched_ref[...], 1, 0).astype(half)
            src = src_ref[here, :]
            negs_at = pl.ds(block * negs, negs)
            neg_dst = neg_dst_ref[negs_at, :]
            neg_src = neg_src_ref[negs_at, :]
            line = lax.broadcasted_iota(jnp.int32, (step, 1), 0) + at
            live = jnp.where(line < count_ref[0, 0], 1.0, 0.0)
            lhs = dot(src, op, 1, 0).astype(half)
            rhs = dot(dst, op, 1, 1).astype(half)
            positive = jnp.sum(lhs.astype(full) * dst.astype(full), axis=1, keepdims=True)

            def softmax(scores):
                highest = jnp.maximum(jnp.max(scores, axis=1, keepdims=True), positive)
                terms = jnp.exp(scores - highest)
                own = jnp.exp(positive - highest)
                scale = live / (own + jnp.sum(terms, axis=1, keepdims=True))
                return (terms * scale).astype(half), own * scale - live

            dst_terms, dst_own = softmax(dot(lhs, neg_dst, 1, 1))
            src_terms, src_own = softmax(dot(rhs, neg_src, 1, 1))
            d_positive = dst_own + src_own
            d_lhs = dot(dst_terms, neg_dst, 1, 0).astype(half)
            d_lhs = d_lhs + (d_positive * dst.astype(full)).astype(half)
            d_rhs = dot(src_terms, neg_src, 1, 0).astype(half)
            neg_dst_sum[...] += dot(lhs, dst_terms, 0, 0)
            neg_src_sum[...] += dot(rhs, src_terms, 0, 0)
            d_src_ref[here, :] = dot(d_lhs, op, 1, 1).astype(half)
            op_sum[...] += dot(src, d_lhs, 0, 0)
            op_turned_sum[...] += dot(d_rhs, dst, 0, 0)
            d_dst[here, :] = dot(d_rhs, op, 1, 0).astype(half) + (
                d_positive * lhs.astype(full)
            ).astype(half)
            return carry

        lax.fori_loop(0, block_len // step, chunk, 0)
        d_neg_dst_ref[block * negs : (block + 1) * negs, :] = neg_dst_sum[...].T.astype(half)
        d_neg_src_ref[block * negs : (block + 1) * negs, :] = neg_src_sum[...].T.astype(half)
        d_op = op_sum[...].astype(half) + op_turned_sum[...].astype(half)
        outgoing_ref[:, places + block * extra : places + (block + 1) * extra, :] = d_op.reshape(
            peers, extra, width
        )

    def send(t, carry):
        spot = place(slot_ref[...], t * 2 * places, 2 * places)
        out = dot(spot, d_dst[...], 1, 0).astype(half)
        outgoing_ref[pl.ds(2 * t, 2), :places, :] = out.reshape(2, places, width)
        return carry

    lax.fori_loop(0, peers // 2, send, 0)


def sums_body(src_ref, neg_src_ref, neg_dst_ref, d_src, d_neg_src, d_neg_dst, own_ref, visit_ref):
    rows = own_ref.shape[0]
    blocks, negs = neg_src_ref.shape
    step = 256

    def part(t, carry):
        first = pl.multiple_of(t * step, step)
        own = dot(place(src_ref[...], first, step), d_src[...], 1, 0)
        visit = jnp.zeros_like(own)
        for block in range(blocks):
            at = slice(block * negs, (block + 1) * negs)
            one = slice(block, block + 1)
            own += dot(place(neg_src_ref[one, :], first, step), d_neg_src[at, :], 1, 0)
            visit += dot(place(neg_dst_ref[one, :], first, step), d_neg_dst[at, :], 1, 0)
        own_ref[pl.ds(first, step), :] = own
        visit_ref[pl.ds(first, step), :] = visit
        return carry

    lax.fori_loop(0, rows // step, part, 0)


def home_body(partner_ref, group_ref, visit_to_ref, asked_ref, returned_ref, visit_ref, *refs):
    outs, (total, list_ref, count_ref) = refs[:4], refs[4:]
    rows, width = visit_ref.shape
    places = asked_ref.shape[1]
    list_peers(partner_ref, group_ref, list_ref, count_ref)
    total[...] = jnp.zeros_like(total)
    total[pl.ds(visit_to_ref[0], 1)] = visit_ref[...].reshape(1, rows, width)
    for part in range(4):
        count = count_ref[part]

        def pair(t, carry, part=part, count=count):
            one = list_ref[part, 2 * t]
            two = list_ref[part, jnp.minimum(2 * t + 1, count - 1)]
            ask_two = jnp.where(2 * t + 1 < count, asked_ref[pl.ds(two, 1), :], -1)
            ask = jnp.concatenate([asked_ref[pl.ds(one, 1), :], ask_two], axis=1)
            back = jnp.concatenate(
                [
                    returned_ref[pl.ds(one, 1), :places, :].reshape(places, width),
                    returned_ref[pl.ds(two, 1), :places, :].reshape(places, width),
                ],
                axis=0,
            )
            for first in range(0, rows, 512):
                total[part, first : first + 512] += dot(place(ask, first, 512), back, 1, 0)
            return carry

        lax.fori_loop(0, (count + 1) // 2, pair, 0)
        outs[part][...] = total[part].astype(half)


def operators_body(ids_ref, part_ref, out_ref, total):
    peers, _, width = part_ref.shape
    blocks = ids_ref.shape[1]
    rows = total.shape[1]
    total[...] = jnp.zeros_like(total)

    def add(peer, carry):
        piece = part_ref[pl.ds(peer, 1)].reshape(blocks * rows, width).astype(full)
        for block in range(blocks):
            at = ids_ref[peer, block]
            total[pl.ds(at, 1)] += piece[block * rows : (block + 1) * rows].reshape(1, rows, width)
        return carry

    lax.fori_loop(0, peers, add, 0)
    out_ref[...] = total[...].astype(half)


def on_device(
    entity,
    entity_acc,
    relation,
    relation_acc,
    partner,
    src_row,
    dst_owner,
    dst_row,
    rel_ids,
    neg_src,
    neg_dst,
    edge_count,
):
    me = lax.axis_index("grp")
    place_id = lax.axis_index("dev")
    peers = lax.axis_size("dev")
    rows, width = entity.shape[1:]
    edges = src_row.shape[1]
    blocks = rel_ids.shape[1]
    negs = neg_src.shape[2]
    relations = relation.shape[0]
    room = 2 * edges // peers
    extra = width // peers
    sds = jax.ShapeDtypeStruct

    def neighbour(x, flip):
        return lax.ppermute(x, "grp", [(g, g ^ flip) for g in range(4)])

    group = me.reshape(1)
    visit_to = (partner[me, place_id] ^ me).reshape(1)
    owners = dst_owner.reshape(1, edges)
    neg_src = neg_src.reshape(blocks, negs)
    neg_dst = neg_dst.reshape(blocks, negs)

    own = entity[0].astype(half)
    cross = neighbour(own, 2)
    sibling = neighbour(own, 1)
    group_ids = lax.all_gather(rel_ids[0], "dev", axis=0)
    slot, wanted = call(
        slots_body, (sds((1, edges), jnp.int32), sds((peers, room), jnp.int32)), specs=[VMEM] * 2
    )(owners, dst_row)
    asked = lax.all_to_all(wanted, "dev", split_axis=0, concat_axis=0, tiled=True)
    cross_sibling = neighbour(cross, 1)
    tables = (own, sibling, cross, cross_sibling)

    lists = [pltpu.SMEM((4, peers), jnp.int32), pltpu.SMEM((4,), jnp.int32)]
    found = call(
        answer_body,
        sds((peers, room, width), half),
        lists,
        [SMEM] * 2 + [VMEM] * 5,
    )(partner, group, asked, *tables)
    fetched = lax.all_to_all(found, "dev", split_axis=0, concat_axis=0, tiled=True)

    src_rows, neg_src_rows, neg_dst_rows = call(
        rows_body,
        (sds((edges, width), half), sds((blocks * negs, width), half), sds((blocks * negs, width), half)),
        [pltpu.VMEM((rows, width), half)],
        [SMEM] + [VMEM] * 7,
        cost(2 * 3 * edges * rows * width, 6 * rows * width * 2),
    )(visit_to, src_row, neg_src, neg_dst, *tables)

    outgoing, d_src, d_neg_src, d_neg_dst = call(
        model_body,
        (
            sds((peers, room + blocks * extra, width), half),
            sds((edges, width), half),
            sds((blocks * negs, width), half),
            sds((blocks * negs, width), half),
        ),
        [
            pltpu.VMEM((edges, width), half),
            pltpu.VMEM((blocks, width, width), full),
            pltpu.VMEM((width, width), half),
            pltpu.VMEM((width, negs), full),
            pltpu.VMEM((width, negs), full),
            pltpu.VMEM((width, width), full),
            pltpu.VMEM((width, width), full),
            pltpu.SemaphoreType.DMA((blocks,)),
        ],
        [SMEM] * 2 + [VMEM] * 5 + [pl.BlockSpec(memory_space=pl.ANY)],
    )(
        rel_ids,
        edge_count,
        slot,
        fetched.reshape(peers * room, width),
        src_rows,
        neg_src_rows,
        neg_dst_rows,
        relation,
    )
    returned = lax.all_to_all(outgoing, "dev", split_axis=0, concat_axis=0, tiled=True)

    own_grad, visit_grad = call(
        sums_body,
        (sds((rows, width), full), sds((rows, width), full)),
        (),
        [VMEM] * 6,
        cost(2 * 3 * edges * rows * width, 7 * rows * width * 2),
    )(src_row, neg_src, neg_dst, d_src, d_neg_src, d_neg_dst)

    rel_part = call(
        operators_body,
        sds((relations, extra, width), half),
        [pltpu.VMEM((relations, extra, width), full)],
        [SMEM, VMEM],
    )(group_ids, returned[:, room:, :])
    core = me & 1
    halves = rel_part.reshape(2, relations // 2, extra, width)
    mine = lax.dynamic_index_in_dim(halves, core, 0, keepdims=False)
    other = lax.dynamic_index_in_dim(halves, 1 - core, 0, keepdims=False)
    chip = (mine.astype(full) + neighbour(other, 1).astype(full)).astype(half)
    pair = (chip.astype(full) + neighbour(chip, 2).astype(full)).astype(half)
    gathered = lax.all_gather(pair, "dev", axis=0)

    home, home_sibling, home_cross, home_cross_sibling = call(
        home_body,
        tuple(sds((rows, width), half) for _ in range(4)),
        [pltpu.VMEM((4, rows, width), full)] + lists,
        [SMEM] * 3 + [VMEM] * 3,
    )(partner, group, visit_to, asked, returned, visit_grad)
    chip_cross = (home_cross.astype(full) + neighbour(home_cross_sibling, 1).astype(full)).astype(half)
    from_cross = neighbour(chip_cross, 2)
    from_sibling = neighbour(home_sibling, 1)
    total_grad = (
        own_grad + home.astype(full) + from_sibling.astype(full) + from_cross.astype(full)
    )
    acc_new = entity_acc[0] + jnp.mean(total_grad * total_grad, axis=1)
    entity_new = entity[0] - step_rate * total_grad / jnp.sqrt(acc_new)[:, None]

    other_half = neighbour(gathered, 1)
    both = jnp.where(core == 0, jnp.stack([gathered, other_half]), jnp.stack([other_half, gathered]))
    rel_total = both.transpose(0, 2, 1, 3, 4).reshape(relations, width, width).astype(full)
    relation_acc_new = relation_acc + jnp.mean(rel_total * rel_total, axis=2)
    relation_new = relation - step_rate * rel_total / jnp.sqrt(relation_acc_new)[:, :, None]
    return (entity_new[None], acc_new[None], relation_new, relation_acc_new)


def solution(mesh):
    return jax.shard_map(
        on_device,
        mesh=mesh,
        in_specs=(
            P("grp", "dev", None),
            P("grp", "dev"),
            P(),
            P(),
            P(),
            P("grp", "dev"),
            P("grp", "dev", None),
            P("grp", "dev"),
            P("grp", "dev"),
            P("grp", "dev", None),
            P("grp", "dev", None),
            P("grp", "dev"),
        ),
        out_specs=(P("grp", "dev", None), P("grp", "dev"), P(), P()),
        check_vma=False,
    )
```

```python
import functools

import jax
import jax.numpy as jnp
from jax import lax
from jax.experimental import pallas as pl
from jax.experimental.pallas import tpu as pltpu
from jax.sharding import PartitionSpec as P

step_rate = 0.1
VMEM_BYTES = 50 * 1024 * 1024
half = jnp.bfloat16
full = jnp.float32
VMEM = pl.BlockSpec(memory_space=pltpu.VMEM)
SMEM = pl.BlockSpec(memory_space=pltpu.SMEM)


def dot(a, b, ca, cb):
    return lax.dot_general(a, b, (((ca,), (cb,)), ((), ())), preferred_element_type=full)


def turned(row):
    pieces = [
        jnp.broadcast_to(row[:, at : at + 128], (128, 128)).T for at in range(0, row.shape[1], 128)
    ]
    return pieces[0] if len(pieces) == 1 else jnp.concatenate(pieces, axis=0)


def pick(row, width):
    spread = turned(row.astype(full))
    lane = lax.broadcasted_iota(jnp.int32, (1, 128), 1).astype(full)
    pieces = [
        jnp.where(spread == lane + float(at), 1.0, 0.0).astype(half) for at in range(0, width, 128)
    ]
    return jnp.concatenate(pieces, axis=1)


def place(row, first, height):
    line = lax.broadcasted_iota(jnp.int32, (height, 1), 0) + first
    return jnp.where(row == line, 1.0, 0.0).astype(half)


def call(body, outs, scratch=(), specs=None, cost=None, **kw):
    return pl.pallas_call(
        body,
        out_shape=outs,
        in_specs=specs,
        out_specs=jax.tree.map(lambda _: VMEM, outs),
        scratch_shapes=list(scratch),
        compiler_params=pltpu.CompilerParams(vmem_limit_bytes=VMEM_BYTES),
        cost_estimate=cost,
        **kw,
    )


def cost(flops, moved):
    return pl.CostEstimate(flops=int(flops), bytes_accessed=int(moved), transcendentals=0)


def slots_body(rel_ref, owner_ref, row_ref, slot_ref, wanted_ref):
    peers, _, room = wanted_ref.shape
    edges = owner_ref.shape[1]
    step = 256
    before = lax.broadcasted_iota(jnp.int32, (step, step), 0)
    after = lax.broadcasted_iota(jnp.int32, (step, step), 1)
    upper = jnp.where(before <= after, 1.0, 0.0).astype(half)
    peer = lax.broadcasted_iota(jnp.int32, (peers, step), 0)
    carry = jnp.zeros((peers, 1), full)
    high = jnp.zeros((peers, room), full)
    low = jnp.zeros((peers, room), full)
    for at in range(0, edges, step):
        owner = owner_ref[:, at : at + step]
        hit = jnp.where(peer == owner, 1.0, 0.0)
        count = dot(hit.astype(half), upper, 1, 0) + carry
        carry = count[:, step - 1 :]
        order = (jnp.sum(count * hit, axis=0, keepdims=True) - 1.0).astype(jnp.int32)
        slot_ref[:, at : at + step] = owner * room + order
        spot = place(order, 0, room)
        row = row_ref[:, at : at + step]
        top = lax.shift_right_logical(row, 4)
        high += dot((hit * top.astype(full)).astype(half), spot, 1, 1)
        low += dot((hit * (row - top * 16).astype(full)).astype(half), spot, 1, 1)
    wanted_ref[:, 0, :] = (high * 16.0 + low).astype(jnp.int32)
    lane = lax.broadcasted_iota(jnp.int32, (peers, room), 1)
    ids = jnp.zeros((peers, room), jnp.int32)
    for block in range(rel_ref.shape[1]):
        ids = jnp.where(lane == block, rel_ref[0, block], ids)
    wanted_ref[:, 1, :] = ids


def list_peers(partner_ref, group_ref, list_ref, count_ref):
    peers = partner_ref.shape[1]
    me = group_ref[0]
    for part in range(4):
        count_ref[part] = 0

    def add(peer, carry):
        part = partner_ref[me, peer] ^ me
        at = count_ref[part]
        list_ref[part, at] = peer
        count_ref[part] = at + 1
        return carry

    lax.fori_loop(0, peers, add, 0)


def answer_body(partner_ref, group_ref, asked_ref, *refs):
    tables, (found_ref, list_ref, count_ref) = refs[:4], refs[4:]
    rows, width = tables[0].shape
    room = asked_ref.shape[2]
    list_peers(partner_ref, group_ref, list_ref, count_ref)
    for part in range(4):
        count = count_ref[part]

        def pair(t, carry, part=part, count=count):
            one = list_ref[part, 2 * t]
            two = list_ref[part, jnp.minimum(2 * t + 1, count - 1)]
            ask = jnp.concatenate(
                [asked_ref[pl.ds(one, 1), 0, :], asked_ref[pl.ds(two, 1), 0, :]], axis=1
            )
            got = dot(pick(ask, rows), tables[part][...], 1, 0).astype(half)
            found_ref[pl.ds(one, 1)] = got[:room].reshape(1, room, width)
            found_ref[pl.ds(two, 1)] = got[room:].reshape(1, room, width)
            return carry

        lax.fori_loop(0, (count + 1) // 2, pair, 0)


def rows_body(visit_ref, src_ref, neg_src_ref, neg_dst_ref, *refs):
    tables, (src_out, neg_src_out, neg_dst_out, visit) = refs[:4], refs[4:]
    rows = tables[0].shape[0]
    for part in range(4):

        @pl.when(visit_ref[0] == part)
        def _(part=part):
            visit[...] = tables[part][...]

    step = 256
    blocks, negs = neg_src_ref.shape
    for at in range(0, src_ref.shape[1], step):
        src_out[at : at + step] = dot(
            pick(src_ref[:, at : at + step], rows), tables[0][...], 1, 0
        ).astype(half)
    for block in range(blocks):
        for at in range(0, negs, step):
            to = block * negs + at
            neg_src_out[to : to + step] = dot(
                pick(neg_src_ref[block : block + 1, at : at + step], rows), tables[0][...], 1, 0
            ).astype(half)
            neg_dst_out[to : to + step] = dot(
                pick(neg_dst_ref[block : block + 1, at : at + step], rows), visit[...], 1, 0
            ).astype(half)


def model_body(
    rel_ref,
    count_ref,
    slot_ref,
    fetched_ref,
    src_ref,
    neg_src_ref,
    neg_dst_ref,
    relation_ref,
    outgoing_ref,
    d_src_ref,
    d_neg_src_ref,
    d_neg_dst_ref,
    d_dst,
    operator,
    op_half,
    neg_dst_sum,
    neg_src_sum,
    op_sum,
    op_turned_sum,
    op_sem,
):
    slots, width = fetched_ref.shape
    edges = src_ref.shape[0]
    blocks = rel_ref.shape[1]
    block_len = edges // blocks
    negs = neg_src_ref.shape[0] // blocks
    peers, room, _ = outgoing_ref.shape
    extra = width // peers
    places = slots // peers
    step = 256
    copies = []
    for block in range(blocks):
        copies.append(
            pltpu.make_async_copy(
                relation_ref.at[rel_ref[0, block]], operator.at[block], op_sem.at[block]
            )
        )
        copies[-1].start()
    for block in range(blocks):
        copies[block].wait()
        op_half[...] = operator[block].astype(half)
        neg_dst_sum[...] = jnp.zeros_like(neg_dst_sum)
        neg_src_sum[...] = jnp.zeros_like(neg_src_sum)
        op_sum[...] = jnp.zeros_like(op_sum)
        op_turned_sum[...] = jnp.zeros_like(op_turned_sum)

        def chunk(t, carry, block=block):
            at = pl.multiple_of(block * block_len + t * step, step)
            here = pl.ds(at, step)
            op = op_half[...]
            dst = dot(pick(slot_ref[:, here], slots), fetched_ref[...], 1, 0).astype(half)
            src = src_ref[here, :]
            negs_at = pl.ds(block * negs, negs)
            neg_dst = neg_dst_ref[negs_at, :]
            neg_src = neg_src_ref[negs_at, :]
            line = lax.broadcasted_iota(jnp.int32, (step, 1), 0) + at
            live = jnp.where(line < count_ref[0, 0], 1.0, 0.0)
            lhs = dot(src, op, 1, 0).astype(half)
            rhs = dot(dst, op, 1, 1).astype(half)
            positive = jnp.sum(lhs.astype(full) * dst.astype(full), axis=1, keepdims=True)

            def softmax(scores):
                highest = jnp.maximum(jnp.max(scores, axis=1, keepdims=True), positive)
                terms = jnp.exp(scores - highest)
                own = jnp.exp(positive - highest)
                scale = live / (own + jnp.sum(terms, axis=1, keepdims=True))
                return (terms * scale).astype(half), own * scale - live

            dst_terms, dst_own = softmax(dot(lhs, neg_dst, 1, 1))
            src_terms, src_own = softmax(dot(rhs, neg_src, 1, 1))
            d_positive = dst_own + src_own
            d_lhs = dot(dst_terms, neg_dst, 1, 0).astype(half)
            d_lhs = d_lhs + (d_positive * dst.astype(full)).astype(half)
            d_rhs = dot(src_terms, neg_src, 1, 0).astype(half)
            neg_dst_sum[...] += dot(lhs, dst_terms, 0, 0)
            neg_src_sum[...] += dot(rhs, src_terms, 0, 0)
            d_src_ref[here, :] = dot(d_lhs, op, 1, 1).astype(half)
            op_sum[...] += dot(src, d_lhs, 0, 0)
            op_turned_sum[...] += dot(d_rhs, dst, 0, 0)
            d_dst[here, :] = dot(d_rhs, op, 1, 0).astype(half) + (
                d_positive * lhs.astype(full)
            ).astype(half)
            return carry

        lax.fori_loop(0, block_len // step, chunk, 0)
        d_neg_dst_ref[block * negs : (block + 1) * negs, :] = neg_dst_sum[...].T.astype(half)
        d_neg_src_ref[block * negs : (block + 1) * negs, :] = neg_src_sum[...].T.astype(half)
        d_op = op_sum[...].astype(half) + op_turned_sum[...].astype(half)
        outgoing_ref[:, places + block * extra : places + (block + 1) * extra, :] = d_op.reshape(
            peers, extra, width
        )

    def send(t, carry):
        spot = place(slot_ref[...], t * 2 * places, 2 * places)
        out = dot(spot, d_dst[...], 1, 0).astype(half)
        outgoing_ref[pl.ds(2 * t, 2), :places, :] = out.reshape(2, places, width)
        return carry

    lax.fori_loop(0, peers // 2, send, 0)


def sums_body(src_ref, neg_src_ref, neg_dst_ref, d_src, d_neg_src, d_neg_dst, own_ref, visit_ref):
    rows = own_ref.shape[0]
    blocks, negs = neg_src_ref.shape
    step = 256

    def part(t, carry):
        first = pl.multiple_of(t * step, step)
        own = dot(place(src_ref[...], first, step), d_src[...], 1, 0)
        visit = jnp.zeros_like(own)
        for block in range(blocks):
            at = slice(block * negs, (block + 1) * negs)
            one = slice(block, block + 1)
            own += dot(place(neg_src_ref[one, :], first, step), d_neg_src[at, :], 1, 0)
            visit += dot(place(neg_dst_ref[one, :], first, step), d_neg_dst[at, :], 1, 0)
        own_ref[pl.ds(first, step), :] = own
        visit_ref[pl.ds(first, step), :] = visit
        return carry

    lax.fori_loop(0, rows // step, part, 0)


def home_body(
    parts, partner_ref, group_ref, visit_to_ref, asked_ref, returned_ref, visit_ref, *refs
):
    outs, (total, list_ref, count_ref) = refs[: len(parts)], refs[len(parts) :]
    rows, width = visit_ref.shape
    places = asked_ref.shape[2]
    list_peers(partner_ref, group_ref, list_ref, count_ref)
    for part, out_ref in zip(parts, outs):
        count = count_ref[part]
        total[...] = jnp.where(visit_to_ref[0] == part, visit_ref[...], 0.0)

        def pair(t, carry, part=part, count=count):
            one = list_ref[part, 2 * t]
            two = list_ref[part, jnp.minimum(2 * t + 1, count - 1)]
            ask_two = jnp.where(2 * t + 1 < count, asked_ref[pl.ds(two, 1), 0, :], -1)
            ask = jnp.concatenate([asked_ref[pl.ds(one, 1), 0, :], ask_two], axis=1)
            back = jnp.concatenate(
                [
                    returned_ref[pl.ds(one, 1), :places, :].reshape(places, width),
                    returned_ref[pl.ds(two, 1), :places, :].reshape(places, width),
                ],
                axis=0,
            )
            for first in range(0, rows, 512):
                total[first : first + 512] += dot(place(ask, first, 512), back, 1, 0)
            return carry

        lax.fori_loop(0, (count + 1) // 2, pair, 0)
        out_ref[...] = total[...].astype(half)


def operators_body(ids_ref, part_ref, out_ref):
    peers, _, width = part_ref.shape
    blocks = ids_ref.shape[1]
    rows = out_ref.shape[1]
    out_ref[...] = jnp.zeros_like(out_ref)

    def add(peer, carry):
        piece = part_ref[pl.ds(peer, 1)].reshape(blocks * rows, width).astype(full)
        for block in range(blocks):
            at = ids_ref[peer, block]
            out_ref[pl.ds(at, 1)] += piece[block * rows : (block + 1) * rows].reshape(1, rows, width)
        return carry

    lax.fori_loop(0, peers, add, 0)


def laid(column):
    return jnp.broadcast_to(column, (column.shape[0], 128)).T[:1, :]


def relation_body(core_ref, mine_ref, other_ref, relation_ref, acc_ref, new_ref, acc_new_ref):
    step, rows, width = relation_ref.shape
    at = pl.program_id(0)
    own_half = at // (pl.num_programs(0) // 2) == core_ref[0]
    for k in range(step):
        line = at * step + k
        mine = mine_ref[:, k].astype(full).reshape(rows, width)
        other = other_ref[:, k].astype(full).reshape(rows, width)
        grad = jnp.where(own_half, mine, other)
        square = jnp.mean(grad * grad, axis=1, keepdims=True)
        acc = acc_ref[pl.ds(line, 1), :]
        acc_new_ref[pl.ds(line, 1), :] = acc + laid(square)
        rate = step_rate / jnp.sqrt(turned(acc)[:, :1] + square)
        new_ref[k] = relation_ref[k] - grad * rate


def entity_body(grad_ref, home_ref, sibling_ref, cross_ref, entity_ref, acc_ref, new_ref, acc_new_ref):
    grad = (
        grad_ref[...]
        + home_ref[...].astype(full)
        + sibling_ref[...].astype(full)
        + cross_ref[...].astype(full)
    )
    square = jnp.mean(grad * grad, axis=1, keepdims=True)
    acc = acc_ref[...]
    acc_new_ref[...] = acc + laid(square)
    new_ref[0] = entity_ref[0] - grad * (step_rate / jnp.sqrt(turned(acc)[:, :1] + square))


def relation_update(core, mine, other, relation, relation_acc):
    peers, count, extra, width = mine.shape
    relations, rows = relation_acc.shape
    step = 4 if count % 4 == 0 else 1
    steps = count // step

    def near(flip):
        def at(i, core):
            return (0, jnp.clip(i - steps * (core[0] ^ flip), 0, steps - 1), 0, 0)

        return pl.BlockSpec((peers, step, extra, width), at)

    whole = pl.BlockSpec((relations, rows), lambda i, core: (0, 0))
    block = pl.BlockSpec((step, rows, width), lambda i, core: (i, 0, 0))
    return pl.pallas_call(
        relation_body,
        grid_spec=pltpu.PrefetchScalarGridSpec(
            num_scalar_prefetch=1,
            grid=(2 * steps,),
            in_specs=[near(0), near(1), block, whole],
            out_specs=[block, whole],
        ),
        out_shape=[
            jax.ShapeDtypeStruct(relation.shape, full),
            jax.ShapeDtypeStruct(relation_acc.shape, full),
        ],
        compiler_params=pltpu.CompilerParams(vmem_limit_bytes=VMEM_BYTES),
    )(core, mine, other, relation, relation_acc)


def entity_update(grad, home, sibling, cross, entity, entity_acc):
    rows, width = grad.shape
    step = 256
    part = pl.BlockSpec((step, width), lambda i: (i, 0))
    block = pl.BlockSpec((1, step, width), lambda i: (0, i, 0))
    line = pl.BlockSpec((1, step), lambda i: (0, i))
    return pl.pallas_call(
        entity_body,
        grid=(rows // step,),
        in_specs=[part] * 4 + [block, line],
        out_specs=[block, line],
        out_shape=[
            jax.ShapeDtypeStruct(entity.shape, full),
            jax.ShapeDtypeStruct(entity_acc.shape, full),
        ],
        compiler_params=pltpu.CompilerParams(vmem_limit_bytes=VMEM_BYTES),
    )(grad, home, sibling, cross, entity, entity_acc)


def on_device(
    entity,
    entity_acc,
    relation,
    relation_acc,
    partner,
    src_row,
    dst_owner,
    dst_row,
    rel_ids,
    neg_src,
    neg_dst,
    edge_count,
):
    me = lax.axis_index("grp")
    place_id = lax.axis_index("dev")
    peers = lax.axis_size("dev")
    rows, width = entity.shape[1:]
    edges = src_row.shape[1]
    blocks = rel_ids.shape[1]
    negs = neg_src.shape[2]
    relations = relation.shape[0]
    room = 2 * edges // peers
    extra = width // peers
    sds = jax.ShapeDtypeStruct

    def neighbour(x, flip):
        return lax.ppermute(x, "grp", [(g, g ^ flip) for g in range(4)])

    group = me.reshape(1)
    visit_to = (partner[me, place_id] ^ me).reshape(1)
    owners = dst_owner.reshape(1, edges)
    neg_src = neg_src.reshape(blocks, negs)
    neg_dst = neg_dst.reshape(blocks, negs)

    own = entity[0].astype(half)
    cross = neighbour(own, 2)
    sibling = neighbour(own, 1)
    slot, wanted = call(
        slots_body,
        (sds((1, edges), jnp.int32), sds((peers, 2, room), jnp.int32)),
        specs=[SMEM] + [VMEM] * 2,
    )(rel_ids, owners, dst_row)
    asked = lax.all_to_all(wanted, "dev", split_axis=0, concat_axis=0, tiled=True)
    cross, asked = lax.optimization_barrier((cross, asked))
    cross_sibling = neighbour(cross, 1)
    tables = (own, sibling, cross, cross_sibling)

    lists = [pltpu.SMEM((4, peers), jnp.int32), pltpu.SMEM((4,), jnp.int32)]
    found = call(
        answer_body,
        sds((peers, room, width), half),
        lists,
        [SMEM] * 2 + [VMEM] * 5,
    )(partner, group, asked, *tables)
    fetched = lax.all_to_all(found, "dev", split_axis=0, concat_axis=0, tiled=True)

    src_rows, neg_src_rows, neg_dst_rows = call(
        rows_body,
        (sds((edges, width), half), sds((blocks * negs, width), half), sds((blocks * negs, width), half)),
        [pltpu.VMEM((rows, width), half)],
        [SMEM] + [VMEM] * 7,
        cost(2 * 3 * edges * rows * width, 6 * rows * width * 2),
    )(visit_to, src_row, neg_src, neg_dst, *tables)

    outgoing, d_src, d_neg_src, d_neg_dst = call(
        model_body,
        (
            sds((peers, room + blocks * extra, width), half),
            sds((edges, width), half),
            sds((blocks * negs, width), half),
            sds((blocks * negs, width), half),
        ),
        [
            pltpu.VMEM((edges, width), half),
            pltpu.VMEM((blocks, width, width), full),
            pltpu.VMEM((width, width), half),
            pltpu.VMEM((width, negs), full),
            pltpu.VMEM((width, negs), full),
            pltpu.VMEM((width, width), full),
            pltpu.VMEM((width, width), full),
            pltpu.SemaphoreType.DMA((blocks,)),
        ],
        [SMEM] * 2 + [VMEM] * 5 + [pl.BlockSpec(memory_space=pl.ANY)],
    )(
        rel_ids,
        edge_count,
        slot,
        fetched.reshape(peers * room, width),
        src_rows,
        neg_src_rows,
        neg_dst_rows,
        relation,
    )
    returned = lax.all_to_all(outgoing, "dev", split_axis=0, concat_axis=0, tiled=True)

    own_grad, visit_grad = call(
        sums_body,
        (sds((rows, width), full), sds((rows, width), full)),
        (),
        [VMEM] * 6,
        cost(2 * 3 * edges * rows * width, 7 * rows * width * 2),
    )(src_row, neg_src, neg_dst, d_src, d_neg_src, d_neg_dst)

    rel_part = call(operators_body, sds((relations, extra, width), full), (), [SMEM, VMEM])(
        asked[:, 1, :blocks], returned[:, room:, :]
    )
    core = me & 1
    halves = rel_part.reshape(2, relations // 2, extra, width)
    mine = lax.dynamic_index_in_dim(halves, core, 0, keepdims=False)
    other = lax.dynamic_index_in_dim(halves, 1 - core, 0, keepdims=False)
    chip = mine + neighbour(other, 1)
    pair = (chip + neighbour(chip, 2)).astype(half)
    gathered = lax.all_to_all(
        jnp.broadcast_to(pair[None], (peers,) + pair.shape), "dev", split_axis=0, concat_axis=0, tiled=True
    )
    other_half = neighbour(gathered, 1)

    def home(parts):
        return call(
            functools.partial(home_body, parts),
            tuple(sds((rows, width), half) for _ in parts),
            [pltpu.VMEM((rows, width), full)] + lists,
            [SMEM] * 3 + [VMEM] * 3,
        )(partner, group, visit_to, asked, returned, visit_grad)

    home_cross_sibling, home_cross = home((3, 2))
    chip_cross = (home_cross.astype(full) + neighbour(home_cross_sibling, 1).astype(full)).astype(half)
    from_cross = neighbour(chip_cross, 2)
    home_sibling, home_own = home((1, 0))
    from_sibling = neighbour(home_sibling, 1)
    entity_new, acc_new = entity_update(
        own_grad, home_own, from_sibling, from_cross, entity, entity_acc
    )
    relation_new, relation_acc_new = relation_update(
        core.reshape(1), gathered, other_half, relation, relation_acc
    )
    return (entity_new, acc_new, relation_new, relation_acc_new)


def solution(mesh):
    return jax.shard_map(
        on_device,
        mesh=mesh,
        in_specs=(
            P("grp", "dev", None),
            P("grp", "dev"),
            P(),
            P(),
            P(),
            P("grp", "dev"),
            P("grp", "dev", None),
            P("grp", "dev"),
            P("grp", "dev"),
            P("grp", "dev", None),
            P("grp", "dev", None),
            P("grp", "dev"),
        ),
        out_specs=(P("grp", "dev", None), P("grp", "dev"), P(), P()),
        check_vma=False,
    )
```

```python
import functools

import jax
import jax.numpy as jnp
from jax import lax
from jax.experimental import pallas as pl
from jax.experimental.pallas import tpu as pltpu
from jax.sharding import PartitionSpec as P

step_rate = 0.1
MEBI = 1024 * 1024
half = jnp.bfloat16
full = jnp.float32
VMEM = pl.BlockSpec(memory_space=pltpu.VMEM)
SMEM = pl.BlockSpec(memory_space=pltpu.SMEM)


def dot(a, b, ca, cb):
    return lax.dot_general(a, b, (((ca,), (cb,)), ((), ())), preferred_element_type=full)


def turned(row):
    pieces = [
        jnp.broadcast_to(row[:, at : at + 128], (128, 128)).T for at in range(0, row.shape[1], 128)
    ]
    return pieces[0] if len(pieces) == 1 else jnp.concatenate(pieces, axis=0)


def pick(row, width):
    spread = turned(row.astype(full))
    lane = lax.broadcasted_iota(jnp.int32, (1, 128), 1).astype(full)
    pieces = [
        jnp.where(spread == lane + float(at), 1.0, 0.0).astype(half) for at in range(0, width, 128)
    ]
    return jnp.concatenate(pieces, axis=1)


def place(row, first, height):
    line = lax.broadcasted_iota(jnp.int32, (height, 1), 0) + first
    return jnp.where(row == line, 1.0, 0.0).astype(half)


def call(body, outs, scratch=(), specs=None, cost=None, mebi=16, **kw):
    return pl.pallas_call(
        body,
        out_shape=outs,
        in_specs=specs,
        out_specs=jax.tree.map(lambda _: VMEM, outs),
        scratch_shapes=list(scratch),
        compiler_params=pltpu.CompilerParams(vmem_limit_bytes=mebi * MEBI),
        cost_estimate=cost,
        **kw,
    )


def cost(flops, moved):
    return pl.CostEstimate(flops=int(flops), bytes_accessed=int(moved), transcendentals=0)


def slots_body(rel_ref, owner_ref, row_ref, slot_ref, wanted_ref):
    peers, _, room = wanted_ref.shape
    edges = owner_ref.shape[1]
    step = 256
    before = lax.broadcasted_iota(jnp.int32, (step, step), 0)
    after = lax.broadcasted_iota(jnp.int32, (step, step), 1)
    upper = jnp.where(before <= after, 1.0, 0.0).astype(half)
    peer = lax.broadcasted_iota(jnp.int32, (peers, step), 0)
    carry = jnp.zeros((peers, 1), full)
    high = jnp.zeros((peers, room), full)
    low = jnp.zeros((peers, room), full)
    for at in range(0, edges, step):
        owner = owner_ref[:, at : at + step]
        hit = jnp.where(peer == owner, 1.0, 0.0)
        count = dot(hit.astype(half), upper, 1, 0) + carry
        carry = count[:, step - 1 :]
        order = (jnp.sum(count * hit, axis=0, keepdims=True) - 1.0).astype(jnp.int32)
        slot_ref[:, at : at + step] = owner * room + order
        spot = place(order, 0, room)
        row = row_ref[:, at : at + step]
        top = lax.shift_right_logical(row, 4)
        high += dot((hit * top.astype(full)).astype(half), spot, 1, 1)
        low += dot((hit * (row - top * 16).astype(full)).astype(half), spot, 1, 1)
    wanted_ref[:, 0, :] = (high * 16.0 + low).astype(jnp.int32)
    lane = lax.broadcasted_iota(jnp.int32, (peers, room), 1)
    ids = jnp.zeros((peers, room), jnp.int32)
    for block in range(rel_ref.shape[1]):
        ids = jnp.where(lane == block, rel_ref[0, block], ids)
    wanted_ref[:, 1, :] = ids


def list_peers(partner_ref, group_ref, list_ref, count_ref):
    peers = partner_ref.shape[1]
    me = group_ref[0]
    for part in range(4):
        count_ref[part] = 0

    def add(peer, carry):
        part = partner_ref[me, peer] ^ me
        at = count_ref[part]
        list_ref[part, at] = peer
        count_ref[part] = at + 1
        return carry

    lax.fori_loop(0, peers, add, 0)


def answer_body(partner_ref, group_ref, asked_ref, *refs):
    tables, (found_ref, list_ref, count_ref) = refs[:4], refs[4:]
    rows, width = tables[0].shape
    room = asked_ref.shape[2]
    list_peers(partner_ref, group_ref, list_ref, count_ref)
    for part in range(4):
        count = count_ref[part]

        def pair(t, carry, part=part, count=count):
            one = list_ref[part, 2 * t]
            two = list_ref[part, jnp.minimum(2 * t + 1, count - 1)]
            ask = jnp.concatenate(
                [asked_ref[pl.ds(one, 1), 0, :], asked_ref[pl.ds(two, 1), 0, :]], axis=1
            )
            got = dot(pick(ask, rows), tables[part][...], 1, 0).astype(half)
            found_ref[pl.ds(one, 1)] = got[:room].reshape(1, room, width)
            found_ref[pl.ds(two, 1)] = got[room:].reshape(1, room, width)
            return carry

        lax.fori_loop(0, (count + 1) // 2, pair, 0)


def rows_body(visit_ref, src_ref, neg_src_ref, neg_dst_ref, *refs):
    tables, (src_out, neg_src_out, neg_dst_out, visit) = refs[:4], refs[4:]
    rows = tables[0].shape[0]
    for part in range(4):

        @pl.when(visit_ref[0] == part)
        def _(part=part):
            visit[...] = tables[part][...]

    step = 256
    blocks, negs = neg_src_ref.shape
    for at in range(0, src_ref.shape[1], step):
        src_out[at : at + step] = dot(
            pick(src_ref[:, at : at + step], rows), tables[0][...], 1, 0
        ).astype(half)
    for block in range(blocks):
        for at in range(0, negs, step):
            to = block * negs + at
            neg_src_out[to : to + step] = dot(
                pick(neg_src_ref[block : block + 1, at : at + step], rows), tables[0][...], 1, 0
            ).astype(half)
            neg_dst_out[to : to + step] = dot(
                pick(neg_dst_ref[block : block + 1, at : at + step], rows), visit[...], 1, 0
            ).astype(half)


def model_body(
    rel_ref,
    count_ref,
    slot_ref,
    fetched_ref,
    src_ref,
    neg_src_ref,
    neg_dst_ref,
    relation_ref,
    outgoing_ref,
    d_src_ref,
    d_neg_src_ref,
    d_neg_dst_ref,
    d_dst,
    operator,
    op_half,
    neg_dst_sum,
    neg_src_sum,
    op_sum,
    op_turned_sum,
    op_sem,
):
    slots, width = fetched_ref.shape
    edges = src_ref.shape[0]
    blocks = rel_ref.shape[1]
    block_len = edges // blocks
    negs = neg_src_ref.shape[0] // blocks
    peers, room, _ = outgoing_ref.shape
    extra = width // peers
    places = slots // peers
    step = 256
    copies = []
    for block in range(blocks):
        copies.append(
            pltpu.make_async_copy(
                relation_ref.at[rel_ref[0, block]], operator.at[block], op_sem.at[block]
            )
        )
        copies[-1].start()
    for block in range(blocks):
        copies[block].wait()
        op_half[...] = operator[block].astype(half)
        neg_dst_sum[...] = jnp.zeros_like(neg_dst_sum)
        neg_src_sum[...] = jnp.zeros_like(neg_src_sum)
        op_sum[...] = jnp.zeros_like(op_sum)
        op_turned_sum[...] = jnp.zeros_like(op_turned_sum)

        def chunk(t, carry, block=block):
            at = pl.multiple_of(block * block_len + t * step, step)
            here = pl.ds(at, step)
            op = op_half[...]
            dst = dot(pick(slot_ref[:, here], slots), fetched_ref[...], 1, 0).astype(half)
            src = src_ref[here, :]
            negs_at = pl.ds(block * negs, negs)
            neg_dst = neg_dst_ref[negs_at, :]
            neg_src = neg_src_ref[negs_at, :]
            line = lax.broadcasted_iota(jnp.int32, (step, 1), 0) + at
            live = jnp.where(line < count_ref[0, 0], 1.0, 0.0)
            lhs = dot(src, op, 1, 0).astype(half)
            rhs = dot(dst, op, 1, 1).astype(half)
            positive = jnp.sum(lhs.astype(full) * dst.astype(full), axis=1, keepdims=True)

            def softmax(scores):
                highest = jnp.maximum(jnp.max(scores, axis=1, keepdims=True), positive)
                terms = jnp.exp(scores - highest)
                own = jnp.exp(positive - highest)
                scale = live / (own + jnp.sum(terms, axis=1, keepdims=True))
                return (terms * scale).astype(half), own * scale - live

            dst_terms, dst_own = softmax(dot(lhs, neg_dst, 1, 1))
            src_terms, src_own = softmax(dot(rhs, neg_src, 1, 1))
            d_positive = dst_own + src_own
            d_lhs = dot(dst_terms, neg_dst, 1, 0).astype(half)
            d_lhs = d_lhs + (d_positive * dst.astype(full)).astype(half)
            d_rhs = dot(src_terms, neg_src, 1, 0).astype(half)
            neg_dst_sum[...] += dot(lhs, dst_terms, 0, 0)
            neg_src_sum[...] += dot(rhs, src_terms, 0, 0)
            d_src_ref[here, :] = dot(d_lhs, op, 1, 1).astype(half)
            op_sum[...] += dot(src, d_lhs, 0, 0)
            op_turned_sum[...] += dot(d_rhs, dst, 0, 0)
            d_dst[here, :] = dot(d_rhs, op, 1, 0).astype(half) + (
                d_positive * lhs.astype(full)
            ).astype(half)
            return carry

        lax.fori_loop(0, block_len // step, chunk, 0)
        d_neg_dst_ref[block * negs : (block + 1) * negs, :] = neg_dst_sum[...].T.astype(half)
        d_neg_src_ref[block * negs : (block + 1) * negs, :] = neg_src_sum[...].T.astype(half)
        d_op = op_sum[...].astype(half) + op_turned_sum[...].astype(half)
        outgoing_ref[:, places + block * extra : places + (block + 1) * extra, :] = d_op.reshape(
            peers, extra, width
        )

    def send(t, carry):
        spot = place(slot_ref[...], t * 2 * places, 2 * places)
        out = dot(spot, d_dst[...], 1, 0).astype(half)
        outgoing_ref[pl.ds(2 * t, 2), :places, :] = out.reshape(2, places, width)
        return carry

    lax.fori_loop(0, peers // 2, send, 0)


def sums_body(src_ref, neg_src_ref, neg_dst_ref, d_src, d_neg_src, d_neg_dst, own_ref, visit_ref):
    rows = own_ref.shape[0]
    blocks, negs = neg_src_ref.shape
    step = 256

    def part(t, carry):
        first = pl.multiple_of(t * step, step)
        own = dot(place(src_ref[...], first, step), d_src[...], 1, 0)
        visit = jnp.zeros_like(own)
        for block in range(blocks):
            at = slice(block * negs, (block + 1) * negs)
            one = slice(block, block + 1)
            own += dot(place(neg_src_ref[one, :], first, step), d_neg_src[at, :], 1, 0)
            visit += dot(place(neg_dst_ref[one, :], first, step), d_neg_dst[at, :], 1, 0)
        own_ref[pl.ds(first, step), :] = own
        visit_ref[pl.ds(first, step), :] = visit
        return carry

    lax.fori_loop(0, rows // step, part, 0)


def home_body(
    parts, partner_ref, group_ref, visit_to_ref, asked_ref, returned_ref, visit_ref, *refs
):
    outs, (total, list_ref, count_ref) = refs[: len(parts)], refs[len(parts) :]
    rows, width = visit_ref.shape
    places = asked_ref.shape[2]
    list_peers(partner_ref, group_ref, list_ref, count_ref)
    for part, out_ref in zip(parts, outs):
        count = count_ref[part]
        total[...] = jnp.where(visit_to_ref[0] == part, visit_ref[...], 0.0)

        def pair(t, carry, part=part, count=count):
            one = list_ref[part, 2 * t]
            two = list_ref[part, jnp.minimum(2 * t + 1, count - 1)]
            ask_two = jnp.where(2 * t + 1 < count, asked_ref[pl.ds(two, 1), 0, :], -1)
            ask = jnp.concatenate([asked_ref[pl.ds(one, 1), 0, :], ask_two], axis=1)
            back = jnp.concatenate(
                [
                    returned_ref[pl.ds(one, 1), :places, :].reshape(places, width),
                    returned_ref[pl.ds(two, 1), :places, :].reshape(places, width),
                ],
                axis=0,
            )
            for first in range(0, rows, 512):
                total[first : first + 512] += dot(place(ask, first, 512), back, 1, 0)
            return carry

        lax.fori_loop(0, (count + 1) // 2, pair, 0)
        out_ref[...] = total[...].astype(half)


def operators_body(ids_ref, part_ref, out_ref):
    peers, _, width = part_ref.shape
    blocks = ids_ref.shape[1]
    rows = out_ref.shape[1]
    out_ref[...] = jnp.zeros_like(out_ref)

    def add(peer, carry):
        piece = part_ref[pl.ds(peer, 1)].reshape(blocks * rows, width).astype(full)
        for block in range(blocks):
            at = ids_ref[peer, block]
            out_ref[pl.ds(at, 1)] += piece[block * rows : (block + 1) * rows].reshape(1, rows, width)
        return carry

    lax.fori_loop(0, peers, add, 0)


def laid(column):
    return jnp.broadcast_to(column, (column.shape[0], 128)).T[:1, :]


def relation_body(
    core_ref, mine_ref, other_ref, relation_ref, acc_ref, new_ref, acc_new_ref, acc_turned, acc_found
):
    step, rows, width = relation_ref.shape
    relations = acc_ref.shape[0]
    at = pl.program_id(0)
    own_half = at // (pl.num_programs(0) // 2) == core_ref[0]
    lane = lax.broadcasted_iota(jnp.int32, (rows, 128), 1)

    @pl.when(at == 0)
    def _():
        short = jnp.zeros((128 - relations, rows), full)
        acc_turned[...] = jnp.concatenate([acc_ref[...], short], axis=0).T
        acc_found[...] = jnp.zeros_like(acc_found)

    for k in range(step):
        here = lane == at * step + k
        mine = mine_ref[:, k].astype(full).reshape(rows, width)
        other = other_ref[:, k].astype(full).reshape(rows, width)
        grad = jnp.where(own_half, mine, other)
        square = grad * grad
        parts = sum(square[:, first : first + 128] for first in range(0, width, 128))
        acc = jnp.sum(
            parts * (1.0 / width) + jnp.where(here, acc_turned[...], 0.0), axis=1, keepdims=True
        )
        acc_found[...] = jnp.where(here, acc, acc_found[...])
        new_ref[k] = relation_ref[k] - grad * (step_rate / jnp.sqrt(acc))

    @pl.when(at == pl.num_programs(0) - 1)
    def _():
        acc_new_ref[...] = acc_found[...].T[:relations]


def entity_body(grad_ref, home_ref, sibling_ref, cross_ref, entity_ref, acc_ref, new_ref, acc_new_ref):
    grad = (
        grad_ref[...]
        + home_ref[...].astype(full)
        + sibling_ref[...].astype(full)
        + cross_ref[...].astype(full)
    )
    square = jnp.mean(grad * grad, axis=1, keepdims=True)
    acc = acc_ref[...]
    acc_new_ref[...] = acc + laid(square)
    new_ref[0] = entity_ref[0] - grad * (step_rate / jnp.sqrt(turned(acc)[:, :1] + square))


def relation_update(core, mine, other, relation, relation_acc):
    peers, count, extra, width = mine.shape
    relations, rows = relation_acc.shape
    step = 4 if count % 4 == 0 else 1
    steps = count // step

    def near(flip):
        def at(i, core):
            return (0, jnp.clip(i - steps * (core[0] ^ flip), 0, steps - 1), 0, 0)

        return pl.BlockSpec((peers, step, extra, width), at)

    whole = pl.BlockSpec((relations, rows), lambda i, core: (0, 0))
    block = pl.BlockSpec((step, rows, width), lambda i, core: (i, 0, 0))
    return pl.pallas_call(
        relation_body,
        grid_spec=pltpu.PrefetchScalarGridSpec(
            num_scalar_prefetch=1,
            grid=(2 * steps,),
            in_specs=[near(0), near(1), block, whole],
            out_specs=[block, whole],
            scratch_shapes=[pltpu.VMEM((rows, 128), full), pltpu.VMEM((rows, 128), full)],
        ),
        out_shape=[
            jax.ShapeDtypeStruct(relation.shape, full),
            jax.ShapeDtypeStruct(relation_acc.shape, full),
        ],
        compiler_params=pltpu.CompilerParams(vmem_limit_bytes=16 * MEBI),
    )(core, mine, other, relation, relation_acc)


def entity_update(grad, home, sibling, cross, entity, entity_acc):
    rows, width = grad.shape
    step = 256
    part = pl.BlockSpec((step, width), lambda i: (i, 0))
    block = pl.BlockSpec((1, step, width), lambda i: (0, i, 0))
    line = pl.BlockSpec((1, step), lambda i: (0, i))
    return pl.pallas_call(
        entity_body,
        grid=(rows // step,),
        in_specs=[part] * 4 + [block, line],
        out_specs=[block, line],
        out_shape=[
            jax.ShapeDtypeStruct(entity.shape, full),
            jax.ShapeDtypeStruct(entity_acc.shape, full),
        ],
        compiler_params=pltpu.CompilerParams(vmem_limit_bytes=16 * MEBI),
    )(grad, home, sibling, cross, entity, entity_acc)


def on_device(
    entity,
    entity_acc,
    relation,
    relation_acc,
    partner,
    src_row,
    dst_owner,
    dst_row,
    rel_ids,
    neg_src,
    neg_dst,
    edge_count,
):
    me = lax.axis_index("grp")
    place_id = lax.axis_index("dev")
    peers = lax.axis_size("dev")
    rows, width = entity.shape[1:]
    edges = src_row.shape[1]
    blocks = rel_ids.shape[1]
    negs = neg_src.shape[2]
    relations = relation.shape[0]
    room = 2 * edges // peers
    extra = width // peers
    sds = jax.ShapeDtypeStruct

    def neighbour(x, flip):
        return lax.ppermute(x, "grp", [(g, g ^ flip) for g in range(4)])

    group = me.reshape(1)
    visit_to = (partner[me, place_id] ^ me).reshape(1)
    owners = dst_owner.reshape(1, edges)
    neg_src = neg_src.reshape(blocks, negs)
    neg_dst = neg_dst.reshape(blocks, negs)

    own = entity[0].astype(half)
    cross = neighbour(own, 2)
    sibling = neighbour(own, 1)
    slot, wanted = call(
        slots_body,
        (sds((1, edges), jnp.int32), sds((peers, 2, room), jnp.int32)),
        specs=[SMEM] + [VMEM] * 2,
    )(rel_ids, owners, dst_row)
    asked = lax.all_to_all(wanted, "dev", split_axis=0, concat_axis=0, tiled=True)
    cross, asked = lax.optimization_barrier((cross, asked))
    cross_sibling = neighbour(cross, 1)
    tables = (own, sibling, cross, cross_sibling)

    lists = [pltpu.SMEM((4, peers), jnp.int32), pltpu.SMEM((4,), jnp.int32)]
    found = call(
        answer_body,
        sds((peers, room, width), half),
        lists,
        [SMEM] * 2 + [VMEM] * 5,
    )(partner, group, asked, *tables)
    fetched = lax.all_to_all(found, "dev", split_axis=0, concat_axis=0, tiled=True)

    src_rows, neg_src_rows, neg_dst_rows = call(
        rows_body,
        (sds((edges, width), half), sds((blocks * negs, width), half), sds((blocks * negs, width), half)),
        [pltpu.VMEM((rows, width), half)],
        [SMEM] + [VMEM] * 7,
        cost(2 * 3 * edges * rows * width, 6 * rows * width * 2),
    )(visit_to, src_row, neg_src, neg_dst, *tables)

    outgoing, d_src, d_neg_src, d_neg_dst = call(
        model_body,
        (
            sds((peers, room + blocks * extra, width), half),
            sds((edges, width), half),
            sds((blocks * negs, width), half),
            sds((blocks * negs, width), half),
        ),
        [
            pltpu.VMEM((edges, width), half),
            pltpu.VMEM((blocks, width, width), full),
            pltpu.VMEM((width, width), half),
            pltpu.VMEM((width, negs), full),
            pltpu.VMEM((width, negs), full),
            pltpu.VMEM((width, width), full),
            pltpu.VMEM((width, width), full),
            pltpu.SemaphoreType.DMA((blocks,)),
        ],
        [SMEM] * 2 + [VMEM] * 5 + [pl.BlockSpec(memory_space=pl.ANY)],
        mebi=28,
    )(
        rel_ids,
        edge_count,
        slot,
        fetched.reshape(peers * room, width),
        src_rows,
        neg_src_rows,
        neg_dst_rows,
        relation,
    )
    returned = lax.all_to_all(outgoing, "dev", split_axis=0, concat_axis=0, tiled=True)

    own_grad, visit_grad = call(
        sums_body,
        (sds((rows, width), full), sds((rows, width), full)),
        (),
        [VMEM] * 6,
        cost(2 * 3 * edges * rows * width, 7 * rows * width * 2),
    )(src_row, neg_src, neg_dst, d_src, d_neg_src, d_neg_dst)

    returned, own_grad, visit_grad = lax.optimization_barrier((returned, own_grad, visit_grad))
    rel_part = call(operators_body, sds((relations, extra, width), full), (), [SMEM, VMEM])(
        asked[:, 1, :blocks], returned[:, room:, :]
    )
    core = me & 1
    halves = rel_part.reshape(2, relations // 2, extra, width)
    mine = lax.dynamic_index_in_dim(halves, core, 0, keepdims=False)
    other = lax.dynamic_index_in_dim(halves, 1 - core, 0, keepdims=False)
    chip = mine + neighbour(other, 1)
    pair = (chip + neighbour(chip, 2)).astype(half)
    gathered = lax.all_to_all(
        jnp.broadcast_to(pair[None], (peers,) + pair.shape), "dev", split_axis=0, concat_axis=0, tiled=True
    )
    def home(parts):
        return call(
            functools.partial(home_body, parts),
            tuple(sds((rows, width), half) for _ in parts),
            [pltpu.VMEM((rows, width), full)] + lists,
            [SMEM] * 3 + [VMEM] * 3,
        )(partner, group, visit_to, asked, returned, visit_grad)

    home_cross_sibling, home_cross = home((3, 2))
    chip_cross = (home_cross.astype(full) + neighbour(home_cross_sibling, 1).astype(full)).astype(half)
    from_cross = neighbour(chip_cross, 2)
    home_sibling, home_own = home((1, 0))
    from_sibling = neighbour(home_sibling, 1)
    gathered, from_cross, home_own, from_sibling = lax.optimization_barrier(
        (gathered, from_cross, home_own, from_sibling)
    )
    other_half = neighbour(gathered, 1)
    entity_new, acc_new = entity_update(
        own_grad, home_own, from_sibling, from_cross, entity, entity_acc
    )
    relation_new, relation_acc_new = relation_update(
        core.reshape(1), gathered, other_half, relation, relation_acc
    )
    return (entity_new, acc_new, relation_new, relation_acc_new)


def solution(mesh):
    return jax.shard_map(
        on_device,
        mesh=mesh,
        in_specs=(
            P("grp", "dev", None),
            P("grp", "dev"),
            P(),
            P(),
            P(),
            P("grp", "dev"),
            P("grp", "dev", None),
            P("grp", "dev"),
            P("grp", "dev"),
            P("grp", "dev", None),
            P("grp", "dev", None),
            P("grp", "dev"),
        ),
        out_specs=(P("grp", "dev", None), P("grp", "dev"), P(), P()),
        check_vma=False,
    )
```

```python
import functools

import jax
import jax.numpy as jnp
from jax import lax
from jax.experimental import pallas as pl
from jax.experimental.pallas import tpu as pltpu
from jax.sharding import PartitionSpec as P

step_rate = 0.1
MEBI = 1024 * 1024
half = jnp.bfloat16
full = jnp.float32
VMEM = pl.BlockSpec(memory_space=pltpu.VMEM)
SMEM = pl.BlockSpec(memory_space=pltpu.SMEM)
ANY = pl.BlockSpec(memory_space=pl.ANY)


def dot(a, b, ca, cb):
    return lax.dot_general(a, b, (((ca,), (cb,)), ((), ())), preferred_element_type=full)


def turned(row):
    pieces = [
        jnp.broadcast_to(row[:, at : at + 128], (128, 128)).T for at in range(0, row.shape[1], 128)
    ]
    return pieces[0] if len(pieces) == 1 else jnp.concatenate(pieces, axis=0)


def pick(row, width):
    spread = turned(row.astype(full))
    lane = lax.broadcasted_iota(jnp.int32, (1, 128), 1).astype(full)
    pieces = [
        jnp.where(spread == lane + float(at), 1.0, 0.0).astype(half) for at in range(0, width, 128)
    ]
    return jnp.concatenate(pieces, axis=1)


def place(row, first, height):
    line = lax.broadcasted_iota(jnp.int32, (height, 1), 0) + first
    return jnp.where(row == line, 1.0, 0.0).astype(half)


def call(body, shapes, scratch=(), specs=None, cost=None, outs=None, mebi=60, **kw):
    return pl.pallas_call(
        body,
        out_shape=shapes,
        in_specs=specs,
        out_specs=outs or jax.tree.map(lambda _: VMEM, shapes),
        scratch_shapes=list(scratch),
        compiler_params=pltpu.CompilerParams(vmem_limit_bytes=mebi * MEBI),
        cost_estimate=cost,
        **kw,
    )


def cost(flops, moved):
    return pl.CostEstimate(flops=int(flops), bytes_accessed=int(moved), transcendentals=0)


def slots_body(rel_ref, owner_ref, row_ref, slot_ref, wanted_ref):
    peers, _, room = wanted_ref.shape
    edges = owner_ref.shape[1]
    step = 256
    before = lax.broadcasted_iota(jnp.int32, (step, step), 0)
    after = lax.broadcasted_iota(jnp.int32, (step, step), 1)
    upper = jnp.where(before <= after, 1.0, 0.0).astype(half)
    peer = lax.broadcasted_iota(jnp.int32, (peers, step), 0)
    carry = jnp.zeros((peers, 1), full)
    high = jnp.zeros((peers, room), full)
    low = jnp.zeros((peers, room), full)
    for at in range(0, edges, step):
        owner = owner_ref[:, at : at + step]
        hit = jnp.where(peer == owner, 1.0, 0.0)
        count = dot(hit.astype(half), upper, 1, 0) + carry
        carry = count[:, step - 1 :]
        order = (jnp.sum(count * hit, axis=0, keepdims=True) - 1.0).astype(jnp.int32)
        slot_ref[:, at : at + step] = owner * room + order
        spot = place(order, 0, room)
        row = row_ref[:, at : at + step]
        top = lax.shift_right_logical(row, 4)
        high += dot((hit * top.astype(full)).astype(half), spot, 1, 1)
        low += dot((hit * (row - top * 16).astype(full)).astype(half), spot, 1, 1)
    wanted_ref[:, 0, :] = (high * 16.0 + low).astype(jnp.int32)
    lane = lax.broadcasted_iota(jnp.int32, (peers, room), 1)
    ids = jnp.zeros((peers, room), jnp.int32)
    for block in range(rel_ref.shape[1]):
        ids = jnp.where(lane == block, rel_ref[0, block], ids)
    wanted_ref[:, 1, :] = ids


def list_peers(partner_ref, group_ref, list_ref, count_ref):
    peers = partner_ref.shape[1]
    me = group_ref[0]
    for part in range(4):
        count_ref[part] = 0

    def add(peer, carry):
        part = partner_ref[me, peer] ^ me
        at = count_ref[part]
        list_ref[part, at] = peer
        count_ref[part] = at + 1
        return carry

    lax.fori_loop(0, peers, add, 0)


def answer_body(partner_ref, group_ref, asked_ref, *refs):
    tables, (found_ref, list_ref, count_ref) = refs[:4], refs[4:]
    rows, width = tables[0].shape
    room = asked_ref.shape[2]
    list_peers(partner_ref, group_ref, list_ref, count_ref)
    for part in range(4):
        count = count_ref[part]

        def pair(t, carry, part=part, count=count):
            one = list_ref[part, 2 * t]
            two = list_ref[part, jnp.minimum(2 * t + 1, count - 1)]
            ask = jnp.concatenate(
                [asked_ref[pl.ds(one, 1), 0, :], asked_ref[pl.ds(two, 1), 0, :]], axis=1
            )
            got = dot(pick(ask, rows), tables[part][...], 1, 0).astype(half)
            found_ref[pl.ds(one, 1)] = got[:room].reshape(1, room, width)
            found_ref[pl.ds(two, 1)] = got[room:].reshape(1, room, width)
            return carry

        lax.fori_loop(0, (count + 1) // 2, pair, 0)


def operators_in(rel_ref, relation_ref, operator, sems):
    copies = [
        pltpu.make_async_copy(relation_ref.at[rel_ref[0, block]], operator.at[block], sems.at[block])
        for block in range(rel_ref.shape[1])
    ]
    for copy in copies:
        copy.start()
    return copies


def front_body(
    rel_ref,
    visit_ref,
    src_ref,
    neg_src_ref,
    neg_dst_ref,
    relation_ref,
    own_table,
    sibling_table,
    cross_table,
    cross_sibling_table,
    src_out,
    neg_src_out,
    lhs_out,
    terms_out,
    pull_out,
    stats_out,
    own,
    visit,
    neg_dst,
    operator,
    op_sems,
    own_sem,
    visit_sem,
):
    rows = own.shape[0]
    blocks, negs = neg_src_ref.shape
    edges = src_ref.shape[1]
    block_len = edges // blocks
    step = 256
    op_copies = operators_in(rel_ref, relation_ref, operator, op_sems)
    own_copy = pltpu.make_async_copy(own_table, own, own_sem)
    own_copy.start()
    for part, table in enumerate((own_table, sibling_table, cross_table, cross_sibling_table)):

        @pl.when(visit_ref[0] == part)
        def _(table=table):
            pltpu.make_async_copy(table, visit, visit_sem).start()

    own_copy.wait()
    pltpu.make_async_copy(own_table, visit, visit_sem).wait()
    for copy in op_copies:
        copy.wait()
    for block in range(blocks):
        for at in range(0, negs, step):
            to = block * negs + at
            neg_src_out[to : to + step] = dot(
                pick(neg_src_ref[block : block + 1, at : at + step], rows), own[...], 1, 0
            ).astype(half)
            neg_dst[at : at + step] = dot(
                pick(neg_dst_ref[block : block + 1, at : at + step], rows), visit[...], 1, 0
            ).astype(half)

        def chunk(t, carry, block=block):
            at = pl.multiple_of(block * block_len + t * step, step)
            here = pl.ds(at, step)
            op = operator[block].astype(half)
            src = dot(pick(src_ref[:, here], rows), own[...], 1, 0).astype(half)
            lhs = dot(src, op, 1, 0).astype(half)
            scores = dot(lhs, neg_dst[...], 1, 1)
            highest = jnp.max(scores, axis=1, keepdims=True)
            terms = jnp.exp(scores - highest)
            lane = lax.broadcasted_iota(jnp.int32, (step, 128), 1)
            stats_out[here, :] = jnp.where(lane < 64, highest, jnp.sum(terms, axis=1, keepdims=True))
            terms = terms.astype(half)
            src_out[here, :] = src
            lhs_out[here, :] = lhs
            terms_out[here, :] = terms
            pull_out[here, :] = dot(terms, neg_dst[...], 1, 0)
            return carry

        lax.fori_loop(0, block_len // step, chunk, 0, unroll=2)


def model_body(
    rel_ref,
    count_ref,
    slot_ref,
    fetched_ref,
    relation_ref,
    src_in,
    neg_src_in,
    lhs_in,
    terms_in,
    pull_in,
    stats_in,
    outgoing_ref,
    d_src_out,
    d_neg_src_out,
    d_neg_dst_out,
    src_ref,
    neg_src_ref,
    lhs_ref,
    terms_ref,
    pull_ref,
    stats_ref,
    d_src_ref,
    d_neg_src_ref,
    d_neg_dst_ref,
    dst_ref,
    d_dst,
    operator,
    neg_dst_sum,
    neg_src_sum,
    op_sum,
    op_turned_sum,
    op_sems,
    in_sems,
    out_sems,
):
    slots, width = fetched_ref.shape
    edges = slot_ref.shape[1]
    blocks = rel_ref.shape[1]
    block_len = edges // blocks
    negs = neg_src_ref.shape[0] // blocks
    peers, room, _ = outgoing_ref.shape
    extra = width // peers
    places = slots // peers
    step = 256
    copies = operators_in(rel_ref, relation_ref, operator, op_sems)
    pairs = (
        (src_in, src_ref),
        (neg_src_in, neg_src_ref),
        (lhs_in, lhs_ref),
        (pull_in, pull_ref),
        (stats_in, stats_ref),
        (terms_in, terms_ref),
    )
    for i, (there, here) in enumerate(pairs):
        copies.append(pltpu.make_async_copy(there, here, in_sems.at[i]))
        copies[-1].start()

    def fetch(t, carry):
        here = pl.ds(pl.multiple_of(t * step, step), step)
        dst_ref[here, :] = dot(pick(slot_ref[:, here], slots), fetched_ref[...], 1, 0).astype(half)
        return carry

    lax.fori_loop(0, edges // step, fetch, 0, unroll=4)
    for copy in copies:
        copy.wait()
    for block in range(blocks):
        neg_dst_sum[...] = jnp.zeros_like(neg_dst_sum)
        neg_src_sum[...] = jnp.zeros_like(neg_src_sum)
        op_sum[...] = jnp.zeros_like(op_sum)
        op_turned_sum[...] = jnp.zeros_like(op_turned_sum)

        def chunk(t, carry, block=block):
            at = pl.multiple_of(block * block_len + t * step, step)
            here = pl.ds(at, step)
            op = operator[block].astype(half)
            dst = dst_ref[here, :]
            src = src_ref[here, :]
            lhs = lhs_ref[here, :]
            neg_src = neg_src_ref[block * negs : (block + 1) * negs, :]
            line = lax.broadcasted_iota(jnp.int32, (step, 1), 0) + at
            live = jnp.where(line < count_ref[0, 0], 1.0, 0.0)
            rhs = dot(dst, op, 1, 1).astype(half)
            positive = jnp.sum(lhs.astype(full) * dst.astype(full), axis=1, keepdims=True)

            scores = dot(rhs, neg_src, 1, 1)
            highest = jnp.maximum(jnp.max(scores, axis=1, keepdims=True), positive)
            terms = jnp.exp(scores - highest)
            own = jnp.exp(positive - highest)
            scale = live / (own + jnp.sum(terms, axis=1, keepdims=True))
            src_terms = (terms * scale).astype(half)
            d_positive = own * scale - live

            top = stats_ref[here, :]
            top, total = top[:, :1], top[:, 64:65]
            highest = jnp.maximum(top, positive)
            lower = jnp.exp(top - highest)
            own = jnp.exp(positive - highest)
            scale = live / (own + total * lower)
            d_positive += own * scale - live
            scale = lower * scale

            d_lhs = (pull_ref[here, :] * scale).astype(half)
            d_lhs = d_lhs + (d_positive * dst.astype(full)).astype(half)
            d_rhs = dot(src_terms, neg_src, 1, 0).astype(half)
            scaled = (lhs.astype(full) * scale).astype(half)
            neg_dst_sum[...] += dot(scaled, terms_ref[here, :], 0, 0)
            neg_src_sum[...] += dot(rhs, src_terms, 0, 0)
            d_src_ref[here, :] = dot(d_lhs, op, 1, 1).astype(half)
            op_sum[...] += dot(src, d_lhs, 0, 0)
            op_turned_sum[...] += dot(d_rhs, dst, 0, 0)
            d_dst[here, :] = dot(d_rhs, op, 1, 0).astype(half) + (
                d_positive * lhs.astype(full)
            ).astype(half)
            return carry

        lax.fori_loop(0, block_len // step, chunk, 0, unroll=4)
        d_neg_dst_ref[block * negs : (block + 1) * negs, :] = neg_dst_sum[...].T.astype(half)
        d_neg_src_ref[block * negs : (block + 1) * negs, :] = neg_src_sum[...].T.astype(half)
        d_op = op_sum[...].astype(half) + op_turned_sum[...].astype(half)
        outgoing_ref[:, places + block * extra : places + (block + 1) * extra, :] = d_op.reshape(
            peers, extra, width
        )
    backs = []
    for i, (here, there) in enumerate(
        ((d_src_ref, d_src_out), (d_neg_src_ref, d_neg_src_out), (d_neg_dst_ref, d_neg_dst_out))
    ):
        backs.append(pltpu.make_async_copy(here, there, out_sems.at[i]))
        backs[-1].start()

    def send(t, carry):
        spot = place(slot_ref[...], t * 2 * places, 2 * places)
        out = dot(spot, d_dst[...], 1, 0).astype(half)
        outgoing_ref[pl.ds(2 * t, 2), :places, :] = out.reshape(2, places, width)
        return carry

    lax.fori_loop(0, peers // 2, send, 0, unroll=4)
    for copy in backs:
        copy.wait()


def front(rel_ids, visit_to, src_row, neg_src, neg_dst, relation, tables):
    rows, width = tables[0].shape
    edges = src_row.shape[1]
    blocks, negs = neg_src.shape
    sds = jax.ShapeDtypeStruct
    return call(
        front_body,
        (
            sds((edges, width), half),
            sds((blocks * negs, width), half),
            sds((edges, width), half),
            sds((edges, negs), half),
            sds((edges, width), full),
            sds((edges, 128), full),
        ),
        [
            pltpu.VMEM((rows, width), half),
            pltpu.VMEM((rows, width), half),
            pltpu.VMEM((negs, width), half),
            pltpu.VMEM((blocks, width, width), full),
            pltpu.SemaphoreType.DMA((blocks,)),
            pltpu.SemaphoreType.DMA,
            pltpu.SemaphoreType.DMA,
        ],
        [SMEM] * 2 + [VMEM] * 3 + [ANY] * 5,
        cost(2 * edges * width * (3 * rows + 2 * negs), 12 * MEBI),
    )(rel_ids, visit_to, src_row, neg_src, neg_dst, relation, *tables)


def model(rel_ids, edge_count, slot, fetched, relation, peers, room, rest):
    slots, width = fetched.shape
    edges = slot.shape[1]
    blocks = rel_ids.shape[1]
    negs = rest[1].shape[0] // blocks
    sds = jax.ShapeDtypeStruct
    return call(
        model_body,
        (
            sds((peers, room + blocks * (width // peers), width), half),
            sds((edges, width), half),
            sds((blocks * negs, width), half),
            sds((blocks * negs, width), half),
        ),
        [pltpu.VMEM(x.shape, x.dtype) for x in rest]
        + [
            pltpu.VMEM((edges, width), half),
            pltpu.VMEM((blocks * negs, width), half),
            pltpu.VMEM((blocks * negs, width), half),
            pltpu.VMEM((edges, width), half),
            pltpu.VMEM((edges, width), half),
            pltpu.VMEM((blocks, width, width), full),
            pltpu.VMEM((width, negs), full),
            pltpu.VMEM((width, negs), full),
            pltpu.VMEM((width, width), full),
            pltpu.VMEM((width, width), full),
            pltpu.SemaphoreType.DMA((blocks,)),
            pltpu.SemaphoreType.DMA((6,)),
            pltpu.SemaphoreType.DMA((3,)),
        ],
        [SMEM] * 2 + [VMEM] * 2 + [ANY] * 7,
        outs=[VMEM] + [ANY] * 3,
    )(rel_ids, edge_count, slot, fetched, relation, *rest)


def sums_body(src_ref, neg_src_ref, neg_dst_ref, d_src, d_neg_src, d_neg_dst, own_ref, visit_ref):
    rows = own_ref.shape[0]
    blocks, negs = neg_src_ref.shape
    step = 256

    def part(t, carry):
        first = pl.multiple_of(t * step, step)
        own = dot(place(src_ref[...], first, step), d_src[...], 1, 0)
        visit = jnp.zeros_like(own)
        for block in range(blocks):
            at = slice(block * negs, (block + 1) * negs)
            one = slice(block, block + 1)
            own += dot(place(neg_src_ref[one, :], first, step), d_neg_src[at, :], 1, 0)
            visit += dot(place(neg_dst_ref[one, :], first, step), d_neg_dst[at, :], 1, 0)
        own_ref[pl.ds(first, step), :] = own
        visit_ref[pl.ds(first, step), :] = visit
        return carry

    lax.fori_loop(0, rows // step, part, 0)


def home_body(
    parts, partner_ref, group_ref, visit_to_ref, asked_ref, returned_ref, visit_ref, *refs
):
    outs, (total, list_ref, count_ref) = refs[: len(parts)], refs[len(parts) :]
    rows, width = visit_ref.shape
    places = asked_ref.shape[2]
    list_peers(partner_ref, group_ref, list_ref, count_ref)
    for part, out_ref in zip(parts, outs):
        count = count_ref[part]
        total[...] = jnp.where(visit_to_ref[0] == part, visit_ref[...], 0.0)

        def pair(t, carry, part=part, count=count):
            one = list_ref[part, 2 * t]
            two = list_ref[part, jnp.minimum(2 * t + 1, count - 1)]
            ask_two = jnp.where(2 * t + 1 < count, asked_ref[pl.ds(two, 1), 0, :], -1)
            ask = jnp.concatenate([asked_ref[pl.ds(one, 1), 0, :], ask_two], axis=1)
            back = jnp.concatenate(
                [
                    returned_ref[pl.ds(one, 1), :places, :].reshape(places, width),
                    returned_ref[pl.ds(two, 1), :places, :].reshape(places, width),
                ],
                axis=0,
            )
            for first in range(0, rows, 512):
                total[first : first + 512] += dot(place(ask, first, 512), back, 1, 0)
            return carry

        lax.fori_loop(0, (count + 1) // 2, pair, 0)
        out_ref[...] = total[...].astype(half)


def operators_body(ids_ref, part_ref, out_ref):
    peers, _, width = part_ref.shape
    blocks = ids_ref.shape[1]
    rows = out_ref.shape[1]
    out_ref[...] = jnp.zeros_like(out_ref)

    def add(peer, carry):
        piece = part_ref[pl.ds(peer, 1)].reshape(blocks * rows, width).astype(full)
        for block in range(blocks):
            at = ids_ref[peer, block]
            out_ref[pl.ds(at, 1)] += piece[block * rows : (block + 1) * rows].reshape(1, rows, width)
        return carry

    lax.fori_loop(0, peers, add, 0)


def laid(column):
    return jnp.broadcast_to(column, (column.shape[0], 128)).T[:1, :]


def relation_body(
    core_ref, mine_ref, other_ref, relation_ref, acc_ref, new_ref, acc_new_ref, acc_turned, acc_found
):
    step, rows, width = relation_ref.shape
    relations = acc_ref.shape[0]
    at = pl.program_id(0)
    own_half = at // (pl.num_programs(0) // 2) == core_ref[0]
    lane = lax.broadcasted_iota(jnp.int32, (rows, 128), 1)

    @pl.when(at == 0)
    def _():
        short = jnp.zeros((128 - relations, rows), full)
        acc_turned[...] = jnp.concatenate([acc_ref[...], short], axis=0).T
        acc_found[...] = jnp.zeros_like(acc_found)

    for k in range(step):
        here = lane == at * step + k
        mine = mine_ref[:, k].astype(full).reshape(rows, width)
        other = other_ref[:, k].astype(full).reshape(rows, width)
        grad = jnp.where(own_half, mine, other)
        square = grad * grad
        parts = sum(square[:, first : first + 128] for first in range(0, width, 128))
        acc = jnp.sum(
            parts * (1.0 / width) + jnp.where(here, acc_turned[...], 0.0), axis=1, keepdims=True
        )
        acc_found[...] = jnp.where(here, acc, acc_found[...])
        new_ref[k] = relation_ref[k] - grad * (step_rate / jnp.sqrt(acc))

    @pl.when(at == pl.num_programs(0) - 1)
    def _():
        acc_new_ref[...] = acc_found[...].T[:relations]


def entity_body(grad_ref, home_ref, sibling_ref, cross_ref, entity_ref, acc_ref, new_ref, acc_new_ref):
    grad = (
        grad_ref[...]
        + home_ref[...].astype(full)
        + sibling_ref[...].astype(full)
        + cross_ref[...].astype(full)
    )
    square = jnp.mean(grad * grad, axis=1, keepdims=True)
    acc = acc_ref[...]
    acc_new_ref[...] = acc + laid(square)
    new_ref[0] = entity_ref[0] - grad * (step_rate / jnp.sqrt(turned(acc)[:, :1] + square))


def relation_update(core, mine, other, relation, relation_acc):
    peers, count, extra, width = mine.shape
    relations, rows = relation_acc.shape
    step = 4 if count % 4 == 0 else 1
    steps = count // step

    def near(flip):
        def at(i, core):
            return (0, jnp.clip(i - steps * (core[0] ^ flip), 0, steps - 1), 0, 0)

        return pl.BlockSpec((peers, step, extra, width), at)

    whole = pl.BlockSpec((relations, rows), lambda i, core: (0, 0))
    block = pl.BlockSpec((step, rows, width), lambda i, core: (i, 0, 0))
    return pl.pallas_call(
        relation_body,
        grid_spec=pltpu.PrefetchScalarGridSpec(
            num_scalar_prefetch=1,
            grid=(2 * steps,),
            in_specs=[near(0), near(1), block, whole],
            out_specs=[block, whole],
            scratch_shapes=[pltpu.VMEM((rows, 128), full), pltpu.VMEM((rows, 128), full)],
        ),
        out_shape=[
            jax.ShapeDtypeStruct(relation.shape, full),
            jax.ShapeDtypeStruct(relation_acc.shape, full),
        ],
        compiler_params=pltpu.CompilerParams(vmem_limit_bytes=60 * MEBI),
    )(core, mine, other, relation, relation_acc)


def entity_update(grad, home, sibling, cross, entity, entity_acc):
    rows, width = grad.shape
    step = 256
    part = pl.BlockSpec((step, width), lambda i: (i, 0))
    block = pl.BlockSpec((1, step, width), lambda i: (0, i, 0))
    line = pl.BlockSpec((1, step), lambda i: (0, i))
    return pl.pallas_call(
        entity_body,
        grid=(rows // step,),
        in_specs=[part] * 4 + [block, line],
        out_specs=[block, line],
        out_shape=[
            jax.ShapeDtypeStruct(entity.shape, full),
            jax.ShapeDtypeStruct(entity_acc.shape, full),
        ],
        compiler_params=pltpu.CompilerParams(vmem_limit_bytes=60 * MEBI),
    )(grad, home, sibling, cross, entity, entity_acc)


def on_device(
    entity,
    entity_acc,
    relation,
    relation_acc,
    partner,
    src_row,
    dst_owner,
    dst_row,
    rel_ids,
    neg_src,
    neg_dst,
    edge_count,
):
    me = lax.axis_index("grp")
    place_id = lax.axis_index("dev")
    peers = lax.axis_size("dev")
    rows, width = entity.shape[1:]
    edges = src_row.shape[1]
    blocks = rel_ids.shape[1]
    negs = neg_src.shape[2]
    relations = relation.shape[0]
    room = 2 * edges // peers
    extra = width // peers
    sds = jax.ShapeDtypeStruct

    def neighbour(x, flip):
        return lax.ppermute(x, "grp", [(g, g ^ flip) for g in range(4)])

    group = me.reshape(1)
    visit_to = (partner[me, place_id] ^ me).reshape(1)
    owners = dst_owner.reshape(1, edges)
    neg_src = neg_src.reshape(blocks, negs)
    neg_dst = neg_dst.reshape(blocks, negs)

    own = entity[0].astype(half)
    cross = neighbour(own, 2)
    sibling = neighbour(own, 1)
    slot, wanted = call(
        slots_body,
        (sds((1, edges), jnp.int32), sds((peers, 2, room), jnp.int32)),
        specs=[SMEM] + [VMEM] * 2,
    )(rel_ids, owners, dst_row)
    asked = lax.all_to_all(wanted, "dev", split_axis=0, concat_axis=0, tiled=True)
    cross, asked = lax.optimization_barrier((cross, asked))
    cross_sibling = neighbour(cross, 1)
    tables = (own, sibling, cross, cross_sibling)

    lists = [pltpu.SMEM((4, peers), jnp.int32), pltpu.SMEM((4,), jnp.int32)]
    found = call(
        answer_body,
        sds((peers, room, width), half),
        lists,
        [SMEM] * 2 + [VMEM] * 5,
    )(partner, group, asked, *tables)
    fetched = lax.all_to_all(found, "dev", split_axis=0, concat_axis=0, tiled=True)

    rest = front(rel_ids, visit_to, src_row, neg_src, neg_dst, relation, tables)
    outgoing, d_src, d_neg_src, d_neg_dst = model(
        rel_ids, edge_count, slot, fetched.reshape(peers * room, width), relation, peers, room, rest
    )
    returned = lax.all_to_all(outgoing, "dev", split_axis=0, concat_axis=0, tiled=True)

    own_grad, visit_grad = call(
        sums_body,
        (sds((rows, width), full), sds((rows, width), full)),
        (),
        [VMEM] * 6,
        cost(2 * 3 * edges * rows * width, 7 * rows * width * 2),
    )(src_row, neg_src, neg_dst, d_src, d_neg_src, d_neg_dst)

    returned, own_grad, visit_grad = lax.optimization_barrier((returned, own_grad, visit_grad))
    rel_part = call(operators_body, sds((relations, extra, width), full), (), [SMEM, VMEM])(
        asked[:, 1, :blocks], returned[:, room:, :]
    )
    core = me & 1
    halves = rel_part.reshape(2, relations // 2, extra, width)
    mine = lax.dynamic_index_in_dim(halves, core, 0, keepdims=False)
    other = lax.dynamic_index_in_dim(halves, 1 - core, 0, keepdims=False)
    chip = mine + neighbour(other, 1)
    pair = (chip + neighbour(chip, 2)).astype(half)
    near = lax.ppermute(pair, "dev", [(d, d ^ 1) for d in range(peers)])
    low = (place_id & 1) == 0
    planes = jnp.stack([jnp.where(low, pair, near), jnp.where(low, near, pair)])
    planes, returned_later = lax.optimization_barrier((planes, returned))
    gathered = lax.all_to_all(
        jnp.broadcast_to(planes[None], (peers // 2,) + planes.shape),
        "dev",
        split_axis=0,
        concat_axis=0,
        axis_index_groups=[list(range(k, peers, 2)) for k in range(2)],
        tiled=True,
    ).reshape((peers,) + pair.shape)

    def home(parts, returned):
        return call(
            functools.partial(home_body, parts),
            tuple(sds((rows, width), half) for _ in parts),
            [pltpu.VMEM((rows, width), full)] + lists,
            [SMEM] * 3 + [VMEM] * 3,
        )(partner, group, visit_to, asked, returned, visit_grad)

    home_cross_sibling, home_cross = home((3, 2), returned)
    chip_cross = (home_cross.astype(full) + neighbour(home_cross_sibling, 1).astype(full)).astype(half)
    from_cross = neighbour(chip_cross, 2)
    home_sibling, home_own = home((1, 0), returned_later)
    from_sibling = neighbour(home_sibling, 1)
    gathered, from_cross, home_own, from_sibling = lax.optimization_barrier(
        (gathered, from_cross, home_own, from_sibling)
    )
    other_half = neighbour(gathered, 1)
    entity_new, acc_new = entity_update(
        own_grad, home_own, from_sibling, from_cross, entity, entity_acc
    )
    relation_new, relation_acc_new = relation_update(
        core.reshape(1), gathered, other_half, relation, relation_acc
    )
    return (entity_new, acc_new, relation_new, relation_acc_new)


def solution(mesh):
    return jax.shard_map(
        on_device,
        mesh=mesh,
        in_specs=(
            P("grp", "dev", None),
            P("grp", "dev"),
            P(),
            P(),
            P(),
            P("grp", "dev"),
            P("grp", "dev", None),
            P("grp", "dev"),
            P("grp", "dev"),
            P("grp", "dev", None),
            P("grp", "dev", None),
            P("grp", "dev"),
        ),
        out_specs=(P("grp", "dev", None), P("grp", "dev"), P(), P()),
        check_vma=False,
    )
```

```python
import functools

import jax
import jax.numpy as jnp
from jax import lax
from jax.experimental import pallas as pl
from jax.experimental.pallas import tpu as pltpu
from jax.sharding import PartitionSpec as P

step_rate = 0.1
MEBI = 1024 * 1024
half = jnp.bfloat16
full = jnp.float32
VMEM = pl.BlockSpec(memory_space=pltpu.VMEM)
SMEM = pl.BlockSpec(memory_space=pltpu.SMEM)
ANY = pl.BlockSpec(memory_space=pl.ANY)


def dot(a, b, ca, cb):
    return lax.dot_general(a, b, (((ca,), (cb,)), ((), ())), preferred_element_type=full)


def turned(row):
    pieces = [
        jnp.broadcast_to(row[:, at : at + 128], (128, 128)).T for at in range(0, row.shape[1], 128)
    ]
    return pieces[0] if len(pieces) == 1 else jnp.concatenate(pieces, axis=0)


def pick(row, width):
    spread = turned(row.astype(full))
    lane = lax.broadcasted_iota(jnp.int32, (1, 128), 1).astype(full)
    pieces = [
        jnp.where(spread == lane + float(at), 1.0, 0.0).astype(half) for at in range(0, width, 128)
    ]
    return jnp.concatenate(pieces, axis=1)


def place(row, first, height):
    line = lax.broadcasted_iota(jnp.int32, (height, 1), 0) + first
    return jnp.where(row == line, 1.0, 0.0).astype(half)


def call(body, shapes, scratch=(), specs=None, cost=None, outs=None, mebi=60, **kw):
    return pl.pallas_call(
        body,
        out_shape=shapes,
        in_specs=specs,
        out_specs=outs or jax.tree.map(lambda _: VMEM, shapes),
        scratch_shapes=list(scratch),
        compiler_params=pltpu.CompilerParams(vmem_limit_bytes=mebi * MEBI),
        cost_estimate=cost,
        **kw,
    )


def cost(flops, moved):
    return pl.CostEstimate(flops=int(flops), bytes_accessed=int(moved), transcendentals=0)


def slots_body(rel_ref, owner_ref, row_ref, slot_ref, wanted_ref):
    peers, _, room = wanted_ref.shape
    edges = owner_ref.shape[1]
    step = 256
    before = lax.broadcasted_iota(jnp.int32, (step, step), 0)
    after = lax.broadcasted_iota(jnp.int32, (step, step), 1)
    upper = jnp.where(before <= after, 1.0, 0.0).astype(half)
    peer = lax.broadcasted_iota(jnp.int32, (peers, step), 0)
    carry = jnp.zeros((peers, 1), full)
    high = jnp.zeros((peers, room), full)
    low = jnp.zeros((peers, room), full)
    for at in range(0, edges, step):
        owner = owner_ref[:, at : at + step]
        hit = jnp.where(peer == owner, 1.0, 0.0)
        count = dot(hit.astype(half), upper, 1, 0) + carry
        carry = count[:, step - 1 :]
        order = (jnp.sum(count * hit, axis=0, keepdims=True) - 1.0).astype(jnp.int32)
        slot_ref[:, at : at + step] = owner * room + order
        spot = place(order, 0, room)
        row = row_ref[:, at : at + step]
        top = lax.shift_right_logical(row, 4)
        high += dot((hit * top.astype(full)).astype(half), spot, 1, 1)
        low += dot((hit * (row - top * 16).astype(full)).astype(half), spot, 1, 1)
    wanted_ref[:, 0, :] = (high * 16.0 + low).astype(jnp.int32)
    lane = lax.broadcasted_iota(jnp.int32, (peers, room), 1)
    ids = jnp.zeros((peers, room), jnp.int32)
    for block in range(rel_ref.shape[1]):
        ids = jnp.where(lane == block, rel_ref[0, block], ids)
    wanted_ref[:, 1, :] = ids


def list_peers(partner_ref, group_ref, list_ref, count_ref):
    peers = partner_ref.shape[1]
    me = group_ref[0]
    for part in range(4):
        count_ref[part] = 0

    def add(peer, carry):
        part = partner_ref[me, peer] ^ me
        at = count_ref[part]
        list_ref[part, at] = peer
        count_ref[part] = at + 1
        return carry

    lax.fori_loop(0, peers, add, 0)


def answer_body(partner_ref, group_ref, asked_ref, *refs):
    tables_in, (found_out, tables, found, sems, out_sem) = refs[:4], refs[4:]
    copies = [
        pltpu.make_async_copy(table, tables.at[part], sems.at[part])
        for part, table in enumerate(tables_in)
    ]
    for copy in copies:
        copy.start()
    peers, _, room = asked_ref.shape
    rows, width = tables.shape[1:]
    me = group_ref[0]
    for copy in copies:
        copy.wait()

    def answer(peer, carry):
        table = tables[partner_ref[me, peer] ^ me]
        got = dot(pick(asked_ref[pl.ds(peer, 1), 0, :], rows), table, 1, 0)
        found[pl.ds(peer, 1)] = got.astype(half).reshape(1, room, width)
        return carry

    lax.fori_loop(0, peers, answer, 0, unroll=4)
    back = pltpu.make_async_copy(found, found_out, out_sem)
    back.start()
    back.wait()


def operators_in(rel_ref, relation_ref, operator, sems):
    copies = [
        pltpu.make_async_copy(relation_ref.at[rel_ref[0, block]], operator.at[block], sems.at[block])
        for block in range(rel_ref.shape[1])
    ]
    for copy in copies:
        copy.start()
    return copies


def front_body(
    rel_ref,
    visit_ref,
    src_ref,
    neg_src_ref,
    neg_dst_ref,
    relation_ref,
    own_table,
    sibling_table,
    cross_table,
    cross_sibling_table,
    src_out,
    neg_src_out,
    lhs_out,
    terms_out,
    pull_out,
    stats_out,
    own,
    visit,
    neg_dst,
    operator,
    op_sems,
    own_sem,
    visit_sem,
):
    rows = own.shape[0]
    blocks, negs = neg_src_ref.shape
    edges = src_ref.shape[1]
    block_len = edges // blocks
    step = 256
    op_copies = operators_in(rel_ref, relation_ref, operator, op_sems)
    own_copy = pltpu.make_async_copy(own_table, own, own_sem)
    own_copy.start()
    for part, table in enumerate((own_table, sibling_table, cross_table, cross_sibling_table)):

        @pl.when(visit_ref[0] == part)
        def _(table=table):
            pltpu.make_async_copy(table, visit, visit_sem).start()

    own_copy.wait()
    pltpu.make_async_copy(own_table, visit, visit_sem).wait()
    for copy in op_copies:
        copy.wait()
    for block in range(blocks):
        for at in range(0, negs, step):
            to = block * negs + at
            neg_src_out[to : to + step] = dot(
                pick(neg_src_ref[block : block + 1, at : at + step], rows), own[...], 1, 0
            ).astype(half)
            neg_dst[at : at + step] = dot(
                pick(neg_dst_ref[block : block + 1, at : at + step], rows), visit[...], 1, 0
            ).astype(half)

        def chunk(t, carry, block=block):
            at = pl.multiple_of(block * block_len + t * step, step)
            here = pl.ds(at, step)
            op = operator[block].astype(half)
            src = dot(pick(src_ref[:, here], rows), own[...], 1, 0).astype(half)
            lhs = dot(src, op, 1, 0).astype(half)
            scores = dot(lhs, neg_dst[...], 1, 1)
            highest = jnp.max(scores, axis=1, keepdims=True)
            terms = jnp.exp(scores - highest)
            lane = lax.broadcasted_iota(jnp.int32, (step, 128), 1)
            stats_out[here, :] = jnp.where(lane < 64, highest, jnp.sum(terms, axis=1, keepdims=True))
            terms = terms.astype(half)
            src_out[here, :] = src
            lhs_out[here, :] = lhs
            terms_out[here, :] = terms
            pull_out[here, :] = dot(terms, neg_dst[...], 1, 0)
            return carry

        lax.fori_loop(0, block_len // step, chunk, 0, unroll=2)


def model_body(
    rel_ref,
    count_ref,
    slot_ref,
    fetched_ref,
    relation_ref,
    src_in,
    neg_src_in,
    lhs_in,
    terms_in,
    pull_in,
    stats_in,
    outgoing_ref,
    d_src_out,
    d_neg_src_out,
    d_neg_dst_out,
    src_ref,
    neg_src_ref,
    lhs_ref,
    terms_ref,
    pull_ref,
    stats_ref,
    d_src_ref,
    d_neg_src_ref,
    d_neg_dst_ref,
    dst_ref,
    d_dst,
    operator,
    neg_dst_sum,
    neg_src_sum,
    op_sum,
    op_turned_sum,
    op_sems,
    in_sems,
    out_sems,
):
    slots, width = fetched_ref.shape
    edges = slot_ref.shape[1]
    blocks = rel_ref.shape[1]
    block_len = edges // blocks
    negs = neg_src_ref.shape[0] // blocks
    peers, room, _ = outgoing_ref.shape
    extra = width // peers
    places = slots // peers
    step = 256
    copies = operators_in(rel_ref, relation_ref, operator, op_sems)
    pairs = (
        (src_in, src_ref),
        (neg_src_in, neg_src_ref),
        (lhs_in, lhs_ref),
        (pull_in, pull_ref),
        (stats_in, stats_ref),
        (terms_in, terms_ref),
    )
    for i, (there, here) in enumerate(pairs):
        copies.append(pltpu.make_async_copy(there, here, in_sems.at[i]))
        copies[-1].start()

    def fetch(t, carry):
        here = pl.ds(pl.multiple_of(t * step, step), step)
        dst_ref[here, :] = dot(pick(slot_ref[:, here], slots), fetched_ref[...], 1, 0).astype(half)
        return carry

    lax.fori_loop(0, edges // step, fetch, 0, unroll=4)
    for copy in copies:
        copy.wait()
    for block in range(blocks):
        neg_dst_sum[...] = jnp.zeros_like(neg_dst_sum)
        neg_src_sum[...] = jnp.zeros_like(neg_src_sum)
        op_sum[...] = jnp.zeros_like(op_sum)
        op_turned_sum[...] = jnp.zeros_like(op_turned_sum)

        def chunk(t, carry, block=block):
            at = pl.multiple_of(block * block_len + t * step, step)
            here = pl.ds(at, step)
            op = operator[block].astype(half)
            dst = dst_ref[here, :]
            src = src_ref[here, :]
            lhs = lhs_ref[here, :]
            neg_src = neg_src_ref[block * negs : (block + 1) * negs, :]
            line = lax.broadcasted_iota(jnp.int32, (step, 1), 0) + at
            live = jnp.where(line < count_ref[0, 0], 1.0, 0.0)
            rhs = dot(dst, op, 1, 1).astype(half)
            positive = jnp.sum(lhs.astype(full) * dst.astype(full), axis=1, keepdims=True)

            scores = dot(rhs, neg_src, 1, 1)
            highest = jnp.maximum(jnp.max(scores, axis=1, keepdims=True), positive)
            terms = jnp.exp(scores - highest)
            own = jnp.exp(positive - highest)
            scale = live / (own + jnp.sum(terms, axis=1, keepdims=True))
            src_terms = (terms * scale).astype(half)
            d_positive = own * scale - live

            top = stats_ref[here, :]
            top, total = top[:, :1], top[:, 64:65]
            highest = jnp.maximum(top, positive)
            lower = jnp.exp(top - highest)
            own = jnp.exp(positive - highest)
            scale = live / (own + total * lower)
            d_positive += own * scale - live
            scale = lower * scale

            d_lhs = (pull_ref[here, :] * scale).astype(half)
            d_lhs = d_lhs + (d_positive * dst.astype(full)).astype(half)
            d_rhs = dot(src_terms, neg_src, 1, 0).astype(half)
            scaled = (lhs.astype(full) * scale).astype(half)
            neg_dst_sum[...] += dot(scaled, terms_ref[here, :], 0, 0)
            neg_src_sum[...] += dot(rhs, src_terms, 0, 0)
            d_src_ref[here, :] = dot(d_lhs, op, 1, 1).astype(half)
            op_sum[...] += dot(src, d_lhs, 0, 0)
            op_turned_sum[...] += dot(d_rhs, dst, 0, 0)
            d_dst[here, :] = dot(d_rhs, op, 1, 0).astype(half) + (
                d_positive * lhs.astype(full)
            ).astype(half)
            return carry

        lax.fori_loop(0, block_len // step, chunk, 0, unroll=4)
        d_neg_dst_ref[block * negs : (block + 1) * negs, :] = neg_dst_sum[...].T.astype(half)
        d_neg_src_ref[block * negs : (block + 1) * negs, :] = neg_src_sum[...].T.astype(half)
        d_op = op_sum[...].astype(half) + op_turned_sum[...].astype(half)
        outgoing_ref[:, places + block * extra : places + (block + 1) * extra, :] = d_op.reshape(
            peers, extra, width
        )
    backs = []
    for i, (here, there) in enumerate(
        ((d_src_ref, d_src_out), (d_neg_src_ref, d_neg_src_out), (d_neg_dst_ref, d_neg_dst_out))
    ):
        backs.append(pltpu.make_async_copy(here, there, out_sems.at[i]))
        backs[-1].start()

    def send(t, carry):
        spot = place(slot_ref[...], t * 2 * places, 2 * places)
        out = dot(spot, d_dst[...], 1, 0).astype(half)
        outgoing_ref[pl.ds(2 * t, 2), :places, :] = out.reshape(2, places, width)
        return carry

    lax.fori_loop(0, peers // 2, send, 0, unroll=4)
    for copy in backs:
        copy.wait()


def front(rel_ids, visit_to, src_row, neg_src, neg_dst, relation, tables):
    rows, width = tables[0].shape
    edges = src_row.shape[1]
    blocks, negs = neg_src.shape
    sds = jax.ShapeDtypeStruct
    return call(
        front_body,
        (
            sds((edges, width), half),
            sds((blocks * negs, width), half),
            sds((edges, width), half),
            sds((edges, negs), half),
            sds((edges, width), full),
            sds((edges, 128), full),
        ),
        [
            pltpu.VMEM((rows, width), half),
            pltpu.VMEM((rows, width), half),
            pltpu.VMEM((negs, width), half),
            pltpu.VMEM((blocks, width, width), full),
            pltpu.SemaphoreType.DMA((blocks,)),
            pltpu.SemaphoreType.DMA,
            pltpu.SemaphoreType.DMA,
        ],
        [SMEM] * 2 + [VMEM] * 3 + [ANY] * 5,
        cost(2 * edges * width * (3 * rows + 2 * negs), 12 * MEBI),
    )(rel_ids, visit_to, src_row, neg_src, neg_dst, relation, *tables)


def model(rel_ids, edge_count, slot, fetched, relation, peers, room, rest):
    slots, width = fetched.shape
    edges = slot.shape[1]
    blocks = rel_ids.shape[1]
    negs = rest[1].shape[0] // blocks
    sds = jax.ShapeDtypeStruct
    return call(
        model_body,
        (
            sds((peers, room + blocks * (width // peers), width), half),
            sds((edges, width), half),
            sds((blocks * negs, width), half),
            sds((blocks * negs, width), half),
        ),
        [pltpu.VMEM(x.shape, x.dtype) for x in rest]
        + [
            pltpu.VMEM((edges, width), half),
            pltpu.VMEM((blocks * negs, width), half),
            pltpu.VMEM((blocks * negs, width), half),
            pltpu.VMEM((edges, width), half),
            pltpu.VMEM((edges, width), half),
            pltpu.VMEM((blocks, width, width), full),
            pltpu.VMEM((width, negs), full),
            pltpu.VMEM((width, negs), full),
            pltpu.VMEM((width, width), full),
            pltpu.VMEM((width, width), full),
            pltpu.SemaphoreType.DMA((blocks,)),
            pltpu.SemaphoreType.DMA((6,)),
            pltpu.SemaphoreType.DMA((3,)),
        ],
        [SMEM] * 2 + [VMEM] * 2 + [ANY] * 7,
        outs=[VMEM] + [ANY] * 3,
    )(rel_ids, edge_count, slot, fetched, relation, *rest)


def sums_body(src_ref, neg_src_ref, neg_dst_ref, d_src, d_neg_src, d_neg_dst, own_ref, visit_ref):
    rows = own_ref.shape[0]
    blocks, negs = neg_src_ref.shape
    step = 256

    def part(t, carry):
        first = pl.multiple_of(t * step, step)
        own = dot(place(src_ref[...], first, step), d_src[...], 1, 0)
        visit = jnp.zeros_like(own)
        for block in range(blocks):
            at = slice(block * negs, (block + 1) * negs)
            one = slice(block, block + 1)
            own += dot(place(neg_src_ref[one, :], first, step), d_neg_src[at, :], 1, 0)
            visit += dot(place(neg_dst_ref[one, :], first, step), d_neg_dst[at, :], 1, 0)
        own_ref[pl.ds(first, step), :] = own
        visit_ref[pl.ds(first, step), :] = visit
        return carry

    lax.fori_loop(0, rows // step, part, 0)


def home_body(
    parts, partner_ref, group_ref, visit_to_ref, asked_ref, returned_ref, visit_ref, *refs
):
    outs, (total, list_ref, count_ref) = refs[: len(parts)], refs[len(parts) :]
    rows, width = visit_ref.shape
    places = asked_ref.shape[2]
    together = 4
    list_peers(partner_ref, group_ref, list_ref, count_ref)
    for part, out_ref in zip(parts, outs):
        count = count_ref[part]
        total[...] = jnp.where(visit_to_ref[0] == part, visit_ref[...], 0.0)

        def add(t, carry, part=part, count=count):
            asks, backs = [], []
            for k in range(together):
                peer = list_ref[part, jnp.minimum(together * t + k, count - 1)]
                ask = asked_ref[pl.ds(peer, 1), 0, :]
                asks.append(jnp.where(together * t + k < count, ask, -1))
                backs.append(returned_ref[pl.ds(peer, 1), :places, :].reshape(places, width))
            ask = jnp.concatenate(asks, axis=1)
            back = jnp.concatenate(backs, axis=0)
            for first in range(0, rows, 512):
                total[first : first + 512] += dot(place(ask, first, 512), back, 1, 0)
            return carry

        lax.fori_loop(0, (count + together - 1) // together, add, 0)
        out_ref[...] = total[...].astype(half)


def operators_body(ids_ref, part_ref, out_ref):
    peers, _, width = part_ref.shape
    blocks = ids_ref.shape[1]
    rows = out_ref.shape[1]
    out_ref[...] = jnp.zeros_like(out_ref)

    def add(peer, carry):
        piece = part_ref[pl.ds(peer, 1)].reshape(blocks * rows, width).astype(full)
        for block in range(blocks):
            at = ids_ref[peer, block]
            out_ref[pl.ds(at, 1)] += piece[block * rows : (block + 1) * rows].reshape(1, rows, width)
        return carry

    lax.fori_loop(0, peers, add, 0)


def laid(column):
    return jnp.broadcast_to(column, (column.shape[0], 128)).T[:1, :]


def relation_body(part_ref, grad_ref, relation_ref, acc_ref, *refs):
    (new_ref, acc_new_ref, acc_turned, acc_found), before = refs[-4:], refs[:-4]
    step, rows, width = relation_ref.shape
    relations = acc_ref.shape[0]
    at = pl.program_id(0)
    first = part_ref[0] * (relations // 2) + at * step
    lane = lax.broadcasted_iota(jnp.int32, (rows, 128), 1)

    @pl.when(at == 0)
    def _():
        short = jnp.zeros((128 - relations, rows), full)
        acc_turned[...] = jnp.concatenate([acc_ref[...], short], axis=0).T
        if before:
            acc_found[...] = jnp.concatenate([before[1][...], short], axis=0).T
        else:
            acc_found[...] = jnp.zeros_like(acc_found)

    for k in range(step):
        here = lane == first + k
        grad = grad_ref[:, k].astype(full).reshape(rows, width)
        square = grad * grad
        parts = sum(square[:, at : at + 128] for at in range(0, width, 128))
        acc = jnp.sum(
            parts * (1.0 / width) + jnp.where(here, acc_turned[...], 0.0), axis=1, keepdims=True
        )
        acc_found[...] = jnp.where(here, acc, acc_found[...])
        new_ref[k] = relation_ref[k] - grad * (step_rate / jnp.sqrt(acc))

    @pl.when(at == pl.num_programs(0) - 1)
    def _():
        acc_new_ref[...] = acc_found[...].T[:relations]


def entity_body(grad_ref, home_ref, sibling_ref, cross_ref, entity_ref, acc_ref, new_ref, acc_new_ref):
    grad = (
        grad_ref[...]
        + home_ref[...].astype(full)
        + sibling_ref[...].astype(full)
        + cross_ref[...].astype(full)
    )
    square = jnp.mean(grad * grad, axis=1, keepdims=True)
    acc = acc_ref[...]
    acc_new_ref[...] = acc + laid(square)
    new_ref[0] = entity_ref[0] - grad * (step_rate / jnp.sqrt(turned(acc)[:, :1] + square))


def relation_update(part, grad, relation, relation_acc, before=()):
    peers, count, extra, width = grad.shape
    relations, rows = relation_acc.shape
    step = 10 if count % 10 == 0 else 1
    steps = count // step
    whole = pl.BlockSpec((relations, rows), lambda i, part: (0, 0))
    block = pl.BlockSpec((step, rows, width), lambda i, part: (part[0] * steps + i, 0, 0))
    return pl.pallas_call(
        relation_body,
        grid_spec=pltpu.PrefetchScalarGridSpec(
            num_scalar_prefetch=1,
            grid=(steps,),
            in_specs=[
                pl.BlockSpec((peers, step, extra, width), lambda i, part: (0, i, 0, 0)),
                block,
                whole,
            ]
            + [ANY, whole][: len(before)],
            out_specs=[block, whole],
            scratch_shapes=[pltpu.VMEM((rows, 128), full), pltpu.VMEM((rows, 128), full)],
        ),
        out_shape=[
            jax.ShapeDtypeStruct(relation.shape, full),
            jax.ShapeDtypeStruct(relation_acc.shape, full),
        ],
        input_output_aliases={4: 0} if before else {},
        compiler_params=pltpu.CompilerParams(vmem_limit_bytes=60 * MEBI),
        cost_estimate=cost(0, 24 * MEBI),
    )(part, grad, relation, relation_acc, *before)


def entity_update(grad, home, sibling, cross, entity, entity_acc):
    rows, width = grad.shape
    step = 256
    part = pl.BlockSpec((step, width), lambda i: (i, 0))
    block = pl.BlockSpec((1, step, width), lambda i: (0, i, 0))
    line = pl.BlockSpec((1, step), lambda i: (0, i))
    return pl.pallas_call(
        entity_body,
        grid=(rows // step,),
        in_specs=[part] * 4 + [block, line],
        out_specs=[block, line],
        out_shape=[
            jax.ShapeDtypeStruct(entity.shape, full),
            jax.ShapeDtypeStruct(entity_acc.shape, full),
        ],
        compiler_params=pltpu.CompilerParams(vmem_limit_bytes=60 * MEBI),
        cost_estimate=cost(0, 24 * MEBI),
    )(grad, home, sibling, cross, entity, entity_acc)


def on_device(
    entity,
    entity_acc,
    relation,
    relation_acc,
    partner,
    src_row,
    dst_owner,
    dst_row,
    rel_ids,
    neg_src,
    neg_dst,
    edge_count,
):
    me = lax.axis_index("grp")
    place_id = lax.axis_index("dev")
    peers = lax.axis_size("dev")
    rows, width = entity.shape[1:]
    edges = src_row.shape[1]
    blocks = rel_ids.shape[1]
    negs = neg_src.shape[2]
    relations = relation.shape[0]
    room = 2 * edges // peers
    extra = width // peers
    sds = jax.ShapeDtypeStruct

    def neighbour(x, flip):
        return lax.ppermute(x, "grp", [(g, g ^ flip) for g in range(4)])

    group = me.reshape(1)
    visit_to = (partner[me, place_id] ^ me).reshape(1)
    owners = dst_owner.reshape(1, edges)
    neg_src = neg_src.reshape(blocks, negs)
    neg_dst = neg_dst.reshape(blocks, negs)

    own = entity[0].astype(half)
    cross = neighbour(own, 2)
    sibling = neighbour(own, 1)
    slot, wanted = call(
        slots_body,
        (sds((1, edges), jnp.int32), sds((peers, 2, room), jnp.int32)),
        specs=[SMEM] + [VMEM] * 2,
    )(rel_ids, owners, dst_row)
    asked = lax.all_to_all(wanted, "dev", split_axis=0, concat_axis=0, tiled=True)
    cross, asked = lax.optimization_barrier((cross, asked))
    cross_sibling = neighbour(cross, 1)
    tables = (own, sibling, cross, cross_sibling)

    lists = [pltpu.SMEM((4, peers), jnp.int32), pltpu.SMEM((4,), jnp.int32)]
    found = call(
        answer_body,
        sds((peers, room, width), half),
        [
            pltpu.VMEM((4, rows, width), half),
            pltpu.VMEM((peers, room, width), half),
            pltpu.SemaphoreType.DMA((4,)),
            pltpu.SemaphoreType.DMA,
        ],
        [SMEM] * 2 + [VMEM] + [ANY] * 4,
        outs=ANY,
    )(partner, group, asked, *tables)
    fetched = lax.all_to_all(found, "dev", split_axis=0, concat_axis=0, tiled=True)

    rest = front(rel_ids, visit_to, src_row, neg_src, neg_dst, relation, tables)
    outgoing, d_src, d_neg_src, d_neg_dst = model(
        rel_ids, edge_count, slot, fetched.reshape(peers * room, width), relation, peers, room, rest
    )
    returned = lax.all_to_all(outgoing, "dev", split_axis=0, concat_axis=0, tiled=True)

    own_grad, visit_grad = call(
        sums_body,
        (sds((rows, width), full), sds((rows, width), full)),
        (),
        [VMEM] * 6,
        cost(2 * 3 * edges * rows * width, 7 * rows * width * 2),
    )(src_row, neg_src, neg_dst, d_src, d_neg_src, d_neg_dst)

    returned, own_grad, visit_grad = lax.optimization_barrier((returned, own_grad, visit_grad))

    def home(parts, returned):
        return call(
            functools.partial(home_body, parts),
            tuple(sds((rows, width), half) for _ in parts),
            [pltpu.VMEM((rows, width), full)] + lists,
            [SMEM] * 3 + [VMEM] * 3,
            cost(0, 24 * MEBI),
        )(partner, group, visit_to, asked, returned, visit_grad)

    home_cross_sibling, home_cross = home((3, 2), returned)
    returned, home_cross_sibling = lax.optimization_barrier((returned, home_cross_sibling))
    chip_cross = (home_cross.astype(full) + neighbour(home_cross_sibling, 1).astype(full)).astype(half)

    rel_part = call(operators_body, sds((relations, extra, width), full), (), [SMEM, VMEM])(
        asked[:, 1, :blocks], returned[:, room:, :]
    )
    core = me & 1
    halves = rel_part.reshape(2, relations // 2, extra, width)
    mine = lax.dynamic_index_in_dim(halves, core, 0, keepdims=False)
    other = lax.dynamic_index_in_dim(halves, 1 - core, 0, keepdims=False)
    chip = mine + neighbour(other, 1)
    pair = (chip + neighbour(chip, 2)).astype(half)
    near = lax.ppermute(pair, "dev", [(d, d ^ 1) for d in range(peers)])
    low = (place_id & 1) == 0
    planes = jnp.stack([jnp.where(low, pair, near), jnp.where(low, near, pair)])
    planes, chip_cross, returned = lax.optimization_barrier((planes, chip_cross, returned))
    from_cross = neighbour(chip_cross, 2)
    gathered = lax.all_to_all(
        jnp.broadcast_to(planes[None], (peers // 2,) + planes.shape),
        "dev",
        split_axis=0,
        concat_axis=0,
        axis_index_groups=[list(range(k, peers, 2)) for k in range(2)],
        tiled=True,
    ).reshape((peers,) + pair.shape)

    home_sibling, home_own = home((1, 0), returned)
    from_sibling = neighbour(home_sibling, 1)
    entity_new, acc_new = entity_update(
        own_grad, home_own, from_sibling, from_cross, entity, entity_acc
    )
    gathered, entity_new, acc_new = lax.optimization_barrier((gathered, entity_new, acc_new))
    other_half = neighbour(gathered, 1)
    before = relation_update(core.reshape(1), gathered, relation, relation_acc)
    relation_new, relation_acc_new = relation_update(
        (1 - core).reshape(1), other_half, relation, relation_acc, before
    )
    return (entity_new, acc_new, relation_new, relation_acc_new)


def solution(mesh):
    return jax.shard_map(
        on_device,
        mesh=mesh,
        in_specs=(
            P("grp", "dev", None),
            P("grp", "dev"),
            P(),
            P(),
            P(),
            P("grp", "dev"),
            P("grp", "dev", None),
            P("grp", "dev"),
            P("grp", "dev"),
            P("grp", "dev", None),
            P("grp", "dev", None),
            P("grp", "dev"),
        ),
        out_specs=(P("grp", "dev", None), P("grp", "dev"), P(), P()),
        check_vma=False,
    )
```

```python
import functools

import jax
import jax.numpy as jnp
from jax import lax
from jax.experimental import pallas as pl
from jax.experimental.pallas import tpu as pltpu
from jax.sharding import PartitionSpec as P

step_rate = 0.1
MEBI = 1024 * 1024
half = jnp.bfloat16
full = jnp.float32
VMEM = pl.BlockSpec(memory_space=pltpu.VMEM)
SMEM = pl.BlockSpec(memory_space=pltpu.SMEM)
HBM = pl.BlockSpec(memory_space=pltpu.HBM)


def dot(a, b, ca, cb):
    return lax.dot_general(a, b, (((ca,), (cb,)), ((), ())), preferred_element_type=full)


def turned(row):
    pieces = [
        jnp.broadcast_to(row[:, at : at + 128], (128, 128)).T for at in range(0, row.shape[1], 128)
    ]
    return pieces[0] if len(pieces) == 1 else jnp.concatenate(pieces, axis=0)


def pick(row, width):
    spread = turned(row.astype(full))
    lane = lax.broadcasted_iota(jnp.int32, (1, 128), 1).astype(full)
    pieces = [
        jnp.where(spread == lane + float(at), 1.0, 0.0).astype(half) for at in range(0, width, 128)
    ]
    return jnp.concatenate(pieces, axis=1)


def place(row, first, height):
    line = lax.broadcasted_iota(jnp.int32, (height, 1), 0) + first
    return jnp.where(row == line, 1.0, 0.0).astype(half)


def call(body, shapes, scratch=(), specs=None, cost=None, outs=None, mebi=40, **kw):
    return pl.pallas_call(
        body,
        out_shape=shapes,
        in_specs=specs,
        out_specs=outs or jax.tree.map(lambda _: VMEM, shapes),
        scratch_shapes=list(scratch),
        compiler_params=pltpu.CompilerParams(vmem_limit_bytes=mebi * MEBI),
        cost_estimate=cost,
        **kw,
    )


def cost(flops, moved):
    return pl.CostEstimate(flops=int(flops), bytes_accessed=int(moved), transcendentals=0)


def slots_body(rel_ref, owner_ref, row_ref, slot_ref, wanted_ref):
    peers, _, room = wanted_ref.shape
    edges = owner_ref.shape[1]
    step = 256
    before = lax.broadcasted_iota(jnp.int32, (step, step), 0)
    after = lax.broadcasted_iota(jnp.int32, (step, step), 1)
    upper = jnp.where(before <= after, 1.0, 0.0).astype(half)
    peer = lax.broadcasted_iota(jnp.int32, (peers, step), 0)
    carry = jnp.zeros((peers, 1), full)
    high = jnp.zeros((peers, room), full)
    low = jnp.zeros((peers, room), full)
    for at in range(0, edges, step):
        owner = owner_ref[:, at : at + step]
        hit = jnp.where(peer == owner, 1.0, 0.0)
        count = dot(hit.astype(half), upper, 1, 0) + carry
        carry = count[:, step - 1 :]
        order = (jnp.sum(count * hit, axis=0, keepdims=True) - 1.0).astype(jnp.int32)
        slot_ref[:, at : at + step] = owner * room + order
        spot = place(order, 0, room)
        row = row_ref[:, at : at + step]
        top = lax.shift_right_logical(row, 4)
        high += dot((hit * top.astype(full)).astype(half), spot, 1, 1)
        low += dot((hit * (row - top * 16).astype(full)).astype(half), spot, 1, 1)
    wanted_ref[:, 0, :] = (high * 16.0 + low).astype(jnp.int32)
    lane = lax.broadcasted_iota(jnp.int32, (peers, room), 1)
    ids = jnp.zeros((peers, room), jnp.int32)
    for block in range(rel_ref.shape[1]):
        ids = jnp.where(lane == block, rel_ref[0, block], ids)
    wanted_ref[:, 1, :] = ids


def list_peers(partner_ref, group_ref, list_ref, count_ref):
    peers = partner_ref.shape[1]
    me = group_ref[0]
    for part in range(4):
        count_ref[part] = 0

    def add(peer, carry):
        part = partner_ref[me, peer] ^ me
        at = count_ref[part]
        list_ref[part, at] = peer
        count_ref[part] = at + 1
        return carry

    lax.fori_loop(0, peers, add, 0)


def answer_body(partner_ref, group_ref, asked_ref, *refs):
    tables_in, (found_out, tables, found, sems, out_sem) = refs[:4], refs[4:]
    copies = [
        pltpu.make_async_copy(table, tables.at[part], sems.at[part])
        for part, table in enumerate(tables_in)
    ]
    for copy in copies:
        copy.start()
    peers, _, room = asked_ref.shape
    rows, width = tables.shape[1:]
    me = group_ref[0]
    for copy in copies:
        copy.wait()

    def answer(peer, carry):
        table = tables[partner_ref[me, peer] ^ me]
        got = dot(pick(asked_ref[pl.ds(peer, 1), 0, :], rows), table, 1, 0)
        found[pl.ds(peer, 1)] = got.astype(half).reshape(1, room, width)
        return carry

    lax.fori_loop(0, peers, answer, 0, unroll=4)
    back = pltpu.make_async_copy(found, found_out, out_sem)
    back.start()
    back.wait()


def operators_in(rel_ref, relation_ref, operator, sems):
    copies = [
        pltpu.make_async_copy(relation_ref.at[rel_ref[0, block]], operator.at[block], sems.at[block])
        for block in range(rel_ref.shape[1])
    ]
    for copy in copies:
        copy.start()
    return copies


def front_body(
    rel_ref,
    visit_ref,
    src_ref,
    neg_src_ref,
    neg_dst_ref,
    relation_ref,
    own_table,
    sibling_table,
    cross_table,
    cross_sibling_table,
    src_out,
    neg_src_out,
    lhs_out,
    terms_out,
    pull_out,
    stats_out,
    own,
    visit,
    neg_dst,
    operator,
    op_sems,
    own_sem,
    visit_sem,
):
    rows = own.shape[0]
    blocks, negs = neg_src_ref.shape
    edges = src_ref.shape[1]
    block_len = edges // blocks
    step = 256
    op_copies = operators_in(rel_ref, relation_ref, operator, op_sems)
    own_copy = pltpu.make_async_copy(own_table, own, own_sem)
    own_copy.start()
    for part, table in enumerate((own_table, sibling_table, cross_table, cross_sibling_table)):

        @pl.when(visit_ref[0] == part)
        def _(table=table):
            pltpu.make_async_copy(table, visit, visit_sem).start()

    own_copy.wait()
    pltpu.make_async_copy(own_table, visit, visit_sem).wait()
    for copy in op_copies:
        copy.wait()
    for block in range(blocks):
        for at in range(0, negs, step):
            to = block * negs + at
            neg_src_out[to : to + step] = dot(
                pick(neg_src_ref[block : block + 1, at : at + step], rows), own[...], 1, 0
            ).astype(half)
            neg_dst[at : at + step] = dot(
                pick(neg_dst_ref[block : block + 1, at : at + step], rows), visit[...], 1, 0
            ).astype(half)

        def chunk(t, carry, block=block):
            at = pl.multiple_of(block * block_len + t * step, step)
            here = pl.ds(at, step)
            op = operator[block].astype(half)
            src = dot(pick(src_ref[:, here], rows), own[...], 1, 0).astype(half)
            lhs = dot(src, op, 1, 0).astype(half)
            scores = dot(lhs, neg_dst[...], 1, 1)
            highest = jnp.max(scores, axis=1, keepdims=True)
            terms = jnp.exp(scores - highest)
            lane = lax.broadcasted_iota(jnp.int32, (step, 128), 1)
            stats_out[here, :] = jnp.where(lane < 64, highest, jnp.sum(terms, axis=1, keepdims=True))
            terms = terms.astype(half)
            src_out[here, :] = src
            lhs_out[here, :] = lhs
            terms_out[here, :] = terms
            pull_out[here, :] = dot(terms, neg_dst[...], 1, 0)
            return carry

        lax.fori_loop(0, block_len // step, chunk, 0, unroll=2)


def model_body(
    rel_ref,
    count_ref,
    slot_ref,
    fetched_ref,
    relation_ref,
    src_in,
    neg_src_in,
    lhs_in,
    terms_in,
    pull_in,
    stats_in,
    outgoing_ref,
    d_src_out,
    d_neg_src_out,
    d_neg_dst_out,
    src_ref,
    neg_src_ref,
    lhs_ref,
    terms_ref,
    pull_ref,
    stats_ref,
    d_src_ref,
    d_neg_src_ref,
    d_neg_dst_ref,
    dst_ref,
    d_dst,
    operator,
    neg_dst_sum,
    neg_src_sum,
    op_sum,
    op_turned_sum,
    op_sems,
    in_sems,
    out_sems,
):
    slots, width = fetched_ref.shape
    edges = slot_ref.shape[1]
    blocks = rel_ref.shape[1]
    block_len = edges // blocks
    negs = neg_src_ref.shape[0] // blocks
    peers, room, _ = outgoing_ref.shape
    extra = width // peers
    places = slots // peers
    step = 256
    copies = operators_in(rel_ref, relation_ref, operator, op_sems)
    pairs = (
        (src_in, src_ref),
        (neg_src_in, neg_src_ref),
        (lhs_in, lhs_ref),
        (pull_in, pull_ref),
        (stats_in, stats_ref),
        (terms_in, terms_ref),
    )
    for i, (there, here) in enumerate(pairs):
        copies.append(pltpu.make_async_copy(there, here, in_sems.at[i]))
        copies[-1].start()

    def fetch(t, carry):
        here = pl.ds(pl.multiple_of(t * step, step), step)
        dst_ref[here, :] = dot(pick(slot_ref[:, here], slots), fetched_ref[...], 1, 0).astype(half)
        return carry

    lax.fori_loop(0, edges // step, fetch, 0, unroll=4)
    for copy in copies:
        copy.wait()
    for block in range(blocks):
        neg_dst_sum[...] = jnp.zeros_like(neg_dst_sum)
        neg_src_sum[...] = jnp.zeros_like(neg_src_sum)
        op_sum[...] = jnp.zeros_like(op_sum)
        op_turned_sum[...] = jnp.zeros_like(op_turned_sum)

        def chunk(t, carry, block=block):
            at = pl.multiple_of(block * block_len + t * step, step)
            here = pl.ds(at, step)
            op = operator[block].astype(half)
            dst = dst_ref[here, :]
            src = src_ref[here, :]
            lhs = lhs_ref[here, :]
            neg_src = neg_src_ref[block * negs : (block + 1) * negs, :]
            line = lax.broadcasted_iota(jnp.int32, (step, 1), 0) + at
            live = jnp.where(line < count_ref[0, 0], 1.0, 0.0)
            rhs = dot(dst, op, 1, 1).astype(half)
            positive = jnp.sum(lhs.astype(full) * dst.astype(full), axis=1, keepdims=True)

            scores = dot(rhs, neg_src, 1, 1)
            highest = jnp.maximum(jnp.max(scores, axis=1, keepdims=True), positive)
            terms = jnp.exp(scores - highest)
            own = jnp.exp(positive - highest)
            scale = live / (own + jnp.sum(terms, axis=1, keepdims=True))
            src_terms = (terms * scale).astype(half)
            d_positive = own * scale - live

            top = stats_ref[here, :]
            top, total = top[:, :1], top[:, 64:65]
            highest = jnp.maximum(top, positive)
            lower = jnp.exp(top - highest)
            own = jnp.exp(positive - highest)
            scale = live / (own + total * lower)
            d_positive += own * scale - live
            scale = lower * scale

            d_lhs = (pull_ref[here, :] * scale).astype(half)
            d_lhs = d_lhs + (d_positive * dst.astype(full)).astype(half)
            d_rhs = dot(src_terms, neg_src, 1, 0).astype(half)
            scaled = (lhs.astype(full) * scale).astype(half)
            neg_dst_sum[...] += dot(scaled, terms_ref[here, :], 0, 0)
            neg_src_sum[...] += dot(rhs, src_terms, 0, 0)
            d_src_ref[here, :] = dot(d_lhs, op, 1, 1).astype(half)
            op_sum[...] += dot(src, d_lhs, 0, 0)
            op_turned_sum[...] += dot(d_rhs, dst, 0, 0)
            d_dst[here, :] = dot(d_rhs, op, 1, 0).astype(half) + (
                d_positive * lhs.astype(full)
            ).astype(half)
            return carry

        lax.fori_loop(0, block_len // step, chunk, 0, unroll=4)
        d_neg_dst_ref[block * negs : (block + 1) * negs, :] = neg_dst_sum[...].T.astype(half)
        d_neg_src_ref[block * negs : (block + 1) * negs, :] = neg_src_sum[...].T.astype(half)
        d_op = op_sum[...].astype(half) + op_turned_sum[...].astype(half)
        outgoing_ref[:, places + block * extra : places + (block + 1) * extra, :] = d_op.reshape(
            peers, extra, width
        )
    backs = []
    for i, (here, there) in enumerate(
        ((d_src_ref, d_src_out), (d_neg_src_ref, d_neg_src_out), (d_neg_dst_ref, d_neg_dst_out))
    ):
        backs.append(pltpu.make_async_copy(here, there, out_sems.at[i]))
        backs[-1].start()

    def send(t, carry):
        spot = place(slot_ref[...], t * 2 * places, 2 * places)
        out = dot(spot, d_dst[...], 1, 0).astype(half)
        outgoing_ref[pl.ds(2 * t, 2), :places, :] = out.reshape(2, places, width)
        return carry

    lax.fori_loop(0, peers // 2, send, 0, unroll=4)
    for copy in backs:
        copy.wait()


def front(rel_ids, visit_to, src_row, neg_src, neg_dst, relation, tables):
    rows, width = tables[0].shape
    edges = src_row.shape[1]
    blocks, negs = neg_src.shape
    sds = jax.ShapeDtypeStruct
    return call(
        front_body,
        (
            sds((edges, width), half),
            sds((blocks * negs, width), half),
            sds((edges, width), half),
            sds((edges, negs), half),
            sds((edges, width), full),
            sds((edges, 128), full),
        ),
        [
            pltpu.VMEM((rows, width), half),
            pltpu.VMEM((rows, width), half),
            pltpu.VMEM((negs, width), half),
            pltpu.VMEM((blocks, width, width), full),
            pltpu.SemaphoreType.DMA((blocks,)),
            pltpu.SemaphoreType.DMA,
            pltpu.SemaphoreType.DMA,
        ],
        [SMEM] * 2 + [VMEM] * 3 + [HBM] * 5,
        cost(2 * edges * width * (3 * rows + 2 * negs), 12 * MEBI),
    )(rel_ids, visit_to, src_row, neg_src, neg_dst, relation, *tables)


def model(rel_ids, edge_count, slot, fetched, relation, peers, room, rest):
    slots, width = fetched.shape
    edges = slot.shape[1]
    blocks = rel_ids.shape[1]
    negs = rest[1].shape[0] // blocks
    sds = jax.ShapeDtypeStruct
    return call(
        model_body,
        (
            sds((peers, room + blocks * (width // peers), width), half),
            sds((edges, width), half),
            sds((blocks * negs, width), half),
            sds((blocks * negs, width), half),
        ),
        [pltpu.VMEM(x.shape, x.dtype) for x in rest]
        + [
            pltpu.VMEM((edges, width), half),
            pltpu.VMEM((blocks * negs, width), half),
            pltpu.VMEM((blocks * negs, width), half),
            pltpu.VMEM((edges, width), half),
            pltpu.VMEM((edges, width), half),
            pltpu.VMEM((blocks, width, width), full),
            pltpu.VMEM((width, negs), full),
            pltpu.VMEM((width, negs), full),
            pltpu.VMEM((width, width), full),
            pltpu.VMEM((width, width), full),
            pltpu.SemaphoreType.DMA((blocks,)),
            pltpu.SemaphoreType.DMA((6,)),
            pltpu.SemaphoreType.DMA((3,)),
        ],
        [SMEM] * 2 + [VMEM] * 2 + [HBM] * 7,
        outs=[VMEM] + [HBM] * 3,
    )(rel_ids, edge_count, slot, fetched, relation, *rest)


def sums_body(src_ref, neg_src_ref, neg_dst_ref, d_src, d_neg_src, d_neg_dst, own_ref, visit_ref):
    rows = own_ref.shape[0]
    blocks, negs = neg_src_ref.shape
    step = 256

    def part(t, carry):
        first = pl.multiple_of(t * step, step)
        own = dot(place(src_ref[...], first, step), d_src[...], 1, 0)
        visit = jnp.zeros_like(own)
        for block in range(blocks):
            at = slice(block * negs, (block + 1) * negs)
            one = slice(block, block + 1)
            own += dot(place(neg_src_ref[one, :], first, step), d_neg_src[at, :], 1, 0)
            visit += dot(place(neg_dst_ref[one, :], first, step), d_neg_dst[at, :], 1, 0)
        own_ref[pl.ds(first, step), :] = own
        visit_ref[pl.ds(first, step), :] = visit
        return carry

    lax.fori_loop(0, rows // step, part, 0)


def home_body(
    parts, partner_ref, group_ref, visit_to_ref, asked_ref, returned_ref, visit_ref, *refs
):
    outs, (total, list_ref, count_ref) = refs[: len(parts)], refs[len(parts) :]
    rows, width = visit_ref.shape
    places = asked_ref.shape[2]
    together = 4
    list_peers(partner_ref, group_ref, list_ref, count_ref)
    for part, out_ref in zip(parts, outs):
        count = count_ref[part]
        total[...] = jnp.where(visit_to_ref[0] == part, visit_ref[...], 0.0)

        def add(t, carry, part=part, count=count):
            asks, backs = [], []
            for k in range(together):
                peer = list_ref[part, jnp.minimum(together * t + k, count - 1)]
                ask = asked_ref[pl.ds(peer, 1), 0, :]
                asks.append(jnp.where(together * t + k < count, ask, -1))
                backs.append(returned_ref[pl.ds(peer, 1), :places, :].reshape(places, width))
            ask = jnp.concatenate(asks, axis=1)
            back = jnp.concatenate(backs, axis=0)
            for first in range(0, rows, 512):
                total[first : first + 512] += dot(place(ask, first, 512), back, 1, 0)
            return carry

        lax.fori_loop(0, (count + together - 1) // together, add, 0)
        out_ref[...] = total[...].astype(half)


def operators_body(ids_ref, part_ref, out_ref):
    peers, _, width = part_ref.shape
    blocks = ids_ref.shape[1]
    rows = out_ref.shape[1]
    out_ref[...] = jnp.zeros_like(out_ref)

    def add(peer, carry):
        piece = part_ref[pl.ds(peer, 1)].reshape(blocks * rows, width).astype(full)
        for block in range(blocks):
            at = ids_ref[peer, block]
            out_ref[pl.ds(at, 1)] += piece[block * rows : (block + 1) * rows].reshape(1, rows, width)
        return carry

    lax.fori_loop(0, peers, add, 0)


def laid(column):
    return jnp.broadcast_to(column, (column.shape[0], 128)).T[:1, :]


def relation_body(part_ref, grad_ref, relation_ref, acc_ref, *refs):
    (new_ref, acc_new_ref, acc_turned, acc_found), before = refs[-4:], refs[:-4]
    step, rows, width = relation_ref.shape
    relations = acc_ref.shape[0]
    at = pl.program_id(0)
    first = part_ref[0] * (relations // 2) + at * step
    lane = lax.broadcasted_iota(jnp.int32, (rows, 128), 1)

    @pl.when(at == 0)
    def _():
        short = jnp.zeros((128 - relations, rows), full)
        acc_turned[...] = jnp.concatenate([acc_ref[...], short], axis=0).T
        if before:
            acc_found[...] = jnp.concatenate([before[1][...], short], axis=0).T
        else:
            acc_found[...] = jnp.zeros_like(acc_found)

    for k in range(step):
        here = lane == first + k
        grad = grad_ref[:, k].astype(full).reshape(rows, width)
        square = grad * grad
        parts = sum(square[:, at : at + 128] for at in range(0, width, 128))
        acc = jnp.sum(
            parts * (1.0 / width) + jnp.where(here, acc_turned[...], 0.0), axis=1, keepdims=True
        )
        acc_found[...] = jnp.where(here, acc, acc_found[...])
        new_ref[k] = relation_ref[k] - grad * (step_rate / jnp.sqrt(acc))

    @pl.when(at == pl.num_programs(0) - 1)
    def _():
        acc_new_ref[...] = acc_found[...].T[:relations]


def entity_body(grad_ref, home_ref, sibling_ref, cross_ref, entity_ref, acc_ref, new_ref, acc_new_ref):
    grad = (
        grad_ref[...]
        + home_ref[...].astype(full)
        + sibling_ref[...].astype(full)
        + cross_ref[...].astype(full)
    )
    square = jnp.mean(grad * grad, axis=1, keepdims=True)
    acc = acc_ref[...]
    acc_new_ref[...] = acc + laid(square)
    new_ref[0] = entity_ref[0] - grad * (step_rate / jnp.sqrt(turned(acc)[:, :1] + square))


def relation_update(part, grad, relation, relation_acc, before=()):
    peers, count, extra, width = grad.shape
    relations, rows = relation_acc.shape
    step = 10 if count % 10 == 0 else 1
    steps = count // step
    whole = pl.BlockSpec((relations, rows), lambda i, part: (0, 0))
    block = pl.BlockSpec((step, rows, width), lambda i, part: (part[0] * steps + i, 0, 0))
    return pl.pallas_call(
        relation_body,
        grid_spec=pltpu.PrefetchScalarGridSpec(
            num_scalar_prefetch=1,
            grid=(steps,),
            in_specs=[
                pl.BlockSpec((peers, step, extra, width), lambda i, part: (0, i, 0, 0)),
                block,
                whole,
            ]
            + [HBM, whole][: len(before)],
            out_specs=[block, whole],
            scratch_shapes=[pltpu.VMEM((rows, 128), full), pltpu.VMEM((rows, 128), full)],
        ),
        out_shape=[
            jax.ShapeDtypeStruct(relation.shape, full),
            jax.ShapeDtypeStruct(relation_acc.shape, full),
        ],
        input_output_aliases={4: 0} if before else {},
        compiler_params=pltpu.CompilerParams(vmem_limit_bytes=60 * MEBI),
        cost_estimate=cost(0, 24 * MEBI),
    )(part, grad, relation, relation_acc, *before)


def entity_update(grad, home, sibling, cross, entity, entity_acc):
    rows, width = grad.shape
    step = 256
    part = pl.BlockSpec((step, width), lambda i: (i, 0))
    block = pl.BlockSpec((1, step, width), lambda i: (0, i, 0))
    line = pl.BlockSpec((1, step), lambda i: (0, i))
    return pl.pallas_call(
        entity_body,
        grid=(rows // step,),
        in_specs=[part] * 4 + [block, line],
        out_specs=[block, line],
        out_shape=[
            jax.ShapeDtypeStruct(entity.shape, full),
            jax.ShapeDtypeStruct(entity_acc.shape, full),
        ],
        compiler_params=pltpu.CompilerParams(vmem_limit_bytes=60 * MEBI),
        cost_estimate=cost(0, 24 * MEBI),
    )(grad, home, sibling, cross, entity, entity_acc)


def on_device(
    entity,
    entity_acc,
    relation,
    relation_acc,
    partner,
    src_row,
    dst_owner,
    dst_row,
    rel_ids,
    neg_src,
    neg_dst,
    edge_count,
):
    me = lax.axis_index("grp")
    place_id = lax.axis_index("dev")
    peers = lax.axis_size("dev")
    rows, width = entity.shape[1:]
    edges = src_row.shape[1]
    blocks = rel_ids.shape[1]
    negs = neg_src.shape[2]
    relations = relation.shape[0]
    room = 2 * edges // peers
    extra = width // peers
    sds = jax.ShapeDtypeStruct

    def neighbour(x, flip):
        return lax.ppermute(x, "grp", [(g, g ^ flip) for g in range(4)])

    group = me.reshape(1)
    visit_to = (partner[me, place_id] ^ me).reshape(1)
    owners = dst_owner.reshape(1, edges)
    neg_src = neg_src.reshape(blocks, negs)
    neg_dst = neg_dst.reshape(blocks, negs)

    own = entity[0].astype(half)
    cross = neighbour(own, 2)
    sibling = neighbour(own, 1)
    slot, wanted = call(
        slots_body,
        (sds((1, edges), jnp.int32), sds((peers, 2, room), jnp.int32)),
        specs=[SMEM] + [VMEM] * 2,
    )(rel_ids, owners, dst_row)
    asked = lax.all_to_all(wanted, "dev", split_axis=0, concat_axis=0, tiled=True)
    cross, asked = lax.optimization_barrier((cross, asked))
    cross_sibling = neighbour(cross, 1)
    tables = (own, sibling, cross, cross_sibling)

    lists = [pltpu.SMEM((4, peers), jnp.int32), pltpu.SMEM((4,), jnp.int32)]
    found = call(
        answer_body,
        sds((peers, room, width), half),
        [
            pltpu.VMEM((4, rows, width), half),
            pltpu.VMEM((peers, room, width), half),
            pltpu.SemaphoreType.DMA((4,)),
            pltpu.SemaphoreType.DMA,
        ],
        [SMEM] * 2 + [VMEM] + [HBM] * 4,
        outs=HBM,
    )(partner, group, asked, *tables)
    fetched = lax.all_to_all(found, "dev", split_axis=0, concat_axis=0, tiled=True)

    rest = front(rel_ids, visit_to, src_row, neg_src, neg_dst, relation, tables)
    outgoing, d_src, d_neg_src, d_neg_dst = model(
        rel_ids, edge_count, slot, fetched.reshape(peers * room, width), relation, peers, room, rest
    )
    returned = lax.all_to_all(outgoing, "dev", split_axis=0, concat_axis=0, tiled=True)

    own_grad, visit_grad = call(
        sums_body,
        (sds((rows, width), full), sds((rows, width), full)),
        (),
        [VMEM] * 6,
        cost(2 * 3 * edges * rows * width, 7 * rows * width * 2),
    )(src_row, neg_src, neg_dst, d_src, d_neg_src, d_neg_dst)

    returned, own_grad, visit_grad = lax.optimization_barrier((returned, own_grad, visit_grad))

    def home(parts, returned):
        return call(
            functools.partial(home_body, parts),
            tuple(sds((rows, width), half) for _ in parts),
            [pltpu.VMEM((rows, width), full)] + lists,
            [SMEM] * 3 + [VMEM] * 3,
            cost(0, 24 * MEBI),
        )(partner, group, visit_to, asked, returned, visit_grad)

    home_cross_sibling, home_cross = home((3, 2), returned)
    chip_cross = (home_cross.astype(full) + neighbour(home_cross_sibling, 1).astype(full)).astype(half)

    rel_part = call(operators_body, sds((relations, extra, width), full), (), [SMEM, VMEM])(
        asked[:, 1, :blocks], returned[:, room:, :]
    )
    core = me & 1
    halves = rel_part.reshape(2, relations // 2, extra, width)
    mine = lax.dynamic_index_in_dim(halves, core, 0, keepdims=False)
    other = lax.dynamic_index_in_dim(halves, 1 - core, 0, keepdims=False)
    chip = mine + neighbour(other, 1)
    pair = (chip + neighbour(chip, 2)).astype(half)
    near = lax.ppermute(pair, "dev", [(d, d ^ 1) for d in range(peers)])
    low = (place_id & 1) == 0
    planes = jnp.stack([jnp.where(low, pair, near), jnp.where(low, near, pair)])
    home_sibling, home_own = home((1, 0), returned)
    planes, chip_cross, home_sibling, home_own = lax.optimization_barrier(
        (planes, chip_cross, home_sibling, home_own)
    )
    from_cross = neighbour(chip_cross, 2)
    from_sibling = neighbour(home_sibling, 1)
    gathered = lax.all_to_all(
        jnp.broadcast_to(planes[None], (peers // 2,) + planes.shape),
        "dev",
        split_axis=0,
        concat_axis=0,
        axis_index_groups=[list(range(k, peers, 2)) for k in range(2)],
        tiled=True,
    ).reshape((peers,) + pair.shape)

    entity_new, acc_new = entity_update(
        own_grad, home_own, from_sibling, from_cross, entity, entity_acc
    )
    gathered, entity_new, acc_new = lax.optimization_barrier((gathered, entity_new, acc_new))
    other_half = neighbour(gathered, 1)
    before = relation_update(core.reshape(1), gathered, relation, relation_acc)
    relation_new, relation_acc_new = relation_update(
        (1 - core).reshape(1), other_half, relation, relation_acc, before
    )
    return (entity_new, acc_new, relation_new, relation_acc_new)


def solution(mesh):
    return jax.shard_map(
        on_device,
        mesh=mesh,
        in_specs=(
            P("grp", "dev", None),
            P("grp", "dev"),
            P(),
            P(),
            P(),
            P("grp", "dev"),
            P("grp", "dev", None),
            P("grp", "dev"),
            P("grp", "dev"),
            P("grp", "dev", None),
            P("grp", "dev", None),
            P("grp", "dev"),
        ),
        out_specs=(P("grp", "dev", None), P("grp", "dev"), P(), P()),
        check_vma=False,
    )
```

```python
import functools

import jax
import jax.numpy as jnp
from jax import lax
from jax.experimental import pallas as pl
from jax.experimental.pallas import tpu as pltpu
from jax.sharding import PartitionSpec as P

step_rate = 0.1
MEBI = 1024 * 1024
half = jnp.bfloat16
full = jnp.float32
VMEM = pl.BlockSpec(memory_space=pltpu.VMEM)
SMEM = pl.BlockSpec(memory_space=pltpu.SMEM)
HBM = pl.BlockSpec(memory_space=pltpu.HBM)


def dot(a, b, ca, cb):
    return lax.dot_general(a, b, (((ca,), (cb,)), ((), ())), preferred_element_type=full)


def turned(row):
    pieces = [
        jnp.broadcast_to(row[:, at : at + 128], (128, 128)).T for at in range(0, row.shape[1], 128)
    ]
    return pieces[0] if len(pieces) == 1 else jnp.concatenate(pieces, axis=0)


def pick(row, width):
    spread = turned(row.astype(full))
    lane = lax.broadcasted_iota(jnp.int32, (1, 128), 1).astype(full)
    pieces = [
        jnp.where(spread == lane + float(at), 1.0, 0.0).astype(half) for at in range(0, width, 128)
    ]
    return jnp.concatenate(pieces, axis=1)


def place(row, first, height):
    line = lax.broadcasted_iota(jnp.int32, (height, 1), 0) + first
    return jnp.where(row == line, 1.0, 0.0).astype(half)


def call(body, shapes, scratch=(), specs=None, cost=None, outs=None, mebi=60, **kw):
    return pl.pallas_call(
        body,
        out_shape=shapes,
        in_specs=specs,
        out_specs=outs or jax.tree.map(lambda _: VMEM, shapes),
        scratch_shapes=list(scratch),
        compiler_params=pltpu.CompilerParams(vmem_limit_bytes=mebi * MEBI),
        cost_estimate=cost,
        **kw,
    )


def cost(flops, moved):
    return pl.CostEstimate(flops=int(flops), bytes_accessed=int(moved), transcendentals=0)


def slots_body(rel_ref, owner_ref, row_ref, slot_ref, wanted_ref):
    peers, _, room = wanted_ref.shape
    edges = owner_ref.shape[1]
    step = 256
    before = lax.broadcasted_iota(jnp.int32, (step, step), 0)
    after = lax.broadcasted_iota(jnp.int32, (step, step), 1)
    upper = jnp.where(before <= after, 1.0, 0.0).astype(half)
    peer = lax.broadcasted_iota(jnp.int32, (peers, step), 0)
    carry = jnp.zeros((peers, 1), full)
    high = jnp.zeros((peers, room), full)
    low = jnp.zeros((peers, room), full)
    for at in range(0, edges, step):
        owner = owner_ref[:, at : at + step]
        hit = jnp.where(peer == owner, 1.0, 0.0)
        count = dot(hit.astype(half), upper, 1, 0) + carry
        carry = count[:, step - 1 :]
        order = (jnp.sum(count * hit, axis=0, keepdims=True) - 1.0).astype(jnp.int32)
        slot_ref[:, at : at + step] = owner * room + order
        spot = place(order, 0, room)
        row = row_ref[:, at : at + step]
        top = lax.shift_right_logical(row, 4)
        high += dot((hit * top.astype(full)).astype(half), spot, 1, 1)
        low += dot((hit * (row - top * 16).astype(full)).astype(half), spot, 1, 1)
    wanted_ref[:, 0, :] = (high * 16.0 + low).astype(jnp.int32)
    lane = lax.broadcasted_iota(jnp.int32, (peers, room), 1)
    ids = jnp.zeros((peers, room), jnp.int32)
    for block in range(rel_ref.shape[1]):
        ids = jnp.where(lane == block, rel_ref[0, block], ids)
    wanted_ref[:, 1, :] = ids


def list_peers(partner_ref, group_ref, list_ref, count_ref):
    peers = partner_ref.shape[1]
    me = group_ref[0]
    for part in range(4):
        count_ref[part] = 0

    def add(peer, carry):
        part = partner_ref[me, peer] ^ me
        at = count_ref[part]
        list_ref[part, at] = peer
        count_ref[part] = at + 1
        return carry

    lax.fori_loop(0, peers, add, 0)


def answer_body(partner_ref, group_ref, asked_ref, *refs):
    tables_in, (found_out, tables, found, sems, out_sem) = refs[:4], refs[4:]
    copies = [
        pltpu.make_async_copy(table, tables.at[part], sems.at[part])
        for part, table in enumerate(tables_in)
    ]
    for copy in copies:
        copy.start()
    peers, _, room = asked_ref.shape
    rows, width = tables.shape[1:]
    me = group_ref[0]
    for copy in copies:
        copy.wait()

    def answer(peer, carry):
        table = tables[partner_ref[me, peer] ^ me]
        got = dot(pick(asked_ref[pl.ds(peer, 1), 0, :], rows), table, 1, 0)
        found[pl.ds(peer, 1)] = got.astype(half).reshape(1, room, width)
        return carry

    lax.fori_loop(0, peers, answer, 0, unroll=4)
    back = pltpu.make_async_copy(found, found_out, out_sem)
    back.start()
    back.wait()


def operators_in(rel_ref, relation_ref, operator, sems):
    copies = [
        pltpu.make_async_copy(relation_ref.at[rel_ref[0, block]], operator.at[block], sems.at[block])
        for block in range(rel_ref.shape[1])
    ]
    for copy in copies:
        copy.start()
    return copies


def front_body(
    rel_ref,
    visit_ref,
    src_ref,
    neg_src_ref,
    neg_dst_ref,
    relation_ref,
    own_table,
    sibling_table,
    cross_table,
    cross_sibling_table,
    src_out,
    neg_src_out,
    lhs_out,
    terms_out,
    pull_out,
    stats_out,
    own,
    visit,
    neg_dst,
    operator,
    op_sems,
    own_sem,
    visit_sem,
):
    rows = own.shape[0]
    blocks, negs = neg_src_ref.shape
    edges = src_ref.shape[1]
    block_len = edges // blocks
    step = 256
    op_copies = operators_in(rel_ref, relation_ref, operator, op_sems)
    own_copy = pltpu.make_async_copy(own_table, own, own_sem)
    own_copy.start()
    for part, table in enumerate((own_table, sibling_table, cross_table, cross_sibling_table)):

        @pl.when(visit_ref[0] == part)
        def _(table=table):
            pltpu.make_async_copy(table, visit, visit_sem).start()

    own_copy.wait()
    pltpu.make_async_copy(own_table, visit, visit_sem).wait()
    for copy in op_copies:
        copy.wait()
    for block in range(blocks):
        for at in range(0, negs, step):
            to = block * negs + at
            neg_src_out[to : to + step] = dot(
                pick(neg_src_ref[block : block + 1, at : at + step], rows), own[...], 1, 0
            ).astype(half)
            neg_dst[at : at + step] = dot(
                pick(neg_dst_ref[block : block + 1, at : at + step], rows), visit[...], 1, 0
            ).astype(half)

        def chunk(t, carry, block=block):
            at = pl.multiple_of(block * block_len + t * step, step)
            here = pl.ds(at, step)
            op = operator[block].astype(half)
            src = dot(pick(src_ref[:, here], rows), own[...], 1, 0).astype(half)
            lhs = dot(src, op, 1, 0).astype(half)
            scores = dot(lhs, neg_dst[...], 1, 1)
            highest = jnp.max(scores, axis=1, keepdims=True)
            terms = jnp.exp(scores - highest)
            lane = lax.broadcasted_iota(jnp.int32, (step, 128), 1)
            stats_out[here, :] = jnp.where(lane < 64, highest, jnp.sum(terms, axis=1, keepdims=True))
            terms = terms.astype(half)
            src_out[here, :] = src
            lhs_out[here, :] = lhs
            terms_out[here, :] = terms
            pull_out[here, :] = dot(terms, neg_dst[...], 1, 0)
            return carry

        lax.fori_loop(0, block_len // step, chunk, 0, unroll=2)


def model_body(
    rel_ref,
    count_ref,
    slot_ref,
    fetched_ref,
    relation_ref,
    src_in,
    neg_src_in,
    lhs_in,
    terms_in,
    pull_in,
    stats_in,
    d_op_ref,
    d_dst_out,
    d_src_out,
    d_neg_src_out,
    d_neg_dst_out,
    src_ref,
    neg_src_ref,
    lhs_ref,
    terms_ref,
    pull_ref,
    stats_ref,
    d_src_ref,
    d_neg_src_ref,
    d_neg_dst_ref,
    dst_ref,
    d_dst,
    operator,
    neg_dst_sum,
    neg_src_sum,
    op_sum,
    op_turned_sum,
    op_sems,
    in_sems,
    out_sems,
):
    slots, width = fetched_ref.shape
    edges = slot_ref.shape[1]
    blocks = rel_ref.shape[1]
    block_len = edges // blocks
    negs = neg_src_ref.shape[0] // blocks
    peers = d_op_ref.shape[0]
    extra = width // peers
    step = 256
    copies = operators_in(rel_ref, relation_ref, operator, op_sems)
    pairs = (
        (src_in, src_ref),
        (neg_src_in, neg_src_ref),
        (lhs_in, lhs_ref),
        (pull_in, pull_ref),
        (stats_in, stats_ref),
        (terms_in, terms_ref),
    )
    for i, (there, here) in enumerate(pairs):
        copies.append(pltpu.make_async_copy(there, here, in_sems.at[i]))
        copies[-1].start()

    def fetch(t, carry):
        here = pl.ds(pl.multiple_of(t * step, step), step)
        dst_ref[here, :] = dot(pick(slot_ref[:, here], slots), fetched_ref[...], 1, 0).astype(half)
        return carry

    lax.fori_loop(0, edges // step, fetch, 0, unroll=4)
    for copy in copies:
        copy.wait()
    for block in range(blocks):
        neg_dst_sum[...] = jnp.zeros_like(neg_dst_sum)
        neg_src_sum[...] = jnp.zeros_like(neg_src_sum)
        op_sum[...] = jnp.zeros_like(op_sum)
        op_turned_sum[...] = jnp.zeros_like(op_turned_sum)

        def chunk(t, carry, block=block):
            at = pl.multiple_of(block * block_len + t * step, step)
            here = pl.ds(at, step)
            op = operator[block].astype(half)
            dst = dst_ref[here, :]
            src = src_ref[here, :]
            lhs = lhs_ref[here, :]
            neg_src = neg_src_ref[block * negs : (block + 1) * negs, :]
            line = lax.broadcasted_iota(jnp.int32, (step, 1), 0) + at
            live = jnp.where(line < count_ref[0, 0], 1.0, 0.0)
            rhs = dot(dst, op, 1, 1).astype(half)
            positive = jnp.sum(lhs.astype(full) * dst.astype(full), axis=1, keepdims=True)

            scores = dot(rhs, neg_src, 1, 1)
            highest = jnp.maximum(jnp.max(scores, axis=1, keepdims=True), positive)
            terms = jnp.exp(scores - highest)
            own = jnp.exp(positive - highest)
            scale = live / (own + jnp.sum(terms, axis=1, keepdims=True))
            src_terms = (terms * scale).astype(half)
            d_positive = own * scale - live

            top = stats_ref[here, :]
            top, total = top[:, :1], top[:, 64:65]
            highest = jnp.maximum(top, positive)
            lower = jnp.exp(top - highest)
            own = jnp.exp(positive - highest)
            scale = live / (own + total * lower)
            d_positive += own * scale - live
            scale = lower * scale

            d_lhs = (pull_ref[here, :] * scale).astype(half)
            d_lhs = d_lhs + (d_positive * dst.astype(full)).astype(half)
            d_rhs = dot(src_terms, neg_src, 1, 0).astype(half)
            scaled = (lhs.astype(full) * scale).astype(half)
            neg_dst_sum[...] += dot(scaled, terms_ref[here, :], 0, 0)
            neg_src_sum[...] += dot(rhs, src_terms, 0, 0)
            d_src_ref[here, :] = dot(d_lhs, op, 1, 1).astype(half)
            op_sum[...] += dot(src, d_lhs, 0, 0)
            op_turned_sum[...] += dot(d_rhs, dst, 0, 0)
            d_dst[here, :] = dot(d_rhs, op, 1, 0).astype(half) + (
                d_positive * lhs.astype(full)
            ).astype(half)
            return carry

        lax.fori_loop(0, block_len // step, chunk, 0, unroll=4)
        d_neg_dst_ref[block * negs : (block + 1) * negs, :] = neg_dst_sum[...].T.astype(half)
        d_neg_src_ref[block * negs : (block + 1) * negs, :] = neg_src_sum[...].T.astype(half)
        d_op = op_sum[...].astype(half) + op_turned_sum[...].astype(half)
        d_op_ref[:, block * extra : (block + 1) * extra, :] = d_op.reshape(peers, extra, width)
    backs = []
    for i, (here, there) in enumerate(
        (
            (d_dst, d_dst_out),
            (d_src_ref, d_src_out),
            (d_neg_src_ref, d_neg_src_out),
            (d_neg_dst_ref, d_neg_dst_out),
        )
    ):
        backs.append(pltpu.make_async_copy(here, there, out_sems.at[i]))
        backs[-1].start()

    for copy in backs:
        copy.wait()


def send_body(slot_ref, d_dst, outgoing_ref):
    peers, places, width = outgoing_ref.shape

    def send(t, carry):
        spot = place(slot_ref[...], t * 2 * places, 2 * places)
        out = dot(spot, d_dst[...], 1, 0).astype(half)
        outgoing_ref[pl.ds(2 * t, 2), :, :] = out.reshape(2, places, width)
        return carry

    lax.fori_loop(0, peers // 2, send, 0, unroll=4)


def front(rel_ids, visit_to, src_row, neg_src, neg_dst, relation, tables):
    rows, width = tables[0].shape
    edges = src_row.shape[1]
    blocks, negs = neg_src.shape
    sds = jax.ShapeDtypeStruct
    return call(
        front_body,
        (
            sds((edges, width), half),
            sds((blocks * negs, width), half),
            sds((edges, width), half),
            sds((edges, negs), half),
            sds((edges, width), full),
            sds((edges, 128), full),
        ),
        [
            pltpu.VMEM((rows, width), half),
            pltpu.VMEM((rows, width), half),
            pltpu.VMEM((negs, width), half),
            pltpu.VMEM((blocks, width, width), full),
            pltpu.SemaphoreType.DMA((blocks,)),
            pltpu.SemaphoreType.DMA,
            pltpu.SemaphoreType.DMA,
        ],
        [SMEM] * 2 + [VMEM] * 3 + [HBM] * 5,
        cost(2 * edges * width * (3 * rows + 2 * negs), 12 * MEBI),
    )(rel_ids, visit_to, src_row, neg_src, neg_dst, relation, *tables)


def model(rel_ids, edge_count, slot, fetched, relation, peers, rest):
    slots, width = fetched.shape
    edges = slot.shape[1]
    blocks = rel_ids.shape[1]
    negs = rest[1].shape[0] // blocks
    sds = jax.ShapeDtypeStruct
    return call(
        model_body,
        (
            sds((peers, blocks * (width // peers), width), half),
            sds((edges, width), half),
            sds((edges, width), half),
            sds((blocks * negs, width), half),
            sds((blocks * negs, width), half),
        ),
        [pltpu.VMEM(x.shape, x.dtype) for x in rest]
        + [
            pltpu.VMEM((edges, width), half),
            pltpu.VMEM((blocks * negs, width), half),
            pltpu.VMEM((blocks * negs, width), half),
            pltpu.VMEM((edges, width), half),
            pltpu.VMEM((edges, width), half),
            pltpu.VMEM((blocks, width, width), full),
            pltpu.VMEM((width, negs), full),
            pltpu.VMEM((width, negs), full),
            pltpu.VMEM((width, width), full),
            pltpu.VMEM((width, width), full),
            pltpu.SemaphoreType.DMA((blocks,)),
            pltpu.SemaphoreType.DMA((6,)),
            pltpu.SemaphoreType.DMA((4,)),
        ],
        [SMEM] * 2 + [VMEM] * 2 + [HBM] * 7,
        outs=[VMEM] + [HBM] * 4,
    )(rel_ids, edge_count, slot, fetched, relation, *rest)


def sums_body(src_ref, neg_src_ref, neg_dst_ref, d_src, d_neg_src, d_neg_dst, own_ref, visit_ref):
    rows = own_ref.shape[0]
    blocks, negs = neg_src_ref.shape
    step = 256

    def part(t, carry):
        first = pl.multiple_of(t * step, step)
        own = dot(place(src_ref[...], first, step), d_src[...], 1, 0)
        visit = jnp.zeros_like(own)
        for block in range(blocks):
            at = slice(block * negs, (block + 1) * negs)
            one = slice(block, block + 1)
            own += dot(place(neg_src_ref[one, :], first, step), d_neg_src[at, :], 1, 0)
            visit += dot(place(neg_dst_ref[one, :], first, step), d_neg_dst[at, :], 1, 0)
        own_ref[pl.ds(first, step), :] = own
        visit_ref[pl.ds(first, step), :] = visit
        return carry

    lax.fori_loop(0, rows // step, part, 0)


def home_body(
    parts, partner_ref, group_ref, visit_to_ref, asked_ref, returned_ref, visit_ref, *refs
):
    outs, (total, list_ref, count_ref) = refs[: len(parts)], refs[len(parts) :]
    rows, width = visit_ref.shape
    places = asked_ref.shape[2]
    together = 4
    list_peers(partner_ref, group_ref, list_ref, count_ref)
    for part, out_ref in zip(parts, outs):
        count = count_ref[part]
        total[...] = jnp.where(visit_to_ref[0] == part, visit_ref[...], 0.0)

        def add(t, carry, part=part, count=count):
            asks, backs = [], []
            for k in range(together):
                peer = list_ref[part, jnp.minimum(together * t + k, count - 1)]
                ask = asked_ref[pl.ds(peer, 1), 0, :]
                asks.append(jnp.where(together * t + k < count, ask, -1))
                backs.append(returned_ref[pl.ds(peer, 1), :places, :].reshape(places, width))
            ask = jnp.concatenate(asks, axis=1)
            back = jnp.concatenate(backs, axis=0)
            for first in range(0, rows, 512):
                total[first : first + 512] += dot(place(ask, first, 512), back, 1, 0)
            return carry

        lax.fori_loop(0, (count + together - 1) // together, add, 0)
        out_ref[...] = total[...].astype(half)


def operators_body(ids_ref, part_ref, out_ref):
    peers, _, width = part_ref.shape
    blocks = ids_ref.shape[1]
    rows = out_ref.shape[1]
    out_ref[...] = jnp.zeros_like(out_ref)

    def add(peer, carry):
        piece = part_ref[pl.ds(peer, 1)].reshape(blocks * rows, width).astype(full)
        for block in range(blocks):
            at = ids_ref[peer, block]
            out_ref[pl.ds(at, 1)] += piece[block * rows : (block + 1) * rows].reshape(1, rows, width)
        return carry

    lax.fori_loop(0, peers, add, 0)


def laid(column):
    return jnp.broadcast_to(column, (column.shape[0], 128)).T[:1, :]


def relation_body(part_ref, grad_ref, relation_ref, acc_ref, *refs):
    (new_ref, acc_new_ref, acc_turned, acc_found), before = refs[-4:], refs[:-4]
    step, rows, width = relation_ref.shape
    relations = acc_ref.shape[0]
    at = pl.program_id(0)
    first = part_ref[0] * (relations // 2) + at * step
    lane = lax.broadcasted_iota(jnp.int32, (rows, 128), 1)

    @pl.when(at == 0)
    def _():
        short = jnp.zeros((128 - relations, rows), full)
        acc_turned[...] = jnp.concatenate([acc_ref[...], short], axis=0).T
        if before:
            acc_found[...] = jnp.concatenate([before[1][...], short], axis=0).T
        else:
            acc_found[...] = jnp.zeros_like(acc_found)

    for k in range(step):
        here = lane == first + k
        grad = grad_ref[:, k].astype(full).reshape(rows, width)
        square = grad * grad
        parts = sum(square[:, at : at + 128] for at in range(0, width, 128))
        acc = jnp.sum(
            parts * (1.0 / width) + jnp.where(here, acc_turned[...], 0.0), axis=1, keepdims=True
        )
        acc_found[...] = jnp.where(here, acc, acc_found[...])
        new_ref[k] = relation_ref[k] - grad * (step_rate / jnp.sqrt(acc))

    @pl.when(at == pl.num_programs(0) - 1)
    def _():
        acc_new_ref[...] = acc_found[...].T[:relations]


def entity_body(grad_ref, home_ref, sibling_ref, cross_ref, entity_ref, acc_ref, new_ref, acc_new_ref):
    grad = (
        grad_ref[...]
        + home_ref[...].astype(full)
        + sibling_ref[...].astype(full)
        + cross_ref[...].astype(full)
    )
    square = jnp.mean(grad * grad, axis=1, keepdims=True)
    acc = acc_ref[...]
    acc_new_ref[...] = acc + laid(square)
    new_ref[0] = entity_ref[0] - grad * (step_rate / jnp.sqrt(turned(acc)[:, :1] + square))


def relation_update(part, grad, relation, relation_acc, before=()):
    peers, count, extra, width = grad.shape
    relations, rows = relation_acc.shape
    step = 10 if count % 10 == 0 else 1
    steps = count // step
    whole = pl.BlockSpec((relations, rows), lambda i, part: (0, 0))
    block = pl.BlockSpec((step, rows, width), lambda i, part: (part[0] * steps + i, 0, 0))
    return pl.pallas_call(
        relation_body,
        grid_spec=pltpu.PrefetchScalarGridSpec(
            num_scalar_prefetch=1,
            grid=(steps,),
            in_specs=[
                pl.BlockSpec((peers, step, extra, width), lambda i, part: (0, i, 0, 0)),
                block,
                whole,
            ]
            + [HBM, whole][: len(before)],
            out_specs=[block, whole],
            scratch_shapes=[pltpu.VMEM((rows, 128), full), pltpu.VMEM((rows, 128), full)],
        ),
        out_shape=[
            jax.ShapeDtypeStruct(relation.shape, full),
            jax.ShapeDtypeStruct(relation_acc.shape, full),
        ],
        input_output_aliases={4: 0} if before else {},
        compiler_params=pltpu.CompilerParams(vmem_limit_bytes=60 * MEBI),
        cost_estimate=cost(0, 24 * MEBI),
    )(part, grad, relation, relation_acc, *before)


def entity_update(grad, home, sibling, cross, entity, entity_acc):
    rows, width = grad.shape
    step = 256
    part = pl.BlockSpec((step, width), lambda i: (i, 0))
    block = pl.BlockSpec((1, step, width), lambda i: (0, i, 0))
    line = pl.BlockSpec((1, step), lambda i: (0, i))
    return pl.pallas_call(
        entity_body,
        grid=(rows // step,),
        in_specs=[part] * 4 + [block, line],
        out_specs=[block, line],
        out_shape=[
            jax.ShapeDtypeStruct(entity.shape, full),
            jax.ShapeDtypeStruct(entity_acc.shape, full),
        ],
        compiler_params=pltpu.CompilerParams(vmem_limit_bytes=60 * MEBI),
        cost_estimate=cost(0, 24 * MEBI),
    )(grad, home, sibling, cross, entity, entity_acc)


def on_device(
    entity,
    entity_acc,
    relation,
    relation_acc,
    partner,
    src_row,
    dst_owner,
    dst_row,
    rel_ids,
    neg_src,
    neg_dst,
    edge_count,
):
    me = lax.axis_index("grp")
    place_id = lax.axis_index("dev")
    peers = lax.axis_size("dev")
    rows, width = entity.shape[1:]
    edges = src_row.shape[1]
    blocks = rel_ids.shape[1]
    negs = neg_src.shape[2]
    relations = relation.shape[0]
    room = 2 * edges // peers
    extra = width // peers
    sds = jax.ShapeDtypeStruct

    def neighbour(x, flip):
        return lax.ppermute(x, "grp", [(g, g ^ flip) for g in range(4)])

    group = me.reshape(1)
    visit_to = (partner[me, place_id] ^ me).reshape(1)
    owners = dst_owner.reshape(1, edges)
    neg_src = neg_src.reshape(blocks, negs)
    neg_dst = neg_dst.reshape(blocks, negs)

    own = entity[0].astype(half)
    cross = neighbour(own, 2)
    sibling = neighbour(own, 1)
    slot, wanted = call(
        slots_body,
        (sds((1, edges), jnp.int32), sds((peers, 2, room), jnp.int32)),
        specs=[SMEM] + [VMEM] * 2,
    )(rel_ids, owners, dst_row)
    asked = lax.all_to_all(wanted, "dev", split_axis=0, concat_axis=0, tiled=True)
    cross, asked = lax.optimization_barrier((cross, asked))
    cross_sibling = neighbour(cross, 1)
    tables = (own, sibling, cross, cross_sibling)

    lists = [pltpu.SMEM((4, peers), jnp.int32), pltpu.SMEM((4,), jnp.int32)]
    found = call(
        answer_body,
        sds((peers, room, width), half),
        [
            pltpu.VMEM((4, rows, width), half),
            pltpu.VMEM((peers, room, width), half),
            pltpu.SemaphoreType.DMA((4,)),
            pltpu.SemaphoreType.DMA,
        ],
        [SMEM] * 2 + [VMEM] + [HBM] * 4,
        outs=HBM,
    )(partner, group, asked, *tables)
    fetched = lax.all_to_all(found, "dev", split_axis=0, concat_axis=0, tiled=True)

    rest = front(rel_ids, visit_to, src_row, neg_src, neg_dst, relation, tables)
    d_op, d_dst, d_src, d_neg_src, d_neg_dst = model(
        rel_ids, edge_count, slot, fetched.reshape(peers * room, width), relation, peers, rest
    )
    d_op_here = lax.all_to_all(d_op, "dev", split_axis=0, concat_axis=0, tiled=True)
    outgoing = call(
        send_body,
        sds((peers, room, width), half),
        (),
        [VMEM] * 2,
        cost(2 * peers * room * edges * width, 4 * MEBI),
    )(slot, d_dst)
    d_op_here, outgoing, d_src, d_neg_src, d_neg_dst = lax.optimization_barrier(
        (d_op_here, outgoing, d_src, d_neg_src, d_neg_dst)
    )
    returned = lax.all_to_all(outgoing, "dev", split_axis=0, concat_axis=0, tiled=True)

    rel_part = call(operators_body, sds((relations, extra, width), full), (), [SMEM, VMEM])(
        asked[:, 1, :blocks], d_op_here
    )
    core = me & 1
    halves = rel_part.reshape(2, relations // 2, extra, width)
    mine = lax.dynamic_index_in_dim(halves, core, 0, keepdims=False)
    other = lax.dynamic_index_in_dim(halves, 1 - core, 0, keepdims=False)
    chip = mine + neighbour(other, 1)
    pair = (chip + neighbour(chip, 2)).astype(half)
    near = lax.ppermute(pair, "dev", [(d, d ^ 1) for d in range(peers)])
    low = (place_id & 1) == 0
    planes = jnp.stack([jnp.where(low, pair, near), jnp.where(low, near, pair)])
    own_grad, visit_grad = call(
        sums_body,
        (sds((rows, width), full), sds((rows, width), full)),
        (),
        [VMEM] * 6,
        cost(2 * 3 * edges * rows * width, 7 * rows * width * 2),
    )(src_row, neg_src, neg_dst, d_src, d_neg_src, d_neg_dst)

    returned, own_grad, visit_grad, planes = lax.optimization_barrier(
        (returned, own_grad, visit_grad, planes)
    )

    def home(parts, returned):
        return call(
            functools.partial(home_body, parts),
            tuple(sds((rows, width), half) for _ in parts),
            [pltpu.VMEM((rows, width), full)] + lists,
            [SMEM] * 3 + [VMEM] * 3,
            cost(0, 24 * MEBI),
        )(partner, group, visit_to, asked, returned, visit_grad)

    home_cross_sibling, home_cross = home((3, 2), returned)
    chip_cross = (home_cross.astype(full) + neighbour(home_cross_sibling, 1).astype(full)).astype(half)
    from_cross = neighbour(chip_cross, 2)
    gathered = lax.all_to_all(
        jnp.broadcast_to(planes[None], (peers // 2,) + planes.shape),
        "dev",
        split_axis=0,
        concat_axis=0,
        axis_index_groups=[list(range(k, peers, 2)) for k in range(2)],
        tiled=True,
    ).reshape((peers,) + pair.shape)

    home_sibling, home_own = home((1, 0), returned)
    from_sibling = neighbour(home_sibling, 1)
    gathered, from_cross = lax.optimization_barrier((gathered, from_cross))
    entity_new, acc_new = entity_update(
        own_grad, home_own, from_sibling, from_cross, entity, entity_acc
    )
    other_half = neighbour(gathered, 1)
    before = relation_update(core.reshape(1), gathered, relation, relation_acc)
    relation_new, relation_acc_new = relation_update(
        (1 - core).reshape(1), other_half, relation, relation_acc, before
    )
    return (entity_new, acc_new, relation_new, relation_acc_new)


def solution(mesh):
    return jax.shard_map(
        on_device,
        mesh=mesh,
        in_specs=(
            P("grp", "dev", None),
            P("grp", "dev"),
            P(),
            P(),
            P(),
            P("grp", "dev"),
            P("grp", "dev", None),
            P("grp", "dev"),
            P("grp", "dev"),
            P("grp", "dev", None),
            P("grp", "dev", None),
            P("grp", "dev"),
        ),
        out_specs=(P("grp", "dev", None), P("grp", "dev"), P(), P()),
        check_vma=False,
    )
```

```python
import functools

import jax
import jax.numpy as jnp
from jax import lax
from jax.experimental import pallas as pl
from jax.experimental.pallas import tpu as pltpu
from jax.sharding import PartitionSpec as P

step_rate = 0.1
MEBI = 1024 * 1024
half = jnp.bfloat16
full = jnp.float32
VMEM = pl.BlockSpec(memory_space=pltpu.VMEM)
SMEM = pl.BlockSpec(memory_space=pltpu.SMEM)
HBM = pl.BlockSpec(memory_space=pltpu.HBM)


def dot(a, b, ca, cb):
    return lax.dot_general(a, b, (((ca,), (cb,)), ((), ())), preferred_element_type=full)


def turned(row):
    pieces = [
        jnp.broadcast_to(row[:, at : at + 128], (128, 128)).T for at in range(0, row.shape[1], 128)
    ]
    return pieces[0] if len(pieces) == 1 else jnp.concatenate(pieces, axis=0)


def pick(row, width):
    spread = turned(row.astype(full))
    lane = lax.broadcasted_iota(jnp.int32, (1, 128), 1).astype(full)
    pieces = [
        jnp.where(spread == lane + float(at), 1.0, 0.0).astype(half) for at in range(0, width, 128)
    ]
    return jnp.concatenate(pieces, axis=1)


def place(row, first, height):
    line = lax.broadcasted_iota(jnp.int32, (height, 1), 0) + first
    return jnp.where(row == line, 1.0, 0.0).astype(half)


def call(body, shapes, scratch=(), specs=None, cost=None, outs=None, mebi=60, **kw):
    return pl.pallas_call(
        body,
        out_shape=shapes,
        in_specs=specs,
        out_specs=outs or jax.tree.map(lambda _: VMEM, shapes),
        scratch_shapes=list(scratch),
        compiler_params=pltpu.CompilerParams(vmem_limit_bytes=mebi * MEBI),
        cost_estimate=cost,
        **kw,
    )


def cost(flops, moved):
    return pl.CostEstimate(flops=int(flops), bytes_accessed=int(moved), transcendentals=0)


def slots_body(rel_ref, owner_ref, row_ref, slot_ref, wanted_ref):
    peers, _, room = wanted_ref.shape
    edges = owner_ref.shape[1]
    step = 256
    before = lax.broadcasted_iota(jnp.int32, (step, step), 0)
    after = lax.broadcasted_iota(jnp.int32, (step, step), 1)
    upper = jnp.where(before <= after, 1.0, 0.0).astype(half)
    peer = lax.broadcasted_iota(jnp.int32, (peers, step), 0)
    carry = jnp.zeros((peers, 1), full)
    high = jnp.zeros((peers, room), full)
    low = jnp.zeros((peers, room), full)
    for at in range(0, edges, step):
        owner = owner_ref[:, at : at + step]
        hit = jnp.where(peer == owner, 1.0, 0.0)
        count = dot(hit.astype(half), upper, 1, 0) + carry
        carry = count[:, step - 1 :]
        order = (jnp.sum(count * hit, axis=0, keepdims=True) - 1.0).astype(jnp.int32)
        slot_ref[:, at : at + step] = owner * room + order
        spot = place(order, 0, room)
        row = row_ref[:, at : at + step]
        top = lax.shift_right_logical(row, 4)
        high += dot((hit * top.astype(full)).astype(half), spot, 1, 1)
        low += dot((hit * (row - top * 16).astype(full)).astype(half), spot, 1, 1)
    wanted_ref[:, 0, :] = (high * 16.0 + low).astype(jnp.int32)
    lane = lax.broadcasted_iota(jnp.int32, (peers, room), 1)
    ids = jnp.zeros((peers, room), jnp.int32)
    for block in range(rel_ref.shape[1]):
        ids = jnp.where(lane == block, rel_ref[0, block], ids)
    wanted_ref[:, 1, :] = ids


def list_peers(partner_ref, group_ref, list_ref, count_ref):
    peers = partner_ref.shape[1]
    me = group_ref[0]
    for part in range(4):
        count_ref[part] = 0

    def add(peer, carry):
        part = partner_ref[me, peer] ^ me
        at = count_ref[part]
        list_ref[part, at] = peer
        count_ref[part] = at + 1
        return carry

    lax.fori_loop(0, peers, add, 0)


def answer_body(partner_ref, group_ref, asked_ref, *refs):
    tables_in, (found_out, tables, found, sems, out_sem) = refs[:4], refs[4:]
    copies = [
        pltpu.make_async_copy(table, tables.at[part], sems.at[part])
        for part, table in enumerate(tables_in)
    ]
    for copy in copies:
        copy.start()
    peers, _, room = asked_ref.shape
    rows, width = tables.shape[1:]
    me = group_ref[0]
    for copy in copies:
        copy.wait()

    def answer(peer, carry):
        table = tables[partner_ref[me, peer] ^ me]
        got = dot(pick(asked_ref[pl.ds(peer, 1), 0, :], rows), table, 1, 0)
        found[pl.ds(peer, 1)] = got.astype(half).reshape(1, room, width)
        return carry

    lax.fori_loop(0, peers, answer, 0, unroll=4)
    back = pltpu.make_async_copy(found, found_out, out_sem)
    back.start()
    back.wait()


def operators_in(rel_ref, relation_ref, operator, sems):
    copies = [
        pltpu.make_async_copy(relation_ref.at[rel_ref[0, block]], operator.at[block], sems.at[block])
        for block in range(rel_ref.shape[1])
    ]
    for copy in copies:
        copy.start()
    return copies


def front_body(
    rel_ref,
    visit_ref,
    src_ref,
    neg_src_ref,
    neg_dst_ref,
    relation_ref,
    own_table,
    sibling_table,
    cross_table,
    cross_sibling_table,
    src_out,
    neg_src_out,
    lhs_out,
    terms_out,
    pull_out,
    stats_out,
    own,
    visit,
    neg_dst,
    operator,
    op_sems,
    own_sem,
    visit_sem,
):
    rows = own.shape[0]
    blocks, negs = neg_src_ref.shape
    edges = src_ref.shape[1]
    block_len = edges // blocks
    step = 256
    op_copies = operators_in(rel_ref, relation_ref, operator, op_sems)
    own_copy = pltpu.make_async_copy(own_table, own, own_sem)
    own_copy.start()
    for part, table in enumerate((own_table, sibling_table, cross_table, cross_sibling_table)):

        @pl.when(visit_ref[0] == part)
        def _(table=table):
            pltpu.make_async_copy(table, visit, visit_sem).start()

    own_copy.wait()
    pltpu.make_async_copy(own_table, visit, visit_sem).wait()
    for copy in op_copies:
        copy.wait()
    for block in range(blocks):
        for at in range(0, negs, step):
            to = block * negs + at
            neg_src_out[to : to + step] = dot(
                pick(neg_src_ref[block : block + 1, at : at + step], rows), own[...], 1, 0
            ).astype(half)
            neg_dst[at : at + step] = dot(
                pick(neg_dst_ref[block : block + 1, at : at + step], rows), visit[...], 1, 0
            ).astype(half)

        def chunk(t, carry, block=block):
            at = pl.multiple_of(block * block_len + t * step, step)
            here = pl.ds(at, step)
            op = operator[block].astype(half)
            src = dot(pick(src_ref[:, here], rows), own[...], 1, 0).astype(half)
            lhs = dot(src, op, 1, 0).astype(half)
            scores = dot(lhs, neg_dst[...], 1, 1)
            highest = jnp.max(scores, axis=1, keepdims=True)
            terms = jnp.exp(scores - highest)
            lane = lax.broadcasted_iota(jnp.int32, (step, 128), 1)
            stats_out[here, :] = jnp.where(lane < 64, highest, jnp.sum(terms, axis=1, keepdims=True))
            terms = terms.astype(half)
            src_out[here, :] = src
            lhs_out[here, :] = lhs
            terms_out[here, :] = terms
            pull_out[here, :] = dot(terms, neg_dst[...], 1, 0)
            return carry

        lax.fori_loop(0, block_len // step, chunk, 0, unroll=2)


def model_body(
    rel_ref,
    count_ref,
    slot_ref,
    fetched_ref,
    relation_ref,
    src_in,
    neg_src_in,
    lhs_in,
    terms_in,
    pull_in,
    stats_in,
    d_op_ref,
    d_dst_out,
    d_src_out,
    d_neg_src_out,
    d_neg_dst_out,
    src_ref,
    neg_src_ref,
    lhs_ref,
    terms_ref,
    pull_ref,
    stats_ref,
    d_src_ref,
    d_neg_src_ref,
    d_neg_dst_ref,
    dst_ref,
    d_dst,
    operator,
    neg_dst_sum,
    neg_src_sum,
    op_sum,
    op_turned_sum,
    op_sems,
    in_sems,
    out_sems,
):
    slots, width = fetched_ref.shape
    edges = slot_ref.shape[1]
    blocks = rel_ref.shape[1]
    block_len = edges // blocks
    negs = neg_src_ref.shape[0] // blocks
    peers = d_op_ref.shape[0]
    extra = width // peers
    step = 256
    copies = operators_in(rel_ref, relation_ref, operator, op_sems)
    pairs = (
        (src_in, src_ref),
        (neg_src_in, neg_src_ref),
        (lhs_in, lhs_ref),
        (pull_in, pull_ref),
        (stats_in, stats_ref),
        (terms_in, terms_ref),
    )
    for i, (there, here) in enumerate(pairs):
        copies.append(pltpu.make_async_copy(there, here, in_sems.at[i]))
        copies[-1].start()

    def fetch(t, carry):
        here = pl.ds(pl.multiple_of(t * step, step), step)
        dst_ref[here, :] = dot(pick(slot_ref[:, here], slots), fetched_ref[...], 1, 0).astype(half)
        return carry

    lax.fori_loop(0, edges // step, fetch, 0, unroll=4)
    for copy in copies:
        copy.wait()
    for block in range(blocks):
        neg_dst_sum[...] = jnp.zeros_like(neg_dst_sum)
        neg_src_sum[...] = jnp.zeros_like(neg_src_sum)
        op_sum[...] = jnp.zeros_like(op_sum)
        op_turned_sum[...] = jnp.zeros_like(op_turned_sum)

        def chunk(t, carry, block=block):
            at = pl.multiple_of(block * block_len + t * step, step)
            here = pl.ds(at, step)
            op = operator[block].astype(half)
            dst = dst_ref[here, :]
            src = src_ref[here, :]
            lhs = lhs_ref[here, :]
            neg_src = neg_src_ref[block * negs : (block + 1) * negs, :]
            line = lax.broadcasted_iota(jnp.int32, (step, 1), 0) + at
            live = jnp.where(line < count_ref[0, 0], 1.0, 0.0)
            rhs = dot(dst, op, 1, 1).astype(half)
            positive = jnp.sum(lhs.astype(full) * dst.astype(full), axis=1, keepdims=True)

            scores = dot(rhs, neg_src, 1, 1)
            highest = jnp.maximum(jnp.max(scores, axis=1, keepdims=True), positive)
            terms = jnp.exp(scores - highest)
            own = jnp.exp(positive - highest)
            scale = live / (own + jnp.sum(terms, axis=1, keepdims=True))
            src_terms = (terms * scale).astype(half)
            d_positive = own * scale - live

            top = stats_ref[here, :]
            top, total = top[:, :1], top[:, 64:65]
            highest = jnp.maximum(top, positive)
            lower = jnp.exp(top - highest)
            own = jnp.exp(positive - highest)
            scale = live / (own + total * lower)
            d_positive += own * scale - live
            scale = lower * scale

            d_lhs = (pull_ref[here, :] * scale).astype(half)
            d_lhs = d_lhs + (d_positive * dst.astype(full)).astype(half)
            d_rhs = dot(src_terms, neg_src, 1, 0).astype(half)
            scaled = (lhs.astype(full) * scale).astype(half)
            neg_dst_sum[...] += dot(scaled, terms_ref[here, :], 0, 0)
            neg_src_sum[...] += dot(rhs, src_terms, 0, 0)
            d_src_ref[here, :] = dot(d_lhs, op, 1, 1).astype(half)
            op_sum[...] += dot(src, d_lhs, 0, 0)
            op_turned_sum[...] += dot(d_rhs, dst, 0, 0)
            d_dst[here, :] = dot(d_rhs, op, 1, 0).astype(half) + (
                d_positive * lhs.astype(full)
            ).astype(half)
            return carry

        lax.fori_loop(0, block_len // step, chunk, 0, unroll=4)
        d_neg_dst_ref[block * negs : (block + 1) * negs, :] = neg_dst_sum[...].T.astype(half)
        d_neg_src_ref[block * negs : (block + 1) * negs, :] = neg_src_sum[...].T.astype(half)
        d_op = op_sum[...].astype(half) + op_turned_sum[...].astype(half)
        d_op_ref[:, block * extra : (block + 1) * extra, :] = d_op.reshape(peers, extra, width)
    backs = []
    for i, (here, there) in enumerate(
        (
            (d_dst, d_dst_out),
            (d_src_ref, d_src_out),
            (d_neg_src_ref, d_neg_src_out),
            (d_neg_dst_ref, d_neg_dst_out),
        )
    ):
        backs.append(pltpu.make_async_copy(here, there, out_sems.at[i]))
        backs[-1].start()

    for copy in backs:
        copy.wait()


def send_body(slot_ref, d_dst, outgoing_ref):
    peers, places, width = outgoing_ref.shape

    def send(t, carry):
        spot = place(slot_ref[...], t * 2 * places, 2 * places)
        out = dot(spot, d_dst[...], 1, 0).astype(half)
        outgoing_ref[pl.ds(2 * t, 2), :, :] = out.reshape(2, places, width)
        return carry

    lax.fori_loop(0, peers // 2, send, 0, unroll=4)


def front(rel_ids, visit_to, src_row, neg_src, neg_dst, relation, tables):
    rows, width = tables[0].shape
    edges = src_row.shape[1]
    blocks, negs = neg_src.shape
    sds = jax.ShapeDtypeStruct
    return call(
        front_body,
        (
            sds((edges, width), half),
            sds((blocks * negs, width), half),
            sds((edges, width), half),
            sds((edges, negs), half),
            sds((edges, width), full),
            sds((edges, 128), full),
        ),
        [
            pltpu.VMEM((rows, width), half),
            pltpu.VMEM((rows, width), half),
            pltpu.VMEM((negs, width), half),
            pltpu.VMEM((blocks, width, width), full),
            pltpu.SemaphoreType.DMA((blocks,)),
            pltpu.SemaphoreType.DMA,
            pltpu.SemaphoreType.DMA,
        ],
        [SMEM] * 2 + [VMEM] * 3 + [HBM] * 5,
        cost(2 * edges * width * (3 * rows + 2 * negs), 12 * MEBI),
    )(rel_ids, visit_to, src_row, neg_src, neg_dst, relation, *tables)


def model(rel_ids, edge_count, slot, fetched, relation, peers, rest):
    slots, width = fetched.shape
    edges = slot.shape[1]
    blocks = rel_ids.shape[1]
    negs = rest[1].shape[0] // blocks
    sds = jax.ShapeDtypeStruct
    return call(
        model_body,
        (
            sds((peers, blocks * (width // peers), width), half),
            sds((edges, width), half),
            sds((edges, width), half),
            sds((blocks * negs, width), half),
            sds((blocks * negs, width), half),
        ),
        [pltpu.VMEM(x.shape, x.dtype) for x in rest]
        + [
            pltpu.VMEM((edges, width), half),
            pltpu.VMEM((blocks * negs, width), half),
            pltpu.VMEM((blocks * negs, width), half),
            pltpu.VMEM((edges, width), half),
            pltpu.VMEM((edges, width), half),
            pltpu.VMEM((blocks, width, width), full),
            pltpu.VMEM((width, negs), full),
            pltpu.VMEM((width, negs), full),
            pltpu.VMEM((width, width), full),
            pltpu.VMEM((width, width), full),
            pltpu.SemaphoreType.DMA((blocks,)),
            pltpu.SemaphoreType.DMA((6,)),
            pltpu.SemaphoreType.DMA((4,)),
        ],
        [SMEM] * 2 + [VMEM] * 2 + [HBM] * 7,
        outs=[VMEM] + [HBM] * 4,
    )(rel_ids, edge_count, slot, fetched, relation, *rest)


def sums_body(src_ref, neg_src_ref, neg_dst_ref, d_src, d_neg_src, d_neg_dst, own_ref, visit_ref):
    rows = own_ref.shape[0]
    blocks, negs = neg_src_ref.shape
    step = 256

    def part(t, carry):
        first = pl.multiple_of(t * step, step)
        own = dot(place(src_ref[...], first, step), d_src[...], 1, 0)
        visit = jnp.zeros_like(own)
        for block in range(blocks):
            at = slice(block * negs, (block + 1) * negs)
            one = slice(block, block + 1)
            own += dot(place(neg_src_ref[one, :], first, step), d_neg_src[at, :], 1, 0)
            visit += dot(place(neg_dst_ref[one, :], first, step), d_neg_dst[at, :], 1, 0)
        own_ref[pl.ds(first, step), :] = own
        visit_ref[pl.ds(first, step), :] = visit
        return carry

    lax.fori_loop(0, rows // step, part, 0)


def home_body(
    parts, partner_ref, group_ref, visit_to_ref, asked_ref, returned_ref, visit_ref, *refs
):
    outs, (total, list_ref, count_ref) = refs[: len(parts)], refs[len(parts) :]
    rows, width = visit_ref.shape
    places = asked_ref.shape[2]
    together = 4
    list_peers(partner_ref, group_ref, list_ref, count_ref)
    for part, out_ref in zip(parts, outs):
        count = count_ref[part]
        total[...] = jnp.where(visit_to_ref[0] == part, visit_ref[...], 0.0)

        def add(t, carry, part=part, count=count):
            asks, backs = [], []
            for k in range(together):
                peer = list_ref[part, jnp.minimum(together * t + k, count - 1)]
                ask = asked_ref[pl.ds(peer, 1), 0, :]
                asks.append(jnp.where(together * t + k < count, ask, -1))
                backs.append(returned_ref[pl.ds(peer, 1), :places, :].reshape(places, width))
            ask = jnp.concatenate(asks, axis=1)
            back = jnp.concatenate(backs, axis=0)
            for first in range(0, rows, 512):
                total[first : first + 512] += dot(place(ask, first, 512), back, 1, 0)
            return carry

        lax.fori_loop(0, (count + together - 1) // together, add, 0)
        out_ref[...] = total[...].astype(half)


def operators_body(ids_ref, part_ref, out_ref):
    peers, _, width = part_ref.shape
    blocks = ids_ref.shape[1]
    rows = out_ref.shape[1]
    out_ref[...] = jnp.zeros_like(out_ref)

    def add(peer, carry):
        piece = part_ref[pl.ds(peer, 1)].reshape(blocks * rows, width).astype(full)
        for block in range(blocks):
            at = ids_ref[peer, block]
            out_ref[pl.ds(at, 1)] += piece[block * rows : (block + 1) * rows].reshape(1, rows, width)
        return carry

    lax.fori_loop(0, peers, add, 0)


def laid(column):
    return jnp.broadcast_to(column, (column.shape[0], 128)).T[:1, :]


def relation_body(part_ref, grad_ref, relation_ref, acc_ref, *refs):
    (new_ref, acc_new_ref, acc_turned, acc_found), before = refs[-4:], refs[:-4]
    step, rows, width = relation_ref.shape
    relations = acc_ref.shape[0]
    at = pl.program_id(0)
    first = part_ref[0] * (relations // 2) + at * step
    lane = lax.broadcasted_iota(jnp.int32, (rows, 128), 1)

    @pl.when(at == 0)
    def _():
        short = jnp.zeros((128 - relations, rows), full)
        acc_turned[...] = jnp.concatenate([acc_ref[...], short], axis=0).T
        if before:
            acc_found[...] = jnp.concatenate([before[1][...], short], axis=0).T
        else:
            acc_found[...] = jnp.zeros_like(acc_found)

    for k in range(step):
        here = lane == first + k
        grad = grad_ref[:, k].astype(full).reshape(rows, width)
        square = grad * grad
        parts = sum(square[:, at : at + 128] for at in range(0, width, 128))
        acc = jnp.sum(
            parts * (1.0 / width) + jnp.where(here, acc_turned[...], 0.0), axis=1, keepdims=True
        )
        acc_found[...] = jnp.where(here, acc, acc_found[...])
        new_ref[k] = relation_ref[k] - grad * (step_rate / jnp.sqrt(acc))

    @pl.when(at == pl.num_programs(0) - 1)
    def _():
        acc_new_ref[...] = acc_found[...].T[:relations]


def entity_body(grad_ref, home_ref, sibling_ref, cross_ref, entity_ref, acc_ref, new_ref, acc_new_ref):
    grad = (
        grad_ref[...]
        + home_ref[...].astype(full)
        + sibling_ref[...].astype(full)
        + cross_ref[...].astype(full)
    )
    square = jnp.mean(grad * grad, axis=1, keepdims=True)
    acc = acc_ref[...]
    acc_new_ref[...] = acc + laid(square)
    new_ref[0] = entity_ref[0] - grad * (step_rate / jnp.sqrt(turned(acc)[:, :1] + square))


def relation_update(part, grad, relation, relation_acc, before=()):
    peers, count, extra, width = grad.shape
    relations, rows = relation_acc.shape
    step = 10 if count % 10 == 0 else 1
    steps = count // step
    whole = pl.BlockSpec((relations, rows), lambda i, part: (0, 0))
    block = pl.BlockSpec((step, rows, width), lambda i, part: (part[0] * steps + i, 0, 0))
    return pl.pallas_call(
        relation_body,
        grid_spec=pltpu.PrefetchScalarGridSpec(
            num_scalar_prefetch=1,
            grid=(steps,),
            in_specs=[
                pl.BlockSpec((peers, step, extra, width), lambda i, part: (0, i, 0, 0)),
                block,
                whole,
            ]
            + [HBM, whole][: len(before)],
            out_specs=[block, whole],
            scratch_shapes=[pltpu.VMEM((rows, 128), full), pltpu.VMEM((rows, 128), full)],
        ),
        out_shape=[
            jax.ShapeDtypeStruct(relation.shape, full),
            jax.ShapeDtypeStruct(relation_acc.shape, full),
        ],
        input_output_aliases={4: 0} if before else {},
        compiler_params=pltpu.CompilerParams(vmem_limit_bytes=60 * MEBI),
        cost_estimate=cost(0, 24 * MEBI),
    )(part, grad, relation, relation_acc, *before)


def entity_update(grad, home, sibling, cross, entity, entity_acc):
    rows, width = grad.shape
    step = 256
    part = pl.BlockSpec((step, width), lambda i: (i, 0))
    block = pl.BlockSpec((1, step, width), lambda i: (0, i, 0))
    line = pl.BlockSpec((1, step), lambda i: (0, i))
    return pl.pallas_call(
        entity_body,
        grid=(rows // step,),
        in_specs=[part] * 4 + [block, line],
        out_specs=[block, line],
        out_shape=[
            jax.ShapeDtypeStruct(entity.shape, full),
            jax.ShapeDtypeStruct(entity_acc.shape, full),
        ],
        compiler_params=pltpu.CompilerParams(vmem_limit_bytes=60 * MEBI),
        cost_estimate=cost(0, 24 * MEBI),
    )(grad, home, sibling, cross, entity, entity_acc)


def on_device(
    entity,
    entity_acc,
    relation,
    relation_acc,
    partner,
    src_row,
    dst_owner,
    dst_row,
    rel_ids,
    neg_src,
    neg_dst,
    edge_count,
):
    me = lax.axis_index("grp")
    place_id = lax.axis_index("dev")
    peers = lax.axis_size("dev")
    rows, width = entity.shape[1:]
    edges = src_row.shape[1]
    blocks = rel_ids.shape[1]
    negs = neg_src.shape[2]
    relations = relation.shape[0]
    room = 2 * edges // peers
    extra = width // peers
    sds = jax.ShapeDtypeStruct

    def neighbour(x, flip):
        return lax.ppermute(x, "grp", [(g, g ^ flip) for g in range(4)])

    group = me.reshape(1)
    visit_to = (partner[me, place_id] ^ me).reshape(1)
    owners = dst_owner.reshape(1, edges)
    neg_src = neg_src.reshape(blocks, negs)
    neg_dst = neg_dst.reshape(blocks, negs)

    own = entity[0].astype(half)
    cross = neighbour(own, 2)
    sibling = neighbour(own, 1)
    slot, wanted = call(
        slots_body,
        (sds((1, edges), jnp.int32), sds((peers, 2, room), jnp.int32)),
        specs=[SMEM] + [VMEM] * 2,
    )(rel_ids, owners, dst_row)
    asked = lax.all_to_all(wanted, "dev", split_axis=0, concat_axis=0, tiled=True)
    cross, asked = lax.optimization_barrier((cross, asked))
    cross_sibling = neighbour(cross, 1)
    tables = (own, sibling, cross, cross_sibling)

    lists = [pltpu.SMEM((4, peers), jnp.int32), pltpu.SMEM((4,), jnp.int32)]
    found = call(
        answer_body,
        sds((peers, room, width), half),
        [
            pltpu.VMEM((4, rows, width), half),
            pltpu.VMEM((peers, room, width), half),
            pltpu.SemaphoreType.DMA((4,)),
            pltpu.SemaphoreType.DMA,
        ],
        [SMEM] * 2 + [VMEM] + [HBM] * 4,
        outs=HBM,
    )(partner, group, asked, *tables)
    fetched = lax.all_to_all(found, "dev", split_axis=0, concat_axis=0, tiled=True)

    rest = front(rel_ids, visit_to, src_row, neg_src, neg_dst, relation, tables)
    d_op, d_dst, d_src, d_neg_src, d_neg_dst = model(
        rel_ids, edge_count, slot, fetched.reshape(peers * room, width), relation, peers, rest
    )
    d_op_here = lax.all_to_all(d_op, "dev", split_axis=0, concat_axis=0, tiled=True)
    outgoing = call(
        send_body,
        sds((peers, room, width), half),
        (),
        [VMEM] * 2,
        cost(2 * peers * room * edges * width, 4 * MEBI),
    )(slot, d_dst)
    d_op_here, outgoing, d_src, d_neg_src, d_neg_dst = lax.optimization_barrier(
        (d_op_here, outgoing, d_src, d_neg_src, d_neg_dst)
    )
    returned = lax.all_to_all(outgoing, "dev", split_axis=0, concat_axis=0, tiled=True)

    own_grad, visit_grad = call(
        sums_body,
        (sds((rows, width), full), sds((rows, width), full)),
        (),
        [VMEM] * 6,
        cost(2 * 3 * edges * rows * width, 7 * rows * width * 2),
    )(src_row, neg_src, neg_dst, d_src, d_neg_src, d_neg_dst)

    rel_part = call(operators_body, sds((relations, extra, width), full), (), [SMEM, VMEM])(
        asked[:, 1, :blocks], d_op_here
    )
    core = me & 1
    halves = rel_part.reshape(2, relations // 2, extra, width)
    mine = lax.dynamic_index_in_dim(halves, core, 0, keepdims=False)
    other = lax.dynamic_index_in_dim(halves, 1 - core, 0, keepdims=False)
    chip = mine + neighbour(other, 1)
    chip_other, own_grad, visit_grad = lax.optimization_barrier(
        (neighbour(chip, 2), own_grad, visit_grad)
    )
    pair = (chip + chip_other).astype(half)
    near = lax.ppermute(pair, "dev", [(d, d ^ 1) for d in range(peers)])
    low = (place_id & 1) == 0
    planes = jnp.stack([jnp.where(low, pair, near), jnp.where(low, near, pair)])
    returned, planes = lax.optimization_barrier((returned, planes))

    def home(parts, returned):
        return call(
            functools.partial(home_body, parts),
            tuple(sds((rows, width), half) for _ in parts),
            [pltpu.VMEM((rows, width), full)] + lists,
            [SMEM] * 3 + [VMEM] * 3,
            cost(0, 24 * MEBI),
        )(partner, group, visit_to, asked, returned, visit_grad)

    home_cross_sibling, home_cross, home_sibling = home((3, 2, 1), returned)
    chip_cross = (home_cross.astype(full) + neighbour(home_cross_sibling, 1).astype(full)).astype(half)
    from_sibling = neighbour(home_sibling, 1)
    from_cross = neighbour(chip_cross, 2)
    gathered = lax.all_to_all(
        jnp.broadcast_to(planes[None], (peers // 2,) + planes.shape),
        "dev",
        split_axis=0,
        concat_axis=0,
        axis_index_groups=[list(range(k, peers, 2)) for k in range(2)],
        tiled=True,
    ).reshape((peers,) + pair.shape)

    (home_own,) = home((0,), returned)
    entity_new, acc_new = entity_update(
        own_grad, home_own, from_sibling, from_cross, entity, entity_acc
    )
    gathered, entity_new, acc_new = lax.optimization_barrier((gathered, entity_new, acc_new))
    other_half = neighbour(gathered, 1)
    before = relation_update(core.reshape(1), gathered, relation, relation_acc)
    relation_new, relation_acc_new = relation_update(
        (1 - core).reshape(1), other_half, relation, relation_acc, before
    )
    return (entity_new, acc_new, relation_new, relation_acc_new)


def solution(mesh):
    return jax.shard_map(
        on_device,
        mesh=mesh,
        in_specs=(
            P("grp", "dev", None),
            P("grp", "dev"),
            P(),
            P(),
            P(),
            P("grp", "dev"),
            P("grp", "dev", None),
            P("grp", "dev"),
            P("grp", "dev"),
            P("grp", "dev", None),
            P("grp", "dev", None),
            P("grp", "dev"),
        ),
        out_specs=(P("grp", "dev", None), P("grp", "dev"), P(), P()),
        check_vma=False,
    )
```

```python
import functools

import jax
import jax.numpy as jnp
from jax import lax
from jax.experimental import pallas as pl
from jax.experimental.pallas import tpu as pltpu
from jax.sharding import PartitionSpec as P

step_rate = 0.1
MEBI = 1024 * 1024
half = jnp.bfloat16
full = jnp.float32
VMEM = pl.BlockSpec(memory_space=pltpu.VMEM)
SMEM = pl.BlockSpec(memory_space=pltpu.SMEM)
HBM = pl.BlockSpec(memory_space=pltpu.HBM)


def dot(a, b, ca, cb):
    return lax.dot_general(a, b, (((ca,), (cb,)), ((), ())), preferred_element_type=full)


def turned(row):
    pieces = [
        jnp.broadcast_to(row[:, at : at + 128], (128, 128)).T for at in range(0, row.shape[1], 128)
    ]
    return pieces[0] if len(pieces) == 1 else jnp.concatenate(pieces, axis=0)


def pick(row, width):
    spread = turned(row.astype(full))
    lane = lax.broadcasted_iota(jnp.int32, (1, 128), 1).astype(full)
    pieces = [
        jnp.where(spread == lane + float(at), 1.0, 0.0).astype(half) for at in range(0, width, 128)
    ]
    return jnp.concatenate(pieces, axis=1)


def place(row, first, height):
    line = lax.broadcasted_iota(jnp.int32, (height, 1), 0) + first
    return jnp.where(row == line, 1.0, 0.0).astype(half)


def call(body, shapes, scratch=(), specs=None, cost=None, outs=None, mebi=60, **kw):
    return pl.pallas_call(
        body,
        out_shape=shapes,
        in_specs=specs,
        out_specs=outs or jax.tree.map(lambda _: VMEM, shapes),
        scratch_shapes=list(scratch),
        compiler_params=pltpu.CompilerParams(vmem_limit_bytes=mebi * MEBI),
        cost_estimate=cost,
        **kw,
    )


def cost(flops, moved):
    return pl.CostEstimate(flops=int(flops), bytes_accessed=int(moved), transcendentals=0)


def slots_body(rel_ref, owner_ref, row_ref, slot_ref, wanted_ref):
    peers, _, room = wanted_ref.shape
    edges = owner_ref.shape[1]
    step = 256
    before = lax.broadcasted_iota(jnp.int32, (step, step), 0)
    after = lax.broadcasted_iota(jnp.int32, (step, step), 1)
    upper = jnp.where(before <= after, 1.0, 0.0).astype(half)
    peer = lax.broadcasted_iota(jnp.int32, (peers, step), 0)
    carry = jnp.zeros((peers, 1), full)
    high = jnp.zeros((peers, room), full)
    low = jnp.zeros((peers, room), full)
    for at in range(0, edges, step):
        owner = owner_ref[:, at : at + step]
        hit = jnp.where(peer == owner, 1.0, 0.0)
        count = dot(hit.astype(half), upper, 1, 0) + carry
        carry = count[:, step - 1 :]
        order = (jnp.sum(count * hit, axis=0, keepdims=True) - 1.0).astype(jnp.int32)
        slot_ref[:, at : at + step] = owner * room + order
        spot = place(order, 0, room)
        row = row_ref[:, at : at + step]
        top = lax.shift_right_logical(row, 4)
        high += dot((hit * top.astype(full)).astype(half), spot, 1, 1)
        low += dot((hit * (row - top * 16).astype(full)).astype(half), spot, 1, 1)
    wanted_ref[:, 0, :] = (high * 16.0 + low).astype(jnp.int32)
    lane = lax.broadcasted_iota(jnp.int32, (peers, room), 1)
    ids = jnp.zeros((peers, room), jnp.int32)
    for block in range(rel_ref.shape[1]):
        ids = jnp.where(lane == block, rel_ref[0, block], ids)
    wanted_ref[:, 1, :] = ids


def list_peers(partner_ref, group_ref, list_ref, count_ref):
    peers = partner_ref.shape[1]
    me = group_ref[0]
    for part in range(4):
        count_ref[part] = 0

    def add(peer, carry):
        part = partner_ref[me, peer] ^ me
        at = count_ref[part]
        list_ref[part, at] = peer
        count_ref[part] = at + 1
        return carry

    lax.fori_loop(0, peers, add, 0)


def answer_body(partner_ref, group_ref, asked_ref, *refs):
    tables_in, (found_out, tables, found, sems, out_sem) = refs[:4], refs[4:]
    copies = [
        pltpu.make_async_copy(table, tables.at[part], sems.at[part])
        for part, table in enumerate(tables_in)
    ]
    for copy in copies:
        copy.start()
    peers, _, room = asked_ref.shape
    rows, width = tables.shape[1:]
    me = group_ref[0]
    for copy in copies:
        copy.wait()

    def answer(peer, carry):
        table = tables[partner_ref[me, peer] ^ me]
        got = dot(pick(asked_ref[pl.ds(peer, 1), 0, :], rows), table, 1, 0)
        found[pl.ds(peer, 1)] = got.astype(half).reshape(1, room, width)
        return carry

    lax.fori_loop(0, peers, answer, 0, unroll=4)
    back = pltpu.make_async_copy(found, found_out, out_sem)
    back.start()
    back.wait()


def operators_in(rel_ref, relation_ref, operator, sems):
    copies = [
        pltpu.make_async_copy(relation_ref.at[rel_ref[0, block]], operator.at[block], sems.at[block])
        for block in range(rel_ref.shape[1])
    ]
    for copy in copies:
        copy.start()
    return copies


def front_body(
    rel_ref,
    visit_ref,
    src_ref,
    neg_src_ref,
    neg_dst_ref,
    relation_ref,
    own_table,
    sibling_table,
    cross_table,
    cross_sibling_table,
    src_out,
    neg_src_out,
    lhs_out,
    terms_out,
    pull_out,
    stats_out,
    own,
    visit,
    neg_dst,
    operator,
    op_sems,
    own_sem,
    visit_sem,
):
    rows = own.shape[0]
    blocks, negs = neg_src_ref.shape
    edges = src_ref.shape[1]
    block_len = edges // blocks
    step = 256
    op_copies = operators_in(rel_ref, relation_ref, operator, op_sems)
    own_copy = pltpu.make_async_copy(own_table, own, own_sem)
    own_copy.start()
    for part, table in enumerate((own_table, sibling_table, cross_table, cross_sibling_table)):

        @pl.when(visit_ref[0] == part)
        def _(table=table):
            pltpu.make_async_copy(table, visit, visit_sem).start()

    own_copy.wait()
    pltpu.make_async_copy(own_table, visit, visit_sem).wait()
    for copy in op_copies:
        copy.wait()
    for block in range(blocks):
        for at in range(0, negs, step):
            to = block * negs + at
            neg_src_out[to : to + step] = dot(
                pick(neg_src_ref[block : block + 1, at : at + step], rows), own[...], 1, 0
            ).astype(half)
            neg_dst[at : at + step] = dot(
                pick(neg_dst_ref[block : block + 1, at : at + step], rows), visit[...], 1, 0
            ).astype(half)

        def chunk(t, carry, block=block):
            at = pl.multiple_of(block * block_len + t * step, step)
            here = pl.ds(at, step)
            op = operator[block].astype(half)
            src = dot(pick(src_ref[:, here], rows), own[...], 1, 0).astype(half)
            lhs = dot(src, op, 1, 0).astype(half)
            scores = dot(lhs, neg_dst[...], 1, 1)
            highest = jnp.max(scores, axis=1, keepdims=True)
            terms = jnp.exp(scores - highest)
            lane = lax.broadcasted_iota(jnp.int32, (step, 128), 1)
            stats_out[here, :] = jnp.where(lane < 64, highest, jnp.sum(terms, axis=1, keepdims=True))
            terms = terms.astype(half)
            src_out[here, :] = src
            lhs_out[here, :] = lhs
            terms_out[here, :] = terms
            pull_out[here, :] = dot(terms, neg_dst[...], 1, 0)
            return carry

        lax.fori_loop(0, block_len // step, chunk, 0, unroll=2)


def model_body(
    rel_ref,
    count_ref,
    slot_ref,
    fetched_ref,
    relation_ref,
    src_in,
    neg_src_in,
    lhs_in,
    terms_in,
    pull_in,
    stats_in,
    d_op_ref,
    d_dst_out,
    d_src_out,
    d_neg_src_out,
    d_neg_dst_out,
    src_ref,
    neg_src_ref,
    lhs_ref,
    terms_ref,
    pull_ref,
    stats_ref,
    d_src_ref,
    d_neg_src_ref,
    d_neg_dst_ref,
    dst_ref,
    d_dst,
    operator,
    neg_dst_sum,
    neg_src_sum,
    op_sum,
    op_turned_sum,
    op_sems,
    in_sems,
    out_sems,
):
    slots, width = fetched_ref.shape
    edges = slot_ref.shape[1]
    blocks = rel_ref.shape[1]
    block_len = edges // blocks
    negs = neg_src_ref.shape[0] // blocks
    peers = d_op_ref.shape[0]
    extra = width // peers
    step = 256
    copies = operators_in(rel_ref, relation_ref, operator, op_sems)
    pairs = (
        (src_in, src_ref),
        (neg_src_in, neg_src_ref),
        (lhs_in, lhs_ref),
        (pull_in, pull_ref),
        (stats_in, stats_ref),
        (terms_in, terms_ref),
    )
    for i, (there, here) in enumerate(pairs):
        copies.append(pltpu.make_async_copy(there, here, in_sems.at[i]))
        copies[-1].start()

    def fetch(t, carry):
        here = pl.ds(pl.multiple_of(t * step, step), step)
        dst_ref[here, :] = dot(pick(slot_ref[:, here], slots), fetched_ref[...], 1, 0).astype(half)
        return carry

    lax.fori_loop(0, edges // step, fetch, 0, unroll=4)
    for copy in copies:
        copy.wait()
    for block in range(blocks):
        neg_dst_sum[...] = jnp.zeros_like(neg_dst_sum)
        neg_src_sum[...] = jnp.zeros_like(neg_src_sum)
        op_sum[...] = jnp.zeros_like(op_sum)
        op_turned_sum[...] = jnp.zeros_like(op_turned_sum)

        def chunk(t, carry, block=block):
            at = pl.multiple_of(block * block_len + t * step, step)
            here = pl.ds(at, step)
            op = operator[block].astype(half)
            dst = dst_ref[here, :]
            src = src_ref[here, :]
            lhs = lhs_ref[here, :]
            neg_src = neg_src_ref[block * negs : (block + 1) * negs, :]
            line = lax.broadcasted_iota(jnp.int32, (step, 1), 0) + at
            live = jnp.where(line < count_ref[0, 0], 1.0, 0.0)
            rhs = dot(dst, op, 1, 1).astype(half)
            positive = jnp.sum(lhs.astype(full) * dst.astype(full), axis=1, keepdims=True)

            scores = dot(rhs, neg_src, 1, 1)
            highest = jnp.maximum(jnp.max(scores, axis=1, keepdims=True), positive)
            terms = jnp.exp(scores - highest)
            own = jnp.exp(positive - highest)
            scale = live / (own + jnp.sum(terms, axis=1, keepdims=True))
            src_terms = (terms * scale).astype(half)
            d_positive = own * scale - live

            top = stats_ref[here, :]
            top, total = top[:, :1], top[:, 64:65]
            highest = jnp.maximum(top, positive)
            lower = jnp.exp(top - highest)
            own = jnp.exp(positive - highest)
            scale = live / (own + total * lower)
            d_positive += own * scale - live
            scale = lower * scale

            d_lhs = (pull_ref[here, :] * scale).astype(half)
            d_lhs = d_lhs + (d_positive * dst.astype(full)).astype(half)
            d_rhs = dot(src_terms, neg_src, 1, 0).astype(half)
            scaled = (lhs.astype(full) * scale).astype(half)
            neg_dst_sum[...] += dot(scaled, terms_ref[here, :], 0, 0)
            neg_src_sum[...] += dot(rhs, src_terms, 0, 0)
            d_src_ref[here, :] = dot(d_lhs, op, 1, 1).astype(half)
            op_sum[...] += dot(src, d_lhs, 0, 0)
            op_turned_sum[...] += dot(d_rhs, dst, 0, 0)
            d_dst[here, :] = dot(d_rhs, op, 1, 0).astype(half) + (
                d_positive * lhs.astype(full)
            ).astype(half)
            return carry

        lax.fori_loop(0, block_len // step, chunk, 0, unroll=4)
        d_neg_dst_ref[block * negs : (block + 1) * negs, :] = neg_dst_sum[...].T.astype(half)
        d_neg_src_ref[block * negs : (block + 1) * negs, :] = neg_src_sum[...].T.astype(half)
        d_op = op_sum[...].astype(half) + op_turned_sum[...].astype(half)
        d_op_ref[:, block * extra : (block + 1) * extra, :] = d_op.reshape(peers, extra, width)
    backs = []
    for i, (here, there) in enumerate(
        (
            (d_dst, d_dst_out),
            (d_src_ref, d_src_out),
            (d_neg_src_ref, d_neg_src_out),
            (d_neg_dst_ref, d_neg_dst_out),
        )
    ):
        backs.append(pltpu.make_async_copy(here, there, out_sems.at[i]))
        backs[-1].start()

    for copy in backs:
        copy.wait()


def send_body(slot_ref, d_dst, outgoing_ref):
    peers, places, width = outgoing_ref.shape

    def send(t, carry):
        spot = place(slot_ref[...], t * 2 * places, 2 * places)
        out = dot(spot, d_dst[...], 1, 0).astype(half)
        outgoing_ref[pl.ds(2 * t, 2), :, :] = out.reshape(2, places, width)
        return carry

    lax.fori_loop(0, peers // 2, send, 0, unroll=4)


def front(rel_ids, visit_to, src_row, neg_src, neg_dst, relation, tables):
    rows, width = tables[0].shape
    edges = src_row.shape[1]
    blocks, negs = neg_src.shape
    sds = jax.ShapeDtypeStruct
    return call(
        front_body,
        (
            sds((edges, width), half),
            sds((blocks * negs, width), half),
            sds((edges, width), half),
            sds((edges, negs), half),
            sds((edges, width), full),
            sds((edges, 128), full),
        ),
        [
            pltpu.VMEM((rows, width), half),
            pltpu.VMEM((rows, width), half),
            pltpu.VMEM((negs, width), half),
            pltpu.VMEM((blocks, width, width), full),
            pltpu.SemaphoreType.DMA((blocks,)),
            pltpu.SemaphoreType.DMA,
            pltpu.SemaphoreType.DMA,
        ],
        [SMEM] * 2 + [VMEM] * 3 + [HBM] * 5,
        cost(2 * edges * width * (3 * rows + 2 * negs), 12 * MEBI),
    )(rel_ids, visit_to, src_row, neg_src, neg_dst, relation, *tables)


def model(rel_ids, edge_count, slot, fetched, relation, peers, rest):
    slots, width = fetched.shape
    edges = slot.shape[1]
    blocks = rel_ids.shape[1]
    negs = rest[1].shape[0] // blocks
    sds = jax.ShapeDtypeStruct
    return call(
        model_body,
        (
            sds((peers, blocks * (width // peers), width), half),
            sds((edges, width), half),
            sds((edges, width), half),
            sds((blocks * negs, width), half),
            sds((blocks * negs, width), half),
        ),
        [pltpu.VMEM(x.shape, x.dtype) for x in rest]
        + [
            pltpu.VMEM((edges, width), half),
            pltpu.VMEM((blocks * negs, width), half),
            pltpu.VMEM((blocks * negs, width), half),
            pltpu.VMEM((edges, width), half),
            pltpu.VMEM((edges, width), half),
            pltpu.VMEM((blocks, width, width), full),
            pltpu.VMEM((width, negs), full),
            pltpu.VMEM((width, negs), full),
            pltpu.VMEM((width, width), full),
            pltpu.VMEM((width, width), full),
            pltpu.SemaphoreType.DMA((blocks,)),
            pltpu.SemaphoreType.DMA((6,)),
            pltpu.SemaphoreType.DMA((4,)),
        ],
        [SMEM] * 2 + [VMEM] * 2 + [HBM] * 7,
        outs=[VMEM] + [HBM] * 4,
    )(rel_ids, edge_count, slot, fetched, relation, *rest)


def sums_body(src_ref, neg_src_ref, neg_dst_ref, d_src, d_neg_src, d_neg_dst, own_ref, visit_ref):
    rows = own_ref.shape[0]
    blocks, negs = neg_src_ref.shape
    step = 256

    def part(t, carry):
        first = pl.multiple_of(t * step, step)
        own = dot(place(src_ref[...], first, step), d_src[...], 1, 0)
        visit = jnp.zeros_like(own)
        for block in range(blocks):
            at = slice(block * negs, (block + 1) * negs)
            one = slice(block, block + 1)
            own += dot(place(neg_src_ref[one, :], first, step), d_neg_src[at, :], 1, 0)
            visit += dot(place(neg_dst_ref[one, :], first, step), d_neg_dst[at, :], 1, 0)
        own_ref[pl.ds(first, step), :] = own
        visit_ref[pl.ds(first, step), :] = visit
        return carry

    lax.fori_loop(0, rows // step, part, 0)


def home_body(
    parts, partner_ref, group_ref, visit_to_ref, asked_ref, returned_ref, visit_ref, *refs
):
    outs, (total, list_ref, count_ref) = refs[: len(parts)], refs[len(parts) :]
    rows, width = visit_ref.shape
    places = asked_ref.shape[2]
    together = 4
    list_peers(partner_ref, group_ref, list_ref, count_ref)
    for part, out_ref in zip(parts, outs):
        count = count_ref[part]
        total[...] = jnp.where(visit_to_ref[0] == part, visit_ref[...], 0.0)

        def add(t, carry, part=part, count=count):
            asks, backs = [], []
            for k in range(together):
                peer = list_ref[part, jnp.minimum(together * t + k, count - 1)]
                ask = asked_ref[pl.ds(peer, 1), 0, :]
                asks.append(jnp.where(together * t + k < count, ask, -1))
                backs.append(returned_ref[pl.ds(peer, 1), :places, :].reshape(places, width))
            ask = jnp.concatenate(asks, axis=1)
            back = jnp.concatenate(backs, axis=0)
            for first in range(0, rows, 512):
                total[first : first + 512] += dot(place(ask, first, 512), back, 1, 0)
            return carry

        lax.fori_loop(0, (count + together - 1) // together, add, 0)
        out_ref[...] = total[...].astype(half)


def operators_body(ids_ref, part_ref, out_ref):
    peers, _, width = part_ref.shape
    blocks = ids_ref.shape[1]
    rows = out_ref.shape[1]
    out_ref[...] = jnp.zeros_like(out_ref)

    def add(peer, carry):
        piece = part_ref[pl.ds(peer, 1)].reshape(blocks * rows, width).astype(full)
        for block in range(blocks):
            at = ids_ref[peer, block]
            out_ref[pl.ds(at, 1)] += piece[block * rows : (block + 1) * rows].reshape(1, rows, width)
        return carry

    lax.fori_loop(0, peers, add, 0)


def laid(column):
    return jnp.broadcast_to(column, (column.shape[0], 128)).T[:1, :]


def relation_body(part_ref, grad_ref, relation_ref, acc_ref, *refs):
    (new_ref, acc_new_ref, acc_turned, acc_found), before = refs[-4:], refs[:-4]
    step, rows, width = relation_ref.shape
    relations = acc_ref.shape[0]
    at = pl.program_id(0)
    first = part_ref[0] * (relations // 2) + at * step
    lane = lax.broadcasted_iota(jnp.int32, (rows, 128), 1)

    @pl.when(at == 0)
    def _():
        short = jnp.zeros((128 - relations, rows), full)
        acc_turned[...] = jnp.concatenate([acc_ref[...], short], axis=0).T
        if before:
            acc_found[...] = jnp.concatenate([before[1][...], short], axis=0).T
        else:
            acc_found[...] = jnp.zeros_like(acc_found)

    for k in range(step):
        here = lane == first + k
        grad = grad_ref[:, k].astype(full).reshape(rows, width)
        square = grad * grad
        parts = sum(square[:, at : at + 128] for at in range(0, width, 128))
        acc = jnp.sum(
            parts * (1.0 / width) + jnp.where(here, acc_turned[...], 0.0), axis=1, keepdims=True
        )
        acc_found[...] = jnp.where(here, acc, acc_found[...])
        new_ref[k] = relation_ref[k] - grad * (step_rate / jnp.sqrt(acc))

    @pl.when(at == pl.num_programs(0) - 1)
    def _():
        acc_new_ref[...] = acc_found[...].T[:relations]


def entity_body(grad_ref, home_ref, sibling_ref, cross_ref, entity_ref, acc_ref, new_ref, acc_new_ref):
    grad = (
        grad_ref[...]
        + home_ref[...].astype(full)
        + sibling_ref[...].astype(full)
        + cross_ref[...].astype(full)
    )
    square = jnp.mean(grad * grad, axis=1, keepdims=True)
    acc = acc_ref[...]
    acc_new_ref[...] = acc + laid(square)
    new_ref[0] = entity_ref[0] - grad * (step_rate / jnp.sqrt(turned(acc)[:, :1] + square))


def relation_update(part, grad, relation, relation_acc, before=()):
    peers, count, extra, width = grad.shape
    relations, rows = relation_acc.shape
    step = 10 if count % 10 == 0 else 1
    steps = count // step
    whole = pl.BlockSpec((relations, rows), lambda i, part: (0, 0))
    block = pl.BlockSpec((step, rows, width), lambda i, part: (part[0] * steps + i, 0, 0))
    return pl.pallas_call(
        relation_body,
        grid_spec=pltpu.PrefetchScalarGridSpec(
            num_scalar_prefetch=1,
            grid=(steps,),
            in_specs=[
                pl.BlockSpec((peers, step, extra, width), lambda i, part: (0, i, 0, 0)),
                block,
                whole,
            ]
            + [HBM, whole][: len(before)],
            out_specs=[block, whole],
            scratch_shapes=[pltpu.VMEM((rows, 128), full), pltpu.VMEM((rows, 128), full)],
        ),
        out_shape=[
            jax.ShapeDtypeStruct(relation.shape, full),
            jax.ShapeDtypeStruct(relation_acc.shape, full),
        ],
        input_output_aliases={4: 0} if before else {},
        compiler_params=pltpu.CompilerParams(vmem_limit_bytes=60 * MEBI),
        cost_estimate=cost(0, 24 * MEBI),
    )(part, grad, relation, relation_acc, *before)


def entity_update(grad, home, sibling, cross, entity, entity_acc):
    rows, width = grad.shape
    step = 1024 if rows % 1024 == 0 else 256
    part = pl.BlockSpec((step, width), lambda i: (i, 0))
    block = pl.BlockSpec((1, step, width), lambda i: (0, i, 0))
    line = pl.BlockSpec((1, step), lambda i: (0, i))
    return pl.pallas_call(
        entity_body,
        grid=(rows // step,),
        in_specs=[part] * 4 + [block, line],
        out_specs=[block, line],
        out_shape=[
            jax.ShapeDtypeStruct(entity.shape, full),
            jax.ShapeDtypeStruct(entity_acc.shape, full),
        ],
        compiler_params=pltpu.CompilerParams(vmem_limit_bytes=60 * MEBI),
        cost_estimate=cost(0, 24 * MEBI),
    )(grad, home, sibling, cross, entity, entity_acc)


def on_device(
    entity,
    entity_acc,
    relation,
    relation_acc,
    partner,
    src_row,
    dst_owner,
    dst_row,
    rel_ids,
    neg_src,
    neg_dst,
    edge_count,
):
    me = lax.axis_index("grp")
    place_id = lax.axis_index("dev")
    peers = lax.axis_size("dev")
    rows, width = entity.shape[1:]
    edges = src_row.shape[1]
    blocks = rel_ids.shape[1]
    negs = neg_src.shape[2]
    relations = relation.shape[0]
    room = 2 * edges // peers
    extra = width // peers
    sds = jax.ShapeDtypeStruct

    def neighbour(x, flip):
        return lax.ppermute(x, "grp", [(g, g ^ flip) for g in range(4)])

    group = me.reshape(1)
    visit_to = (partner[me, place_id] ^ me).reshape(1)
    owners = dst_owner.reshape(1, edges)
    neg_src = neg_src.reshape(blocks, negs)
    neg_dst = neg_dst.reshape(blocks, negs)

    own = entity[0].astype(half)
    cross = neighbour(own, 2)
    sibling = neighbour(own, 1)
    slot, wanted = call(
        slots_body,
        (sds((1, edges), jnp.int32), sds((peers, 2, room), jnp.int32)),
        specs=[SMEM] + [VMEM] * 2,
    )(rel_ids, owners, dst_row)
    asked = lax.all_to_all(wanted, "dev", split_axis=0, concat_axis=0, tiled=True)
    cross, asked = lax.optimization_barrier((cross, asked))
    cross_sibling = neighbour(cross, 1)
    tables = (own, sibling, cross, cross_sibling)

    lists = [pltpu.SMEM((4, peers), jnp.int32), pltpu.SMEM((4,), jnp.int32)]
    found = call(
        answer_body,
        sds((peers, room, width), half),
        [
            pltpu.VMEM((4, rows, width), half),
            pltpu.VMEM((peers, room, width), half),
            pltpu.SemaphoreType.DMA((4,)),
            pltpu.SemaphoreType.DMA,
        ],
        [SMEM] * 2 + [VMEM] + [HBM] * 4,
        outs=HBM,
    )(partner, group, asked, *tables)
    fetched = lax.all_to_all(found, "dev", split_axis=0, concat_axis=0, tiled=True)

    rest = front(rel_ids, visit_to, src_row, neg_src, neg_dst, relation, tables)
    d_op, d_dst, d_src, d_neg_src, d_neg_dst = model(
        rel_ids, edge_count, slot, fetched.reshape(peers * room, width), relation, peers, rest
    )
    d_op_here = lax.all_to_all(d_op, "dev", split_axis=0, concat_axis=0, tiled=True)
    outgoing = call(
        send_body,
        sds((peers, room, width), half),
        (),
        [VMEM] * 2,
        cost(2 * peers * room * edges * width, 4 * MEBI),
    )(slot, d_dst)
    d_op_here, outgoing, d_src, d_neg_src, d_neg_dst = lax.optimization_barrier(
        (d_op_here, outgoing, d_src, d_neg_src, d_neg_dst)
    )
    returned = lax.all_to_all(outgoing, "dev", split_axis=0, concat_axis=0, tiled=True)

    own_grad, visit_grad = call(
        sums_body,
        (sds((rows, width), full), sds((rows, width), full)),
        (),
        [VMEM] * 6,
        cost(2 * 3 * edges * rows * width, 7 * rows * width * 2),
    )(src_row, neg_src, neg_dst, d_src, d_neg_src, d_neg_dst)

    rel_part = call(operators_body, sds((relations, extra, width), full), (), [SMEM, VMEM])(
        asked[:, 1, :blocks], d_op_here
    )
    core = me & 1
    halves = rel_part.reshape(2, relations // 2, extra, width)
    mine = lax.dynamic_index_in_dim(halves, core, 0, keepdims=False)
    other = lax.dynamic_index_in_dim(halves, 1 - core, 0, keepdims=False)
    chip = mine + neighbour(other, 1)
    chip_other, own_grad, visit_grad = lax.optimization_barrier(
        (neighbour(chip, 2), own_grad, visit_grad)
    )
    pair = (chip + chip_other).astype(half)
    near = lax.ppermute(pair, "dev", [(d, d ^ 1) for d in range(peers)])
    low = (place_id & 1) == 0
    planes = jnp.stack([jnp.where(low, pair, near), jnp.where(low, near, pair)])
    returned, planes = lax.optimization_barrier((returned, planes))

    def home(parts, returned):
        return call(
            functools.partial(home_body, parts),
            tuple(sds((rows, width), half) for _ in parts),
            [pltpu.VMEM((rows, width), full)] + lists,
            [SMEM] * 3 + [VMEM] * 3,
            cost(0, 24 * MEBI),
        )(partner, group, visit_to, asked, returned, visit_grad)

    home_cross_sibling, home_cross, home_sibling = home((3, 2, 1), returned)
    chip_cross = (home_cross.astype(full) + neighbour(home_cross_sibling, 1).astype(full)).astype(half)
    from_sibling = neighbour(home_sibling, 1)
    from_cross = neighbour(chip_cross, 2)
    gathered = lax.all_to_all(
        jnp.broadcast_to(planes[None], (peers // 2,) + planes.shape),
        "dev",
        split_axis=0,
        concat_axis=0,
        axis_index_groups=[list(range(k, peers, 2)) for k in range(2)],
        tiled=True,
    ).reshape((peers,) + pair.shape)

    (home_own,) = home((0,), returned)
    entity_new, acc_new = entity_update(
        own_grad, home_own, from_sibling, from_cross, entity, entity_acc
    )
    gathered, entity_new, acc_new = lax.optimization_barrier((gathered, entity_new, acc_new))
    other_half = neighbour(gathered, 1)
    before = relation_update(core.reshape(1), gathered, relation, relation_acc)
    relation_new, relation_acc_new = relation_update(
        (1 - core).reshape(1), other_half, relation, relation_acc, before
    )
    return (entity_new, acc_new, relation_new, relation_acc_new)


def solution(mesh):
    return jax.shard_map(
        on_device,
        mesh=mesh,
        in_specs=(
            P("grp", "dev", None),
            P("grp", "dev"),
            P(),
            P(),
            P(),
            P("grp", "dev"),
            P("grp", "dev", None),
            P("grp", "dev"),
            P("grp", "dev"),
            P("grp", "dev", None),
            P("grp", "dev", None),
            P("grp", "dev"),
        ),
        out_specs=(P("grp", "dev", None), P("grp", "dev"), P(), P()),
        check_vma=False,
    )
```
